128 devices in a mesh: rep: 16 (over y, z_lo, core), ep: 8 (over x, z_hi).
Axes of the slice: x: 4, y: 4, z: 4 (z_hi: 2, z_lo: 2; z = z_hi * 2 + z_lo), core: 2. Of those that a mesh axis runs over, the one named last changes fastest.
Arguments:
- tokens: bfloat16 [16384, 1280], P(('rep', 'ep')), may hold values from -6 to 6
- cotangent: bfloat16 [16384, 1280], P(('rep', 'ep')), may hold values from -6 to 6
- lengths: int32 [16], P('rep'), may hold values from 128 to 1024, as said below
- token_mask: int32 [16384], P(('rep', 'ep')), may hold values 0 or 1
- routes: int32 [16384, 7], P(('rep', 'ep')), may hold values from 0 to 15, all different within a row; in each aligned block of 128 rows (0 to 127, 128 to 255, ...) at most 88 rows name the same one
- w_query: bfloat16 [1280, 1280], P(('rep', 'ep')), may hold values from -0.15625 to 0.15625
- w_key: bfloat16 [1280, 1280], P(('rep', 'ep')), may hold values from -0.15625 to 0.15625
- w_value: bfloat16 [1280, 1280], P(('rep', 'ep')), may hold values from -0.15625 to 0.15625
- w_output: bfloat16 [1280, 1280], P(('rep', 'ep')), may hold values from -1.25 to 1.25
- w_router: bfloat16 [1280, 16], P(('rep', 'ep')), may hold values from -0.078125 to 0.078125
- shared_gate: bfloat16 [1280, 896], P(('rep', 'ep')), may hold values from -0.15625 to 0.15625
- shared_up: bfloat16 [1280, 896], P(('rep', 'ep')), may hold values from -0.15625 to 0.15625
- shared_down: bfloat16 [896, 1280], P(('rep', 'ep')), may hold values from -0.375 to 0.375
- norm_attn: bfloat16 [1280], P(('rep', 'ep')), may hold values from 0.5 to 1.5
- norm_ffn: bfloat16 [1280], P(('rep', 'ep')), may hold values from 0.5 to 1.5
- expert_gate: bfloat16 [16, 1280, 896], P('ep'), may hold values from -0.15625 to 0.15625
- expert_up: bfloat16 [16, 1280, 896], P('ep'), may hold values from -0.15625 to 0.15625
- expert_down: bfloat16 [16, 896, 1280], P('ep'), may hold values from -1.5 to 1.5
Outputs:
- out: bfloat16 [16384, 1280], P(('rep', 'ep'))
- d_tokens: float32 [16384, 1280], P(('rep', 'ep'))
- d_query: float32 [1280, 1280], P(('rep', 'ep'))
- d_key: float32 [1280, 1280], P(('rep', 'ep'))
- d_value: float32 [1280, 1280], P(('rep', 'ep'))
- d_output: float32 [1280, 1280], P(('rep', 'ep'))
- d_router: float32 [1280, 16], P(('rep', 'ep'))
- d_shared_gate: float32 [1280, 896], P(('rep', 'ep'))
- d_shared_up: float32 [1280, 896], P(('rep', 'ep'))
- d_shared_down: float32 [896, 1280], P(('rep', 'ep'))
- d_norm_attn: float32 [1280], P(('rep', 'ep'))
- d_norm_ffn: float32 [1280], P(('rep', 'ep'))
- d_expert_gate: float32 [16, 1280, 896], P('ep')
- d_expert_up: float32 [16, 1280, 896], P('ep')
- d_expert_down: float32 [16, 896, 1280], P('ep')
The draws below stay inside these ranges and needn't reach their ends.
Inputs may be any that keep to these rules, and one draw needn't show every extreme that they name: `lengths`: in every draw some sequence has length 1024. `routes`: each token names 7 different experts. Among the rows of one device, no expert is named more than 88 times, a bound that some block reaches.
All inputs are finite; a program needn't handle non-finite values. No bound on the sum of `token_mask` on one device may be relied on, other than what follows from the above.
Results may differ from the reference program's by a relative error of at most 0.024.
Values may be sent and summed in bfloat16 or wider, within the bound.
A program may use at most 320 MiB of HBM per device.

```python
import math
import jax
import jax.numpy as jnp
import numpy as np
from jax import lax

D = 1280
HEADS = 10
HD = 128
FF = 896
TOP = 7
TOK_DEV = 128
GROUP = 1024
EXPERTS = 16
CAP = 88
TOKENS = 16384
N_REP = 16
N_EP = 8


def draw_lengths(key, part):
    length_key, pick_key = jax.random.split(jax.random.fold_in(key, 11))
    drawn = jax.random.randint(length_key, (N_REP,), GROUP // 8, GROUP + 1)
    chosen = jax.random.randint(pick_key, (), 0, N_REP)
    return jnp.where(jnp.arange(N_REP) == chosen, GROUP, drawn).astype(jnp.int32)


def place_ends(values, own_key, least, high):
    longest = values.shape.index(max(values.shape))
    spots = []
    for shift in (0, 1):
        where = [jax.random.randint(jax.random.fold_in(own_key, axis), (), 0, length) for axis, length in enumerate(values.shape)]
        where[longest] = (where[longest] + shift) % values.shape[longest]
        spots.append(tuple(where))
    return values.at[spots[0]].set(least).at[spots[1]].set(high)


def block_scale(rng, extent, shards, least, top_value):
    def one(dim, parts):
        draws = jax.random.uniform(jax.random.fold_in(jax.random.fold_in(rng, 6), dim), (parts,), jnp.float32, least / len(shards), top_value / len(shards))
        return jnp.repeat(jnp.exp(draws), extent[dim] // parts).reshape((-1,) + (1,) * (len(extent) - dim - 1))

    factor_of = one(*shards[0])
    for cut in shards[1:]:
        factor_of = factor_of * one(*cut)
    return factor_of


def deal_out(rng, own, number, rows, count, top, limit, skew):
    order = jax.random.permutation(rng, count)
    crowded, usual = shares(count, rows * top, limit, skew, True), shares(count, rows * top, limit, skew, False)
    places = jnp.arange(count)

    def named(sizes, offset_by):
        used = int((sizes > 0).sum())
        fixed = max(1, used // 4)
        passed = fixed + (places - fixed + offset_by * (used - fixed)) % max(1, count - fixed)
        return jnp.zeros((count,), jnp.int32).at[order[jnp.where(places < fixed, places, passed)]].set(jnp.asarray(sizes, jnp.int32))

    sizes = jnp.where(number % 4 == 0, named(crowded, number // 4), named(usual, number - number // 4 - 1))
    mixed = jax.random.permutation(jax.random.fold_in(own, 3), count)
    giver, receiver = mixed[0:count // 2 * 2:2], mixed[1:count // 2 * 2:2]
    room = jnp.minimum(sizes[giver] - 1, limit - sizes[receiver]) // 2
    room = jnp.where((giver == order[0]) | (receiver == order[0]) | (sizes[receiver] == 0), 0, jnp.maximum(room, 0))
    passed = jax.random.randint(jax.random.fold_in(own, 4), (count // 2,), 0, 1 << 20) % (room + 1)
    sizes = sizes.at[giver].add(-passed).at[receiver].add(passed)
    labels = jnp.searchsorted(jnp.cumsum(sizes), jnp.arange(rows * top), side="right").astype(jnp.int32)
    listing = labels.reshape(top, rows).T
    listing = listing[jax.random.permutation(jax.random.fold_in(own, 1), rows)]
    offset_by = jax.random.randint(jax.random.fold_in(own, 2), (rows, 1), 0, top)
    return jnp.take_along_axis(listing, (jnp.arange(top)[None, :] + offset_by) % top, axis=1)


def shares(number_of, total, reach, slope, full):
    weights = [(1 << 20) // math.isqrt(grade ** slope) + 1 for grade in range(1, number_of + 1)]
    largest = reach if full else min(reach, max(-(-total // number_of), total * weights[0] // sum(weights)))
    least = 1 if total - largest >= number_of - 1 else 0
    counts, spare = [largest] + [least] * (number_of - 1), total - largest - least * (number_of - 1)
    while spare > 0:
        movable = [i for i in range(1, number_of) if counts[i] < largest] or [i for i in range(1, number_of) if counts[i] < reach]
        mass, left = sum([weights[i] for i in movable]), spare
        for i in movable:
            more = min(reach - counts[i], max(1, left * weights[i] // mass), spare)
            counts[i] = counts[i] + more
            spare = spare - more
    return np.array(counts)


def bell_draw(own_key, shape, deviation, most, shards=(), kind=jnp.bfloat16):
    loudness = block_scale(own_key, shape, shards, -0.22, 0.18) if shards else 1.0
    values = jax.random.normal(own_key, shape, jnp.float32) * deviation * loudness
    return jnp.minimum(jnp.maximum(values, -most), most).astype(kind)


def setup_inputs(seed: int = 0) -> dict:
    seeds = jax.random.split(jax.random.key(seed), 19)
    tokens = bell_draw(seeds[0], (TOKENS, D), 1.0, 6.0, ((0, 128),))
    cotangent = bell_draw(seeds[1], (TOKENS, D), 1.0, 6.0, ((0, 128),))
    lengths = draw_lengths(jax.random.fold_in(seeds[18], 71), 0)
    token_mask = place_ends((jax.random.randint(seeds[3], (TOKENS,), 0, 8) < 7).astype(jnp.int32), jax.random.fold_in(seeds[3], 1), 0, 1)
    routes_keys = jax.random.split(jax.random.fold_in(seeds[4], 1), TOKENS // TOK_DEV)
    routes_turns = jax.random.permutation(jax.random.fold_in(seeds[4], 3), TOKENS // TOK_DEV)
    routes = jax.vmap(lambda own, number: deal_out(jax.random.fold_in(seeds[4], 2), own, number, TOK_DEV, EXPERTS, TOP, CAP, 1))(routes_keys, routes_turns).reshape((TOKENS, TOP))
    w_query = bell_draw(seeds[5], (D, D), D ** -0.5, 0.15625, ((0, 128),))
    w_key = bell_draw(seeds[6], (D, D), D ** -0.5, 0.15625, ((0, 128),))
    w_value = bell_draw(seeds[7], (D, D), D ** -0.5, 0.15625, ((0, 128),))
    w_output = bell_draw(seeds[8], (D, D), (D // 64) ** -0.5, 1.25, ((0, 128),))
    w_router = bell_draw(seeds[9], (D, EXPERTS), (4 * D) ** -0.5, 0.078125, ((0, 128),))
    shared_gate = bell_draw(seeds[10], (D, FF), D ** -0.5, 0.15625, ((0, 128),))
    shared_up = bell_draw(seeds[11], (D, FF), D ** -0.5, 0.15625, ((0, 128),))
    shared_down = bell_draw(seeds[12], (FF, D), (FF // 4) ** -0.5, 0.375, ((0, 128),))
    norm_attn = jnp.clip(1.0 + 0.1 * jax.random.normal(seeds[13], (D,), jnp.float32), 0.5, 1.5).astype(jnp.bfloat16)
    norm_ffn = jnp.clip(1.0 + 0.1 * jax.random.normal(seeds[14], (D,), jnp.float32), 0.5, 1.5).astype(jnp.bfloat16)
    expert_gate = bell_draw(seeds[15], (EXPERTS, D, FF), D ** -0.5, 0.15625, ((0, 8),))
    expert_up = bell_draw(seeds[16], (EXPERTS, D, FF), D ** -0.5, 0.15625, ((0, 8),))
    expert_down = bell_draw(seeds[17], (EXPERTS, FF, D), (FF // 64) ** -0.5, 1.5, ((0, 8),))
    return {"tokens": tokens, "cotangent": cotangent, "lengths": lengths, "token_mask": token_mask, "routes": routes, "w_query": w_query, "w_key": w_key, "w_value": w_value, "w_output": w_output, "w_router": w_router, "shared_gate": shared_gate, "shared_up": shared_up, "shared_down": shared_down, "norm_attn": norm_attn, "norm_ffn": norm_ffn, "expert_gate": expert_gate, "expert_up": expert_up, "expert_down": expert_down}


epsilon = 1e-06
highest = lax.Precision.HIGHEST

@jax.custom_vjp
def low(v):
    return lax.optimization_barrier(v.astype(jnp.bfloat16)).astype(jnp.float32)

@jax.custom_vjp
def low_back(v):
    return v

def low_keep(v):
    return (low(v), None)

def low_pass(kept, grad):
    return (grad,)

def back_keep(v):
    return (v, None)

def back_low(kept, grad):
    return (low(grad),)
low.defvjp(low_keep, low_pass)
low_back.defvjp(back_keep, back_low)

def product(operand, matrix):
    return jnp.dot(operand, matrix, precision=highest, preferred_element_type=jnp.float32)

def normalize(values, gain_vector):
    return values * lax.rsqrt(lax.optimization_barrier(jnp.mean(values * values, axis=-1, keepdims=True)) + epsilon) * gain_vector

def rotate(values, cosine, sine_table):
    half_dim = values.shape[-1] // 2
    front_half = values[..., :half_dim]
    back_half = values[..., half_dim:]
    cos_part = cosine[:, None, :]
    sin_part = sine_table[:, None, :]
    return jnp.concatenate([front_half * cos_part - back_half * sin_part, back_half * cos_part + front_half * sin_part], axis=-1)

def swiglu(gate_part, lift_part):
    return jax.nn.silu(gate_part) * lift_part

def attend(pieces):
    queries, keys, values, live_group = pieces
    score_scale = HD ** (-0.5)
    scores = low_back(jnp.einsum('qhd,khd->hqk', queries, keys, precision=highest) * score_scale)
    query_pos = jnp.arange(GROUP, dtype=jnp.int32)[:, None]
    key_pos = jnp.arange(GROUP, dtype=jnp.int32)[None, :]
    allowed = (key_pos <= query_pos) & ((live_group[None, :] > 0.5) | (key_pos == query_pos))
    scores = jnp.where(allowed[None], scores, -1e+30)
    weights = low(jax.nn.softmax(scores, axis=-1))
    return jnp.einsum('hqk,khd->qhd', weights, values, precision=highest)

def reference(tokens, cotangent, lengths, token_mask, routes, w_query, w_key, w_value, w_output, w_router, shared_gate, shared_up, shared_down, norm_attn, norm_ffn, expert_gate, expert_up, expert_down):
    block_count = N_REP * N_EP
    row_count = TOK_DEV * TOP
    position = jnp.arange(TOKENS, dtype=jnp.int32) % GROUP
    live_length = jnp.repeat(lengths, GROUP)
    token_live = ((position < live_length) & (token_mask == 1)).astype(jnp.float32)
    half_dim = HD // 2
    frequency = 10000.0 ** (-(jnp.arange(half_dim, dtype=jnp.float32) * 2.0 / HD))
    angles = position.astype(jnp.float32)[:, None] * frequency[None, :]
    cosine = jnp.cos(angles)
    sine_table = jnp.sin(angles)
    block_routes = routes.reshape(block_count, row_count)
    one_hot = (block_routes[:, :, None] == jnp.arange(EXPERTS, dtype=jnp.int32)[None, None, :]).astype(jnp.int32)
    slot_index = lax.optimization_barrier(jnp.sum((jnp.cumsum(one_hot, axis=1) - 1) * one_hot, axis=2))
    block_ids = jnp.broadcast_to(jnp.arange(block_count, dtype=jnp.int32)[:, None], (block_count, row_count))
    row_ids = jnp.broadcast_to(jnp.arange(row_count, dtype=jnp.int32)[None, :], (block_count, row_count))
    slot_token = jnp.full((block_count, EXPERTS, CAP), TOKENS, jnp.int32).at[block_ids, block_routes, slot_index].set(block_ids * TOK_DEV + row_ids // TOP)
    slot_choice = jnp.zeros((block_count, EXPERTS, CAP), jnp.int32).at[block_ids, block_routes, slot_index].set(row_ids % TOP)
    slot_token = jnp.transpose(slot_token, (1, 0, 2)).reshape(EXPERTS, block_count * CAP)
    slot_choice = jnp.transpose(slot_choice, (1, 0, 2)).reshape(EXPERTS, block_count * CAP)

    def forward(inputs, query_matrix, key_matrix, value_matrix, output_matrix, router_matrix, gate_matrix, lift_matrix, down_matrix, first_gain, second_gain, expert_gates, expert_lifts, expert_downs):
        hidden_one = low(normalize(inputs, first_gain))
        query_raw = low_back(product(hidden_one, query_matrix)).reshape(TOKENS, HEADS, HD)
        key_raw = low_back(product(hidden_one, key_matrix)).reshape(TOKENS, HEADS, HD)
        value_all = low(low_back(product(hidden_one, value_matrix))).reshape(N_REP, GROUP, HEADS, HD)
        query_all = low(rotate(query_raw, cosine, sine_table)).reshape(N_REP, GROUP, HEADS, HD)
        key_all = low(rotate(key_raw, cosine, sine_table)).reshape(N_REP, GROUP, HEADS, HD)
        attended = lax.map(jax.checkpoint(attend), (query_all, key_all, value_all, token_live.reshape(N_REP, GROUP)))
        attended = low(low_back(attended.reshape(TOKENS, D)))
        branch = low_back(product(attended, output_matrix))
        residual = inputs + token_live[:, None] * branch
        hidden_two = low(normalize(residual, second_gain))
        logits = product(hidden_two, router_matrix)
        gate_weights = jnp.take_along_axis(jax.nn.softmax(logits, axis=-1), routes, axis=1) * token_live[:, None]
        shared_act = low(swiglu(low_back(product(hidden_two, gate_matrix)), low_back(product(hidden_two, lift_matrix))))
        shared_out = low_back(product(shared_act, down_matrix))
        padded_hidden = jnp.concatenate([hidden_two, jnp.zeros((1, D), hidden_two.dtype)], axis=0)
        padded_gates = jnp.concatenate([gate_weights, jnp.zeros((1, TOP), gate_weights.dtype)], axis=0)

        def one_expert(routed, expert_index):
            rows_token = slot_token[expert_index]
            rows_choice = slot_choice[expert_index]
            rows = low_back(padded_hidden[rows_token])
            expert_act = low(swiglu(low_back(product(rows, expert_gates[expert_index])), low_back(product(rows, expert_lifts[expert_index]))))
            expert_out = low(low_back(product(expert_act, expert_downs[expert_index])))
            weight_rows = padded_gates[rows_token, rows_choice]
            return (routed.at[rows_token].add(weight_rows[:, None] * expert_out), None)
        routed, _ = lax.scan(jax.checkpoint(one_expert), jnp.zeros((TOKENS + 1, D), inputs.dtype), jnp.arange(EXPERTS, dtype=jnp.int32))
        return residual + token_live[:, None] * shared_out + routed[:TOKENS]
    params = tuple((array.astype(jnp.float32) for array in (tokens, w_query, w_key, w_value, w_output, w_router, shared_gate, shared_up, shared_down, norm_attn, norm_ffn, expert_gate, expert_up, expert_down)))
    result, pullback = jax.vjp(forward, *params)
    grads = pullback(cotangent.astype(jnp.float32))
    return (result.astype(jnp.bfloat16), grads[0], grads[1], grads[2], grads[3], grads[4], grads[5], grads[6], grads[7], grads[8], grads[9], grads[10], grads[11], grads[12], grads[13])
```

```python
import functools
import itertools

import jax
import jax.numpy as jnp
from jax import lax
from jax.experimental import pallas as pl
from jax.experimental.pallas import tpu as pltpu
from jax.sharding import PartitionSpec as P

HD = 128
EPS = 1e-6
BF = jnp.bfloat16
F32 = jnp.float32
MESH = pl.DeviceIdType.MESH
HIGH = lax.Precision.HIGHEST
HEADS_DEV = 2
EXTRA = 128
ROW_PAD = 16
VMEM_LIMIT = 60 << 20


def dot(a, b):
    return jnp.dot(a, b, preferred_element_type=F32)


def dot_nt(a, b):
    return lax.dot_general(a, b, (((1,), (1,)), ((), ())), preferred_element_type=F32)


def dot_tn(a, b):
    return lax.dot_general(a, b, (((0,), (0,)), ((), ())), preferred_element_type=F32)


class Place:
    def __init__(self):
        self.rep = lax.axis_index("rep")
        self.ep = lax.axis_index("ep")
        self.y = self.rep // 4
        self.zl = (self.rep // 2) % 2
        self.core = self.rep % 2
        self.x = self.ep // 2
        self.zh = self.ep % 2

    def rep_at(self, y, zl, core):
        return (y % 4) * 4 + zl * 2 + core

    def ep_at(self, x, zh):
        return (x % 4) * 2 + zh

    def to_x(self, step):
        return (self.rep, self.ep_at(self.x + step, self.zh))

    def to_zh(self):
        return (self.rep, self.ep_at(self.x, 1 - self.zh))

    def to_ep(self, shift):
        return (self.rep, (self.ep + shift) % 8)

    def to_y(self, step):
        return (self.rep_at(self.y + step, self.zl, self.core), self.ep)

    def to_zl(self):
        return (self.rep_at(self.y, 1 - self.zl, self.core), self.ep)

    def to_core(self):
        return (self.rep_at(self.y, self.zl, 1 - self.core), self.ep)


class Copies:
    def __init__(self, send_sem, recv_sem):
        self.send_sem, self.recv_sem = send_sem, recv_sem
        self.number = itertools.count()
        self.sent, self.open = [], []

    def send(self, src, dst, device):
        i = next(self.number)
        copy = pltpu.make_async_remote_copy(
            src_ref=src,
            dst_ref=dst,
            send_sem=self.send_sem.at[i],
            recv_sem=self.recv_sem.at[i],
            device_id=device,
            device_id_type=MESH,
        )
        copy.start()
        self.sent.append(copy)
        self.open.append(copy)
        return copy

    def local(self, src, dst):
        i = next(self.number)
        copy = pltpu.make_async_copy(src, dst, self.recv_sem.at[i])
        copy.start()
        self.open.append(copy)
        return copy

    def arrived(self, copy):
        if any(copy is c for c in self.sent):
            copy.wait_recv()
        else:
            copy.wait()
        self.open = [c for c in self.open if c is not copy]

    def sent_off(self, copy):
        copy.wait_send()
        self.sent = [c for c in self.sent if c is not copy]

    def finish(self):
        for copy in list(self.open):
            self.arrived(copy)
        for copy in self.sent:
            copy.wait_send()


def greet(devices):
    barrier = pltpu.get_barrier_semaphore()
    for device in devices:
        pl.semaphore_signal(barrier, inc=1, device_id=device, device_id_type=MESH)
    pl.semaphore_wait(barrier, len(devices))


def run_streams(*streams):
    live = list(streams)
    while live:
        for stream in list(live):
            try:
                next(stream)
            except StopIteration:
                live.remove(stream)


def half_columns(columns):
    return (columns // 128 + 1) // 2 * 128


def ep_peers(place):
    return [place.to_ep(k) for k in range(1, 8)]


def rep_peers(place):
    return [place.to_y(1), place.to_y(-1), place.to_zl(), place.to_core()]


def gather_ep(cp, place, src, dst, columns):
    cut = half_columns(columns)
    lo, hi = pl.ds(0, cut), pl.ds(cut, columns - cut)
    mine = place.ep
    own = cp.local(src, dst.at[mine])
    right = cp.send(src, dst.at[mine], place.to_x(1))
    left = cp.send(src, dst.at[mine], place.to_x(-1))
    over = cp.send(src, dst.at[mine], place.to_zh())
    yield
    from_left = place.ep_at(place.x - 1, place.zh)
    from_right = place.ep_at(place.x + 1, place.zh)
    from_over = place.ep_at(place.x, 1 - place.zh)
    far = place.ep_at(place.x + 2, place.zh)
    cp.arrived(right)
    half_a = cp.send(dst.at[from_left, :, lo], dst.at[from_left, :, lo], place.to_x(1))
    cp.arrived(left)
    half_b = cp.send(dst.at[from_right, :, hi], dst.at[from_right, :, hi], place.to_x(-1))
    yield
    cp.arrived(over)
    cp.send(dst.at[from_over], dst.at[from_over], place.to_x(1))
    cp.send(dst.at[from_over], dst.at[from_over], place.to_x(-1))
    yield
    cp.arrived(half_a)
    cp.arrived(half_b)
    cp.send(dst.at[far], dst.at[far], place.to_zh())
    yield
    cp.arrived(own)


def gather_ring_y(cp, place, src, dst, columns, slot):
    cut = half_columns(columns)
    lo, hi = pl.ds(0, cut), pl.ds(cut, columns - cut)
    up = cp.send(src, dst.at[slot(place.y)], place.to_y(1))
    down = cp.send(src, dst.at[slot(place.y)], place.to_y(-1))
    yield
    cp.arrived(up)
    below = slot(place.y - 1)
    half_a = cp.send(dst.at[below, :, lo], dst.at[below, :, lo], place.to_y(1))
    cp.arrived(down)
    above = slot(place.y + 1)
    half_b = cp.send(dst.at[above, :, hi], dst.at[above, :, hi], place.to_y(-1))
    yield
    cp.arrived(half_a)
    cp.arrived(half_b)


def gather_rep(cp, place, src, dst, columns, z_first):
    mine = place.rep
    own = cp.local(src, dst.at[mine])
    cp.send(src, dst.at[mine], place.to_core())

    def slot(zl):
        return lambda y: place.rep_at(y, zl, place.core)

    def pass_core(index):
        cp.send(dst.at[index], dst.at[index], place.to_core())

    here, there = slot(place.zl), slot(1 - place.zl)
    if z_first:
        over = cp.send(src, dst.at[mine], place.to_zl())
        first = gather_ring_y(cp, place, src, dst, columns, here)
        next(first)
        yield
        cp.arrived(over)
        second = gather_ring_y(
            cp, place, dst.at[there(place.y)], dst, columns, there
        )
        next(second)
        pass_core(there(place.y))
        yield
        next(first)
        for k in (-1, 1):
            pass_core(here(place.y + k))
        yield
        next(second)
        for k in (-1, 1):
            pass_core(there(place.y + k))
        yield
        next(first, None)
        pass_core(here(place.y + 2))
        yield
        next(second, None)
        pass_core(there(place.y + 2))
    else:
        over = [cp.send(src, dst.at[mine], place.to_zl())]
        ring = gather_ring_y(cp, place, src, dst, columns, here)
        next(ring)
        yield
        next(ring)
        for k in (-1, 1):
            block = dst.at[here(place.y + k)]
            over.append(cp.send(block, block, place.to_zl()))
            pass_core(here(place.y + k))
        yield
        next(ring, None)
        block = dst.at[here(place.y + 2)]
        over.append(cp.send(block, block, place.to_zl()))
        pass_core(here(place.y + 2))
        yield
        for copy, k in zip(over, (0, -1, 1, 2)):
            cp.arrived(copy)
            pass_core(there(place.y + k))
            yield
    cp.arrived(own)


def spread_matrix(rows, blocks, used):
    shape = (rows, blocks * ROW_PAD)
    to = lax.broadcasted_iota(jnp.int32, shape, 0)
    at = lax.broadcasted_iota(jnp.int32, shape, 1)
    return jnp.where((at // ROW_PAD) * used + at % ROW_PAD == to, 1.0, 0.0) * jnp.where(
        at % ROW_PAD < used, 1.0, 0.0
    )


def kernel_a(
    slices, whole, down, tok, cot,
    tok_all, cot_all, w_slices, w_whole, w_down,
    land_slices, land_whole, pack_slices, pack_whole, send_sem, recv_sem,
):
    place = Place()
    cp = Copies(send_sem, recv_sem)
    greet(ep_peers(place) + rep_peers(place))
    first = []
    mine = place.ep
    first.append(cp.local(slices.at[mine], land_slices.at[mine]))
    first.append(cp.local(whole, land_whole.at[mine]))
    for k in range(1, 8):
        first.append(cp.send(slices.at[(mine + k) % 8], land_slices.at[mine], place.to_ep(k)))
        first.append(cp.send(whole, land_whole.at[mine], place.to_ep(k)))
    tok_stream = gather_ep(cp, place, tok, tok_all, tok.shape[1])
    next(tok_stream)
    down_stream = gather_rep(cp, place, down, w_down, down.shape[1], True)
    next(down_stream)
    for copy in first:
        cp.arrived(copy)
    used = pack_slices.shape[0] // 8
    spread = spread_matrix(8 * used, 8, used).astype(BF)
    for land, pack in ((land_slices, pack_slices), (land_whole, pack_whole)):
        columns = land.shape[2]
        step = 128
        for c in range(0, columns, step):
            block = land[:, :, c : c + step].reshape(8 * ROW_PAD, step)
            pack[:, c : c + step] = dot(spread, block).astype(BF)
    slice_stream = gather_rep(cp, place, pack_slices, w_slices, slices.shape[2], False)
    next(slice_stream)
    whole_stream = gather_rep(cp, place, pack_whole, w_whole, whole.shape[1], True)
    next(whole_stream)
    cot_stream = gather_ep(cp, place, cot, cot_all, cot.shape[1])
    run_streams(tok_stream, slice_stream, whole_stream, cot_stream, down_stream)
    cp.finish()


def call_a(slices, whole, down, tok, cot, used):
    anyspace = pl.BlockSpec(memory_space=pl.ANY)
    copies = 160
    return pl.pallas_call(
        kernel_a,
        out_shape=(
            jax.ShapeDtypeStruct((8,) + tok.shape, BF),
            jax.ShapeDtypeStruct((8,) + cot.shape, BF),
            jax.ShapeDtypeStruct((16, 8 * used, slices.shape[2]), BF),
            jax.ShapeDtypeStruct((16, 8 * used, whole.shape[1]), BF),
            jax.ShapeDtypeStruct((16,) + down.shape, BF),
        ),
        in_specs=[anyspace] * 5,
        out_specs=(anyspace,) * 5,
        scratch_shapes=[
            pltpu.VMEM((8, ROW_PAD, slices.shape[2]), BF),
            pltpu.VMEM((8, ROW_PAD, whole.shape[1]), BF),
            pltpu.VMEM((8 * used, slices.shape[2]), BF),
            pltpu.VMEM((8 * used, whole.shape[1]), BF),
            pltpu.SemaphoreType.DMA((copies,)),
            pltpu.SemaphoreType.DMA((copies,)),
        ],
        compiler_params=pltpu.CompilerParams(
            collective_id=0, has_side_effects=True, vmem_limit_bytes=VMEM_LIMIT
        ),
        name="gather_inputs",
    )(slices, whole, down, tok, cot)


def kernel_b(
    heads, tok, live, w_out, gain,
    residual, attended, hidden_all,
    land, hidden, send_sem, recv_sem,
):
    place = Place()
    cp = Copies(send_sem, recv_sem)
    greet(ep_peers(place))
    rows, width = tok.shape
    mine = place.ep
    span = heads.shape[2]
    column = pl.ds(pl.multiple_of(mine * span, 128), span)
    first = [cp.local(heads.at[mine], land.at[:, column])]
    for k in range(1, 8):
        first.append(cp.send(heads.at[(mine + k) % 8], land.at[:, column], place.to_ep(k)))
    for copy in first:
        cp.arrived(copy)
    low = land[:, :width]
    attended[...] = low
    step = 256
    squares = jnp.zeros((rows, 1), F32)
    for c in range(0, width, step):
        part = tok[:, c : c + step].astype(F32) + live[...] * dot(low, w_out[:, c : c + step])
        residual[:, c : c + step] = part
        squares += jnp.sum(part * part, axis=1, keepdims=True)
    scale = lax.rsqrt(squares / width + EPS)
    hidden[...] = (residual[...] * scale * gain[...]).astype(BF)
    run_streams(gather_ep(cp, place, hidden, hidden_all, width))
    cp.finish()


def call_b(heads, tok, live, w_out, gain):
    anyspace = pl.BlockSpec(memory_space=pl.ANY)
    vmem = pl.BlockSpec(memory_space=pltpu.VMEM)
    rows, width = tok.shape
    return pl.pallas_call(
        kernel_b,
        out_shape=(
            jax.ShapeDtypeStruct((rows, width), F32),
            jax.ShapeDtypeStruct((rows, width), BF),
            jax.ShapeDtypeStruct((8, rows, width), BF),
        ),
        in_specs=[anyspace, vmem, vmem, vmem, vmem],
        out_specs=(vmem, vmem, anyspace),
        scratch_shapes=[
            pltpu.VMEM((rows, 8 * heads.shape[2]), BF),
            pltpu.VMEM((rows, width), BF),
            pltpu.SemaphoreType.DMA((32,)),
            pltpu.SemaphoreType.DMA((32,)),
        ],
        compiler_params=pltpu.CompilerParams(
            collective_id=1, has_side_effects=True, vmem_limit_bytes=VMEM_LIMIT
        ),
        name="attention_out",
    )(heads, tok, live, w_out, gain)


def add_into(out, first, others):
    lead = out.shape[:-2]
    rows = out.shape[-2]

    for index in itertools.product(*(range(n) for n in lead)):

        @pl.loop(0, rows // ROW_PAD)
        def _(i):
            at = index + (pl.ds(pl.multiple_of(i * ROW_PAD, ROW_PAD), ROW_PAD),)
            total = first[at].astype(F32)
            for other in others:
                total += other[at].astype(F32)
            out[at] = total.astype(out.dtype)


def sum_ring_y(cp, place, mine, work, near_lo, near_hi, last_up, last_down, chunk, lo, hi):
    y = place.y
    up, down = place.to_y(1), place.to_y(-1)
    a = cp.send(lo(chunk(mine, y + 2)), near_lo, up)
    b = cp.send(hi(chunk(mine, y + 2)), near_hi, down)
    c = cp.send(hi(chunk(mine, y + 1)), hi(last_up), up)
    d = cp.send(lo(chunk(mine, y - 1)), lo(last_down), down)
    yield
    cp.arrived(a)
    add_into(lo(chunk(work, y + 1)), lo(chunk(mine, y + 1)), [near_lo])
    e = cp.send(lo(chunk(work, y + 1)), lo(last_up), up)
    cp.arrived(b)
    add_into(hi(chunk(work, y - 1)), hi(chunk(mine, y - 1)), [near_hi])
    f = cp.send(hi(chunk(work, y - 1)), hi(last_down), down)
    yield
    for copy in (c, d, e, f):
        cp.arrived(copy)


def sum_rep_yz(cp, place, mine, bufs, out):
    work, near_lo, near_hi, last_up, last_down, half, over = bufs
    ring = sum_ring_y(
        cp, place, mine, work, near_lo, near_hi, last_up, last_down,
        lambda ref, y: ref.at[y % 4],
        lambda ref: ref.at[0],
        lambda ref: ref.at[1],
    )
    yield from ring
    other = 1 - place.zl
    chunk = mine.at[place.y]
    add_into(half, chunk.at[other], [last_up.at[other], last_down.at[other]])
    copy = cp.send(half, over, place.to_zl())
    yield
    cp.arrived(copy)
    add_into(
        out, chunk.at[place.zl], [last_up.at[place.zl], last_down.at[place.zl], over]
    )


def sum_bufs(rows, columns):
    return [
        pltpu.VMEM((4, 2, rows, columns), BF),
        pltpu.VMEM((rows, columns), BF),
        pltpu.VMEM((rows, columns), BF),
        pltpu.VMEM((2, rows, columns), BF),
        pltpu.VMEM((2, rows, columns), BF),
        pltpu.VMEM((rows, columns), BF),
        pltpu.VMEM((rows, columns), BF),
    ]


def kernel_c(
    grads, outs, g_gate, g_up, g_down,
    residual, cot, live, probs, w_out, w_router, gain,
    out, g_residual, g_branch, g_logits, d_gain, g_heads, s_gate, s_up, s_down,
    land_grads, land_outs, g_att, pair, bufs, send_sem, recv_sem,
):
    place = Place()
    cp = Copies(send_sem, recv_sem)
    greet(ep_peers(place) + rep_peers(place))
    rows, width = residual.shape
    mine = place.ep
    summed = ((g_gate, s_gate), (g_up, s_up), (g_down, s_down))
    core = place.core
    own_half, mate_half = [], []
    for (grad, _), (own, got) in zip(summed, pair):
        own_half.append(cp.local(grad.at[core], own))
        mate_half.append(cp.send(grad.at[1 - core], got, place.to_core()))
    first = [cp.local(grads.at[mine], land_grads.at[mine])]
    second = [cp.local(outs.at[mine], land_outs.at[mine])]
    for k in range(1, 8):
        first.append(cp.send(grads.at[(mine + k) % 8], land_grads.at[mine], place.to_ep(k)))
    for k in range(1, 8):
        second.append(cp.send(outs.at[(mine + k) % 8], land_outs.at[mine], place.to_ep(k)))
    streams = []
    for ((_, total), (own, got), buf, a, b) in zip(summed, pair, bufs, own_half, mate_half):
        cp.arrived(a)
        cp.arrived(b)
        add_into(own, own, [got])
        streams.append(sum_rep_yz(cp, place, own, buf, total))
        next(streams[-1])
    for copy in first:
        cp.arrived(copy)

    def total_of(land, c, n):
        total = land[0, :, c : c + n].astype(F32)
        for i in range(1, 8):
            total += land[i, :, c : c + n].astype(F32)
        return total

    alive = live[...]
    router_grad = total_of(land_grads, width, EXTRA) * alive
    prob = probs[...]
    logit_grad = prob * (router_grad - jnp.sum(prob * router_grad, axis=1, keepdims=True))
    g_logits[...] = logit_grad
    step = 256
    squares = jnp.zeros((rows, 1), F32)
    mean_k = jnp.zeros((rows, 1), F32)
    for c in range(0, width, step):
        part = residual[:, c : c + step]
        squares += jnp.sum(part * part, axis=1, keepdims=True)
    scale = lax.rsqrt(squares / width + EPS)
    for c in range(0, width, step):
        k = total_of(land_grads, c, step) + lax.dot_general(
            logit_grad, w_router[c : c + step, :].astype(F32), (((1,), (1,)), ((), ())),
            preferred_element_type=F32, precision=HIGH,
        )
        normed = residual[:, c : c + step] * scale
        d_gain[:, c : c + step] = jnp.sum(k * normed, axis=0, keepdims=True)
        k = k * gain[:, c : c + step]
        mean_k += jnp.sum(k * normed, axis=1, keepdims=True)
        g_residual[:, c : c + step] = k
    mean_k = mean_k / width
    for c in range(0, width, step):
        normed = residual[:, c : c + step] * scale
        grad = cot[:, c : c + step].astype(F32) + scale * (
            g_residual[:, c : c + step] - normed * mean_k
        )
        g_residual[:, c : c + step] = grad
        g_branch[:, c : c + step] = (alive * grad).astype(BF)
    g_att[...] = jnp.zeros_like(g_att)
    low = g_branch[...]
    for c in range(0, width, step):
        g_att[c // step] = dot_nt(low, w_out[c : c + step, :]).astype(BF)
    third = [cp.local(g_att.at[mine], g_heads.at[mine])]
    for k in range(1, 8):
        third.append(cp.send(g_att.at[(mine + k) % 8], g_heads.at[mine], place.to_ep(k)))
    run_streams(*streams)
    for copy in second:
        cp.arrived(copy)
    for c in range(0, width, step):
        out[:, c : c + step] = (
            residual[:, c : c + step] + total_of(land_outs, c, step)
        ).astype(BF)
    cp.finish()


def call_c(grads, outs, g_gate, g_up, g_down, residual, cot, live, probs, w_out, w_router, gain):
    anyspace = pl.BlockSpec(memory_space=pl.ANY)
    vmem = pl.BlockSpec(memory_space=pltpu.VMEM)
    rows, width = residual.shape
    summed = [g.shape for g in (g_gate, g_up, g_down)]
    small = [s[3:] for s in summed]
    return pl.pallas_call(
        kernel_c,
        out_shape=(
            jax.ShapeDtypeStruct((rows, width), BF),
            jax.ShapeDtypeStruct((rows, width), F32),
            jax.ShapeDtypeStruct((rows, width), BF),
            jax.ShapeDtypeStruct((rows, EXTRA), F32),
            jax.ShapeDtypeStruct((1, width), F32),
            jax.ShapeDtypeStruct((8, rows, HEADS_DEV * HD), BF),
        )
        + tuple(jax.ShapeDtypeStruct(s, BF) for s in small),
        in_specs=[anyspace] * 5 + [vmem] * 7,
        out_specs=(vmem,) * 5 + (anyspace,) + (vmem,) * 3,
        scratch_shapes=[
            pltpu.VMEM((8, rows, grads.shape[2]), BF),
            pltpu.VMEM((8, rows, width), BF),
            pltpu.VMEM((8, rows, HEADS_DEV * HD), BF),
            [[pltpu.VMEM(s[1:], BF)] * 2 for s in summed],
            [sum_bufs(*s) for s in small],
            pltpu.SemaphoreType.DMA((80,)),
            pltpu.SemaphoreType.DMA((80,)),
        ],
        compiler_params=pltpu.CompilerParams(
            collective_id=2, has_side_effects=True, vmem_limit_bytes=VMEM_LIMIT
        ),
        name="sum_hidden_two",
    )(grads, outs, g_gate, g_up, g_down, residual, cot, live, probs, w_out, w_router, gain)


def gather_expert(cp, place, src, dst):
    core, y, zl = place.core, place.y, place.zl
    columns = src.shape[1]
    cut = half_columns(columns)
    lo, hi = pl.ds(0, cut), pl.ds(cut, columns - cut)
    at = lambda k, z: dst.at[core, (y + k) % 4, z]
    own = cp.local(src, at(0, zl))
    over = cp.send(src, at(0, zl), place.to_zl())
    ups = {zl_: None for zl_ in (0, 1)}
    cp.send(src, at(0, zl), place.to_core())
    first = (
        cp.send(src, at(0, zl), place.to_y(1)),
        cp.send(src, at(0, zl), place.to_y(-1)),
    )
    yield
    cp.arrived(over)
    other = 1 - zl
    second = (
        cp.send(at(0, other), at(0, other), place.to_y(1)),
        cp.send(at(0, other), at(0, other), place.to_y(-1)),
    )
    cp.send(at(0, other), at(0, other), place.to_core())
    yield
    halves = []
    for (up, down), z in ((first, zl), (second, other)):
        cp.arrived(up)
        a = cp.send(at(-1, z).at[:, lo], at(-1, z).at[:, lo], place.to_y(1))
        cp.send(at(-1, z), at(-1, z), place.to_core())
        cp.arrived(down)
        b = cp.send(at(1, z).at[:, hi], at(1, z).at[:, hi], place.to_y(-1))
        cp.send(at(1, z), at(1, z), place.to_core())
        halves.append((a, b))
        yield
    for (a, b), z in zip(halves, (zl, other)):
        cp.arrived(a)
        cp.arrived(b)
        cp.send(at(2, z), at(2, z), place.to_core())
        yield
    cp.arrived(own)


def sum_rep_dense(cp, place, mine, mate, bufs, out):
    add_into(mine, mine, [mate])
    yield from sum_rep_yz(cp, place, mine, bufs, out)


def kernel_d(
    grads, s_gate, s_up, s_down, d_slices, d_whole, d_down,
    g_hidden, e_gate, e_up, e_down, o_slices, o_whole, o_down,
    land, pair, bufs, totals, wide, send_sem, recv_sem,
):
    place = Place()
    cp = Copies(send_sem, recv_sem)
    greet(ep_peers(place) + rep_peers(place))
    mine = place.ep
    core = place.core
    first = [cp.local(grads.at[mine], land.at[mine])]
    for k in range(1, 8):
        first.append(cp.send(grads.at[(mine + k) % 8], land.at[mine], place.to_ep(k)))
    streams = []
    parts = (d_slices, d_whole, d_down)
    started = []
    for grad, (own, got) in zip(parts, pair):
        started.append(
            (
                cp.local(grad.at[:, :, core], own),
                cp.send(grad.at[:, :, 1 - core], got, place.to_core()),
            )
        )
    for (own, got), (a, b), buf, total in zip(pair, started, bufs, totals):
        cp.arrived(a)
        cp.arrived(b)
        streams.append(sum_rep_dense(cp, place, own, got, buf, total))
        next(streams[-1])
    experts = [
        gather_expert(cp, place, s, e)
        for s, e in ((s_gate, e_gate), (s_up, e_up), (s_down, e_down))
    ]
    for stream in experts:
        next(stream)
    run_streams(*streams, *experts)
    used = totals[0].shape[0] // 8
    spread = spread_matrix(8 * used, 8, used).astype(BF)
    for total, padded in zip(totals, wide):
        columns = total.shape[1]
        for c in range(0, columns, 128):
            padded[:, :, c : c + 128] = (
                dot_tn(spread, total[:, c : c + 128]).astype(BF).reshape(8, ROW_PAD, 128)
            )
    for padded, result in zip(wide, (o_slices, o_whole)):
        cp.local(padded.at[mine], result.at[mine])
        for k in range(1, 8):
            cp.send(padded.at[(mine + k) % 8], result.at[mine], place.to_ep(k))
    o_down[...] = totals[2][...]
    for copy in first:
        cp.arrived(copy)
    width = g_hidden.shape[1]
    for c in range(0, width, 256):
        total = land[0, :, c : c + 256].astype(F32)
        for i in range(1, 8):
            total += land[i, :, c : c + 256].astype(F32)
        g_hidden[:, c : c + 256] = total
    cp.finish()


def call_d(grads, s_gate, s_up, s_down, d_slices, d_whole, d_down):
    anyspace = pl.BlockSpec(memory_space=pl.ANY)
    vmem = pl.BlockSpec(memory_space=pltpu.VMEM)
    _, rows, width = grads.shape
    parts = [g.shape for g in (d_slices, d_whole, d_down)]
    small = [s[3:] for s in parts]
    return pl.pallas_call(
        kernel_d,
        out_shape=(jax.ShapeDtypeStruct((rows, width), F32),)
        + tuple(jax.ShapeDtypeStruct((2, 4, 2) + s.shape, BF) for s in (s_gate, s_up, s_down))
        + tuple(jax.ShapeDtypeStruct((8, ROW_PAD, s[1]), BF) for s in small[:2])
        + (jax.ShapeDtypeStruct(small[2], BF),),
        in_specs=[anyspace] * 7,
        out_specs=(vmem,) + (anyspace,) * 5 + (vmem,),
        scratch_shapes=[
            pltpu.VMEM((8, rows, width), BF),
            [[pltpu.VMEM((4, 2) + s, BF)] * 2 for s in small],
            [sum_bufs(*s) for s in small],
            [pltpu.VMEM(s, BF) for s in small],
            [pltpu.VMEM((8, ROW_PAD, s[1]), BF) for s in small[:2]],
            pltpu.SemaphoreType.DMA((140,)),
            pltpu.SemaphoreType.DMA((140,)),
        ],
        compiler_params=pltpu.CompilerParams(
            collective_id=3, has_side_effects=True, vmem_limit_bytes=VMEM_LIMIT
        ),
        name="sum_hidden_one",
    )(grads, s_gate, s_up, s_down, d_slices, d_whole, d_down)


def rotate(values, cosine, sine):
    half = values.shape[-1] // 2
    front, back = values[..., :half], values[..., half:]
    cos, sin = cosine[:, None, :], sine[:, None, :]
    return jnp.concatenate([front * cos - back * sin, back * cos + front * sin], axis=-1)


def norm_parts(values):
    scale = lax.rsqrt(jnp.mean(values * values, axis=-1, keepdims=True) + EPS)
    return scale, values * scale


def pad_rows(values, rows):
    return jnp.pad(values, ((0, rows - values.shape[0]),) + ((0, 0),) * (values.ndim - 1))


def body(
    tokens, cotangent, lengths, token_mask, routes,
    w_query, w_key, w_value, w_output, w_router,
    shared_gate, shared_up, shared_down, norm_attn, norm_ffn,
    expert_gate, expert_up, expert_down,
):
    rows, width = tokens.shape
    top = routes.shape[1]
    used = w_query.shape[0]
    hidden = expert_gate.shape[2]
    experts = w_router.shape[1]
    exp_dev = expert_gate.shape[0]
    ep = lax.axis_index("ep")
    group = rows * 8
    span = HEADS_DEV * HD
    owners = width // span
    down_used = shared_down.shape[0]
    shared_cols = 16 * down_used

    def by_owner(w):
        return jnp.pad(w.reshape(used, owners, span), ((0, 0), (0, 8 - owners), (0, 0)))

    def by_shared(w):
        w = w.reshape(used, 16, 8, down_used).transpose(0, 2, 1, 3).reshape(used, 8, shared_cols)
        return jnp.pad(w, ((0, 0), (0, 0), (0, 128 - shared_cols)))

    slices = jnp.concatenate(
        [by_owner(w_query), by_owner(w_key), by_owner(w_value), by_shared(shared_gate), by_shared(shared_up)],
        axis=2,
    ).transpose(1, 0, 2)
    slices = jnp.pad(slices, ((0, 0), (0, ROW_PAD - used), (0, 0)))
    whole = jnp.concatenate(
        [w_output, w_router, norm_attn[:, None], norm_ffn[:, None]], axis=1
    )
    whole = jnp.pad(whole, ((0, ROW_PAD - used), (0, width + EXTRA - whole.shape[1])))
    down = pad_rows(shared_down, ROW_PAD)
    position = ep * rows + jnp.arange(rows, dtype=jnp.int32)
    live_own = ((position < lengths[0]) & (token_mask == 1)).astype(F32)
    tok_wide = jnp.concatenate(
        [
            tokens,
            jnp.pad(
                jnp.concatenate([routes.astype(BF), live_own[:, None].astype(BF)], axis=1),
                ((0, 0), (0, EXTRA - top - 1)),
            ),
        ],
        axis=1,
    )
    tok_all, cot_all, w_slices, w_whole, w_down = call_a(
        slices, whole, down, tok_wide, cotangent, used
    )
    tok_all = tok_all.reshape(group, width + EXTRA)
    cot_all = cot_all.reshape(group, width)
    w_slices = w_slices.reshape(width, -1)
    w_whole = w_whole.reshape(width, -1)
    w_down = jnp.pad(
        w_down[:, :down_used].reshape(shared_cols, width), ((0, 128 - shared_cols), (0, 0))
    )
    live = tok_all[:, width + top].astype(F32)
    routes_all = tok_all[:, width : width + top].astype(jnp.int32)
    gain_one = w_whole[:, width + experts].astype(F32)
    gain_two = w_whole[:, width + experts + 1].astype(F32)
    router = w_whole[:, width : width + experts]
    w_out = w_whole[:, :width]
    w_qkv = w_slices[:, : 3 * span]
    w_gate = w_slices[:, 3 * span : 3 * span + 128]
    w_up = w_slices[:, 3 * span + 128 :]

    pos = jnp.arange(group, dtype=jnp.int32)
    frequency = 10000.0 ** (-(jnp.arange(HD // 2, dtype=F32) * 2.0 / HD))
    angles = pos.astype(F32)[:, None] * frequency[None, :]
    cosine, sine = jnp.cos(angles), jnp.sin(angles)
    inputs_all = tok_all[:, :width].astype(F32)
    _, normed_one = norm_parts(inputs_all)
    hidden_one = (normed_one * gain_one).astype(BF)
    qkv = dot(hidden_one, w_qkv)
    query = rotate(qkv[:, :span].reshape(group, HEADS_DEV, HD), cosine, sine).astype(BF)
    key = rotate(qkv[:, span : 2 * span].reshape(group, HEADS_DEV, HD), cosine, sine).astype(BF)
    value = qkv[:, 2 * span :].astype(BF).reshape(group, HEADS_DEV, HD)
    allowed = (pos[None, :] <= pos[:, None]) & (
        (live[None, :] > 0.5) | (pos[None, :] == pos[:, None])
    )
    scale = HD**-0.5
    scores = jnp.einsum("qhd,khd->hqk", query, key, preferred_element_type=F32) * scale
    scores = jnp.where(allowed[None], scores, -1e30)
    top_score = jnp.max(scores, axis=-1, keepdims=True)
    exponent = jnp.exp(scores - top_score)
    probs = exponent / jnp.sum(exponent, axis=-1, keepdims=True)
    attend = jnp.einsum("hqk,khd->qhd", probs.astype(BF), value, preferred_element_type=F32)
    heads = attend.reshape(8, rows, span).astype(BF)

    live_col = live_own[:, None]
    residual, attended, hidden_all = call_b(heads, tokens, live_col, w_out, gain_two[None])
    hidden_all = hidden_all.reshape(group, width)

    logits = dot(hidden_all, router)
    router_probs = jax.nn.softmax(logits, axis=-1)
    named = jnp.any(
        routes_all[:, :, None] == jnp.arange(experts, dtype=jnp.int32)[None, None, :], axis=1
    )
    gates = jnp.where(named, router_probs, 0.0) * live[:, None]
    expert_ids = ep * exp_dev + jnp.arange(exp_dev)
    pick = (expert_ids[:, None] == jnp.arange(experts)[None, :]).astype(F32)
    weight = jnp.sum(gates[:, None, :] * pick[None], axis=2)
    routed_here = jnp.sum(named.astype(F32)[:, None, :] * pick[None], axis=2)

    def pair_back(gate, up, grad):
        sig = jax.nn.sigmoid(gate)
        silu = gate * sig
        return grad * up * (sig + silu * (1.0 - sig)), grad * silu

    gate_val = jnp.einsum("td,edf->etf", hidden_all, expert_gate, preferred_element_type=F32)
    up_val = jnp.einsum("td,edf->etf", hidden_all, expert_up, preferred_element_type=F32)
    act = jax.nn.silu(gate_val) * up_val
    raw = jnp.einsum("td,efd->etf", cot_all, expert_down, preferred_element_type=F32)
    weight_t = weight.T[:, :, None]
    wact = (act * weight_t).astype(BF)
    q_here = jnp.sum(act * raw, axis=2).T * routed_here
    g_a, g_b = pair_back(gate_val, up_val, raw * weight_t)
    g_a, g_b = g_a.astype(BF), g_b.astype(BF)
    d_eg = jnp.einsum("td,etf->edf", hidden_all, g_a, preferred_element_type=F32).astype(BF)
    d_eu = jnp.einsum("td,etf->edf", hidden_all, g_b, preferred_element_type=F32).astype(BF)
    d_ed = jnp.einsum("etf,td->efd", wact, cot_all, preferred_element_type=F32).astype(BF)

    s_gate = dot(hidden_all, w_gate)
    s_up = dot(hidden_all, w_up)
    s_act = (jax.nn.silu(s_gate) * s_up * live[:, None]).astype(BF)
    s_raw = dot_nt(cot_all, w_down) * live[:, None]
    sg_a, sg_b = pair_back(s_gate, s_up, s_raw)
    sg_a, sg_b = sg_a.astype(BF), sg_b.astype(BF)
    d_sg, d_su = dot_tn(hidden_all, sg_a), dot_tn(hidden_all, sg_b)
    d_sd = dot_tn(s_act, cot_all)

    out_part = jnp.einsum("etf,efd->td", wact, expert_down, preferred_element_type=F32) + dot(
        s_act, w_down
    )
    grad_part = (
        jnp.einsum("etf,edf->td", g_a, expert_gate, preferred_element_type=F32)
        + jnp.einsum("etf,edf->td", g_b, expert_up, preferred_element_type=F32)
        + dot_nt(sg_a, w_gate)
        + dot_nt(sg_b, w_up)
    )
    q_wide = jnp.sum(q_here[:, :, None] * pick[None], axis=1)
    grad_wide = jnp.concatenate(
        [grad_part.astype(BF), jnp.pad(q_wide.astype(BF), ((0, 0), (0, EXTRA - experts)))], axis=1
    )
    own = lambda a: lax.dynamic_slice_in_dim(a, ep * rows, rows, axis=0)
    probs_own = jnp.pad(own(router_probs), ((0, 0), (0, EXTRA - experts)))
    router_wide = jnp.pad(router, ((0, 0), (0, EXTRA - experts)))
    out, g_residual, g_branch, g_logits, d_gain_two, g_heads, sum_gate, sum_up, sum_down = call_c(
        grad_wide.reshape(8, rows, width + EXTRA),
        out_part.astype(BF).reshape(8, rows, width),
        d_eg.reshape(exp_dev, 4, 2, width // 8, hidden),
        d_eu.reshape(exp_dev, 4, 2, width // 8, hidden),
        d_ed.reshape(exp_dev, 4, 2, hidden // 8, width),
        residual, cotangent, live_col, probs_own, w_out, router_wide, gain_two[None],
    )

    g_att = g_heads.reshape(group, HEADS_DEV, HD)
    g_values = jnp.einsum("hqk,qhd->khd", probs.astype(BF), g_att, preferred_element_type=F32)
    g_probs = jnp.einsum("qhd,khd->hqk", g_att, value, preferred_element_type=F32)
    delta = jnp.sum(probs * g_probs, axis=-1, keepdims=True)
    g_scores = (probs * (g_probs - delta)).astype(BF)
    g_query = jnp.einsum("hqk,khd->qhd", g_scores, key, preferred_element_type=F32) * scale
    g_key = jnp.einsum("hqk,qhd->khd", g_scores, query, preferred_element_type=F32) * scale
    g_qkv = jnp.concatenate(
        [
            rotate(g_query, cosine, -sine).reshape(group, span),
            rotate(g_key, cosine, -sine).reshape(group, span),
            g_values.reshape(group, span),
        ],
        axis=1,
    ).astype(BF)
    d_qkv = dot_tn(hidden_one, g_qkv)
    g_hidden_part = dot_nt(g_qkv, w_qkv)
    d_gain_one = jnp.sum(g_hidden_part * normed_one, axis=0)
    hidden_own = own(hidden_all)
    d_router = lax.dot_general(
        hidden_own.astype(F32), g_logits, (((0,), (0,)), ((), ())),
        preferred_element_type=F32, precision=HIGH,
    )[:, :experts]
    d_out = dot_tn(attended, g_branch)
    d_slices = jnp.concatenate([d_qkv, d_sg, d_su], axis=1).astype(BF)
    d_whole = jnp.concatenate(
        [
            d_out,
            d_router,
            d_gain_one[:, None],
            d_gain_two.reshape(width, 1),
            jnp.zeros((width, EXTRA - experts - 2), F32),
        ],
        axis=1,
    ).astype(BF)
    d_down = jnp.pad(
        d_sd[:shared_cols].reshape(16, down_used, width), ((0, 0), (0, ROW_PAD - down_used), (0, 0))
    ).astype(BF)
    split = lambda a: a.reshape((4, 2, 2, -1, a.shape[-1]))
    g_hidden, e_gate, e_up, e_down, o_slices, o_whole, o_down = call_d(
        g_hidden_part.astype(BF).reshape(8, rows, width),
        sum_gate, sum_up, sum_down,
        split(d_slices), split(d_whole), split(d_down),
    )
    inputs = tokens.astype(F32)
    scale_one, normed_own = norm_parts(inputs)
    k = g_hidden * gain_one
    d_tokens = g_residual + scale_one * (
        k - normed_own * jnp.mean(k * normed_own, axis=-1, keepdims=True)
    )
    o_slices = o_slices[:, :used].astype(F32)
    o_whole = jnp.sum(o_whole[:, :used].astype(F32), axis=0)

    def from_owner(i):
        return o_slices[:owners, :, i * span : (i + 1) * span].transpose(1, 0, 2).reshape(used, width)

    def from_shared(i):
        at = 3 * span + 128 * i
        return (
            o_slices[:, :, at : at + shared_cols]
            .reshape(8, used, 16, down_used)
            .transpose(1, 2, 0, 3)
            .reshape(used, hidden)
        )

    return (
        out,
        d_tokens,
        from_owner(0),
        from_owner(1),
        from_owner(2),
        o_whole[:, :width],
        o_whole[:, width : width + experts],
        from_shared(0),
        from_shared(1),
        o_down[:down_used].astype(F32),
        o_whole[:, width + experts],
        o_whole[:, width + experts + 1],
        e_gate.reshape(exp_dev, width, hidden).astype(F32),
        e_up.reshape(exp_dev, width, hidden).astype(F32),
        e_down.reshape(exp_dev, hidden, width).astype(F32),
    )


def solution(mesh):
    both = ("rep", "ep")
    row = P(both, None)
    expert = P("ep", None, None)
    in_specs = (
        row, row, P("rep"), P(both), row, row, row, row, row, row, row, row, row,
        P(both), P(both), expert, expert, expert,
    )
    out_specs = (
        row, row, row, row, row, row, row, row, row, row, P(both), P(both),
        expert, expert, expert,
    )
    return jax.shard_map(body, mesh=mesh, in_specs=in_specs, out_specs=out_specs, check_vma=False)
```

```python
import functools
import itertools

import jax
import jax.numpy as jnp
import numpy as np
from jax import lax
from jax.experimental import pallas as pl
from jax.experimental.pallas import tpu as pltpu
from jax.sharding import PartitionSpec as P

HD = 128
EPS = 1e-6
BF = jnp.bfloat16
F32 = jnp.float32
MESH = pl.DeviceIdType.MESH
HIGH = lax.Precision.HIGHEST
HEADS_DEV = 2
EXTRA = 128
ROW_PAD = 16
VMEM_LIMIT = 60 << 20


def dot(a, b):
    return jnp.dot(a, b, preferred_element_type=F32)


def dot_nt(a, b):
    return lax.dot_general(a, b, (((1,), (1,)), ((), ())), preferred_element_type=F32)


def dot_tn(a, b):
    return lax.dot_general(a, b, (((0,), (0,)), ((), ())), preferred_element_type=F32)


class Place:
    def __init__(self):
        self.rep = lax.axis_index("rep")
        self.ep = lax.axis_index("ep")
        self.y = self.rep // 4
        self.zl = (self.rep // 2) % 2
        self.core = self.rep % 2
        self.x = self.ep // 2
        self.zh = self.ep % 2

    def rep_at(self, y, zl, core):
        return (y % 4) * 4 + zl * 2 + core

    def ep_at(self, x, zh):
        return (x % 4) * 2 + zh

    def to_x(self, step):
        return (self.rep, self.ep_at(self.x + step, self.zh))

    def to_zh(self):
        return (self.rep, self.ep_at(self.x, 1 - self.zh))

    def to_ep(self, shift):
        return (self.rep, (self.ep + shift) % 8)

    def to_y(self, step):
        return (self.rep_at(self.y + step, self.zl, self.core), self.ep)

    def to_zl(self):
        return (self.rep_at(self.y, 1 - self.zl, self.core), self.ep)

    def to_core(self):
        return (self.rep_at(self.y, self.zl, 1 - self.core), self.ep)


class Copies:
    def __init__(self, send_sem, recv_sem):
        self.send_sem, self.recv_sem = send_sem, recv_sem
        self.number = itertools.count()
        self.sent, self.open = [], []

    def send(self, src, dst, device):
        i = next(self.number)
        copy = pltpu.make_async_remote_copy(
            src_ref=src,
            dst_ref=dst,
            send_sem=self.send_sem.at[i],
            recv_sem=self.recv_sem.at[i],
            device_id=device,
            device_id_type=MESH,
        )
        copy.start()
        self.sent.append(copy)
        self.open.append(copy)
        return copy

    def local(self, src, dst):
        i = next(self.number)
        copy = pltpu.make_async_copy(src, dst, self.recv_sem.at[i])
        copy.start()
        self.open.append(copy)
        return copy

    def arrived(self, copy):
        if any(copy is c for c in self.sent):
            copy.wait_recv()
        else:
            copy.wait()
        self.open = [c for c in self.open if c is not copy]

    def sent_off(self, copy):
        copy.wait_send()
        self.sent = [c for c in self.sent if c is not copy]

    def finish(self):
        for copy in list(self.open):
            self.arrived(copy)
        for copy in self.sent:
            copy.wait_send()


def greet(devices):
    barrier = pltpu.get_barrier_semaphore()
    for device in devices:
        pl.semaphore_signal(barrier, inc=1, device_id=device, device_id_type=MESH)
    pl.semaphore_wait(barrier, len(devices))


def run_streams(*streams):
    live = list(streams)
    while live:
        for stream in list(live):
            try:
                next(stream)
            except StopIteration:
                live.remove(stream)


def half_columns(columns):
    return (columns // 128 + 1) // 2 * 128


def ep_peers(place):
    return [place.to_ep(k) for k in range(1, 8)]


def rep_peers(place):
    return [place.to_y(1), place.to_y(-1), place.to_zl(), place.to_core()]


def gather_ep(cp, place, src, dst, columns):
    cut = half_columns(columns)
    lo, hi = pl.ds(0, cut), pl.ds(cut, columns - cut)
    mine = place.ep
    own = cp.local(src, dst.at[mine])
    right = cp.send(src, dst.at[mine], place.to_x(1))
    left = cp.send(src, dst.at[mine], place.to_x(-1))
    over = cp.send(src, dst.at[mine], place.to_zh())
    yield
    from_left = place.ep_at(place.x - 1, place.zh)
    from_right = place.ep_at(place.x + 1, place.zh)
    from_over = place.ep_at(place.x, 1 - place.zh)
    far = place.ep_at(place.x + 2, place.zh)
    cp.arrived(right)
    half_a = cp.send(dst.at[from_left, :, lo], dst.at[from_left, :, lo], place.to_x(1))
    cp.arrived(left)
    half_b = cp.send(dst.at[from_right, :, hi], dst.at[from_right, :, hi], place.to_x(-1))
    yield
    cp.arrived(over)
    cp.send(dst.at[from_over], dst.at[from_over], place.to_x(1))
    cp.send(dst.at[from_over], dst.at[from_over], place.to_x(-1))
    yield
    cp.arrived(half_a)
    cp.arrived(half_b)
    cp.send(dst.at[far], dst.at[far], place.to_zh())
    yield
    cp.arrived(own)


def gather_ring_y(cp, place, src, dst, columns, slot):
    cut = half_columns(columns)
    lo, hi = pl.ds(0, cut), pl.ds(cut, columns - cut)
    up = cp.send(src, dst.at[slot(place.y)], place.to_y(1))
    down = cp.send(src, dst.at[slot(place.y)], place.to_y(-1))
    yield
    cp.arrived(up)
    below = slot(place.y - 1)
    half_a = cp.send(dst.at[below, :, lo], dst.at[below, :, lo], place.to_y(1))
    cp.arrived(down)
    above = slot(place.y + 1)
    half_b = cp.send(dst.at[above, :, hi], dst.at[above, :, hi], place.to_y(-1))
    yield
    cp.arrived(half_a)
    cp.arrived(half_b)


def gather_rep(cp, place, src, dst, columns, z_first):
    mine = place.rep
    own = cp.local(src, dst.at[mine])
    cp.send(src, dst.at[mine], place.to_core())

    def slot(zl):
        return lambda y: place.rep_at(y, zl, place.core)

    def pass_core(index):
        cp.send(dst.at[index], dst.at[index], place.to_core())

    here, there = slot(place.zl), slot(1 - place.zl)
    if z_first:
        over = cp.send(src, dst.at[mine], place.to_zl())
        first = gather_ring_y(cp, place, src, dst, columns, here)
        next(first)
        yield
        cp.arrived(over)
        second = gather_ring_y(
            cp, place, dst.at[there(place.y)], dst, columns, there
        )
        next(second)
        pass_core(there(place.y))
        yield
        next(first)
        for k in (-1, 1):
            pass_core(here(place.y + k))
        yield
        next(second)
        for k in (-1, 1):
            pass_core(there(place.y + k))
        yield
        next(first, None)
        pass_core(here(place.y + 2))
        yield
        next(second, None)
        pass_core(there(place.y + 2))
    else:
        over = [cp.send(src, dst.at[mine], place.to_zl())]
        ring = gather_ring_y(cp, place, src, dst, columns, here)
        next(ring)
        yield
        next(ring)
        for k in (-1, 1):
            block = dst.at[here(place.y + k)]
            over.append(cp.send(block, block, place.to_zl()))
            pass_core(here(place.y + k))
        yield
        next(ring, None)
        block = dst.at[here(place.y + 2)]
        over.append(cp.send(block, block, place.to_zl()))
        pass_core(here(place.y + 2))
        yield
        for copy, k in zip(over, (0, -1, 1, 2)):
            cp.arrived(copy)
            pass_core(there(place.y + k))
            yield
    cp.arrived(own)


def spread_matrix(rows, blocks, used):
    shape = (rows, blocks * ROW_PAD)
    to = lax.broadcasted_iota(jnp.int32, shape, 0)
    at = lax.broadcasted_iota(jnp.int32, shape, 1)
    return jnp.where((at // ROW_PAD) * used + at % ROW_PAD == to, 1.0, 0.0) * jnp.where(
        at % ROW_PAD < used, 1.0, 0.0
    )


def kernel_a(
    slices, whole, down, tok, cot,
    tok_all, cot_all, w_slices, w_whole, w_down,
    land_slices, land_whole, pack_slices, pack_whole, send_sem, recv_sem,
):
    place = Place()
    cp = Copies(send_sem, recv_sem)
    greet(ep_peers(place) + rep_peers(place))
    first = []
    mine = place.ep
    first.append(cp.local(slices.at[mine], land_slices.at[mine]))
    first.append(cp.local(whole, land_whole.at[mine]))
    for k in range(1, 8):
        first.append(cp.send(slices.at[(mine + k) % 8], land_slices.at[mine], place.to_ep(k)))
        first.append(cp.send(whole, land_whole.at[mine], place.to_ep(k)))
    tok_stream = gather_ep(cp, place, tok, tok_all, tok.shape[1])
    next(tok_stream)
    down_stream = gather_rep(cp, place, down, w_down, down.shape[1], True)
    next(down_stream)
    for copy in first:
        cp.arrived(copy)
    used = pack_slices.shape[0] // 8
    spread = spread_matrix(8 * used, 8, used).astype(BF)
    for land, pack in ((land_slices, pack_slices), (land_whole, pack_whole)):
        columns = land.shape[2]
        step = 128
        for c in range(0, columns, step):
            block = land[:, :, c : c + step].reshape(8 * ROW_PAD, step)
            pack[:, c : c + step] = dot(spread, block).astype(BF)
    slice_stream = gather_rep(cp, place, pack_slices, w_slices, slices.shape[2], False)
    next(slice_stream)
    whole_stream = gather_rep(cp, place, pack_whole, w_whole, whole.shape[1], True)
    next(whole_stream)
    cot_stream = gather_ep(cp, place, cot, cot_all, cot.shape[1])
    run_streams(tok_stream, slice_stream, whole_stream, cot_stream, down_stream)
    cp.finish()


def call_a(slices, whole, down, tok, cot, used):
    anyspace = pl.BlockSpec(memory_space=pl.ANY)
    copies = 160
    return pl.pallas_call(
        kernel_a,
        out_shape=(
            jax.ShapeDtypeStruct((8,) + tok.shape, BF),
            jax.ShapeDtypeStruct((8,) + cot.shape, BF),
            jax.ShapeDtypeStruct((16, 8 * used, slices.shape[2]), BF),
            jax.ShapeDtypeStruct((16, 8 * used, whole.shape[1]), BF),
            jax.ShapeDtypeStruct((16,) + down.shape, BF),
        ),
        in_specs=[anyspace] * 5,
        out_specs=(anyspace,) * 5,
        scratch_shapes=[
            pltpu.VMEM((8, ROW_PAD, slices.shape[2]), BF),
            pltpu.VMEM((8, ROW_PAD, whole.shape[1]), BF),
            pltpu.VMEM((8 * used, slices.shape[2]), BF),
            pltpu.VMEM((8 * used, whole.shape[1]), BF),
            pltpu.SemaphoreType.DMA((copies,)),
            pltpu.SemaphoreType.DMA((copies,)),
        ],
        compiler_params=pltpu.CompilerParams(
            collective_id=0, has_side_effects=True, vmem_limit_bytes=VMEM_LIMIT
        ),
        name="gather_inputs",
    )(slices, whole, down, tok, cot)


def kernel_b(
    heads, tok, live, w_out, gain,
    residual, attended, hidden_all,
    land, hidden, send_sem, recv_sem,
):
    place = Place()
    cp = Copies(send_sem, recv_sem)
    greet(ep_peers(place))
    rows, width = tok.shape
    mine = place.ep
    span = heads.shape[2]
    column = pl.ds(pl.multiple_of(mine * span, 128), span)
    first = [cp.local(heads.at[mine], land.at[:, column])]
    for k in range(1, 8):
        first.append(cp.send(heads.at[(mine + k) % 8], land.at[:, column], place.to_ep(k)))
    for copy in first:
        cp.arrived(copy)
    low = land[:, :width]
    attended[...] = low
    step = 256
    squares = jnp.zeros((rows, 1), F32)
    for c in range(0, width, step):
        part = tok[:, c : c + step].astype(F32) + live[...] * dot(low, w_out[:, c : c + step])
        residual[:, c : c + step] = part
        squares += jnp.sum(part * part, axis=1, keepdims=True)
    scale = lax.rsqrt(squares / width + EPS)
    hidden[...] = (residual[...] * scale * gain[...]).astype(BF)
    run_streams(gather_ep(cp, place, hidden, hidden_all, width))
    cp.finish()


def call_b(heads, tok, live, w_out, gain):
    anyspace = pl.BlockSpec(memory_space=pl.ANY)
    vmem = pl.BlockSpec(memory_space=pltpu.VMEM)
    rows, width = tok.shape
    return pl.pallas_call(
        kernel_b,
        out_shape=(
            jax.ShapeDtypeStruct((rows, width), F32),
            jax.ShapeDtypeStruct((rows, width), BF),
            jax.ShapeDtypeStruct((8, rows, width), BF),
        ),
        in_specs=[anyspace, vmem, vmem, vmem, vmem],
        out_specs=(vmem, vmem, anyspace),
        scratch_shapes=[
            pltpu.VMEM((rows, 8 * heads.shape[2]), BF),
            pltpu.VMEM((rows, width), BF),
            pltpu.SemaphoreType.DMA((32,)),
            pltpu.SemaphoreType.DMA((32,)),
        ],
        compiler_params=pltpu.CompilerParams(
            collective_id=1, has_side_effects=True, vmem_limit_bytes=VMEM_LIMIT
        ),
        name="attention_out",
    )(heads, tok, live, w_out, gain)


def add_into(out, terms):
    lead = out.shape[:-2]
    rows = out.shape[-2]

    for index in itertools.product(*(range(n) for n in lead)):

        @pl.loop(0, rows // ROW_PAD)
        def _(i):
            at = index + (pl.ds(pl.multiple_of(i * ROW_PAD, ROW_PAD), ROW_PAD),)
            total = terms[0][at].astype(F32)
            for term in terms[1:]:
                total += term[at].astype(F32)
            out[at] = total.astype(out.dtype)


class Grid:
    def __init__(self, ring, pair, up, down, over):
        self.here, self.up_at, self.down_at, self.far = ring, (ring + 1) % 4, (ring + 3) % 4, (ring + 2) % 4
        self.pair, self.other = pair, 1 - pair
        self.up, self.down, self.over = up, down, over


def grid_rep(place):
    return Grid(place.y, place.zl, place.to_y(1), place.to_y(-1), place.to_zl())


def grid_ep(place):
    return Grid(place.x, place.zh, place.to_x(1), place.to_x(-1), place.to_zh())


def ring_pair_bufs(rows, columns):
    return [pltpu.VMEM((8, rows, columns), BF)]


def sum_ring_pair(cp, g, source, mine, bufs, out):
    (buf,) = bufs
    near, last, half, over = (0, 1), ((2, 3), (4, 5)), 6, 7
    b = lambda i: buf.at[i]
    s1 = cp.send(source.at[g.far, 0], b(near[0]), g.up)
    s2 = cp.send(source.at[g.far, 1], b(near[1]), g.down)
    s3 = cp.send(source.at[g.up_at, 1], b(last[0][1]), g.up)
    s4 = cp.send(source.at[g.down_at, 0], b(last[1][0]), g.down)
    yield
    cp.arrived(s1)
    add_into(mine.at[g.up_at, 0], [mine.at[g.up_at, 0], b(near[0])])
    s5 = cp.send(mine.at[g.up_at, 0], b(last[0][0]), g.up)
    cp.arrived(s2)
    add_into(mine.at[g.down_at, 1], [mine.at[g.down_at, 1], b(near[1])])
    s6 = cp.send(mine.at[g.down_at, 1], b(last[1][1]), g.down)
    yield
    for copy in (s3, s4, s5, s6):
        cp.arrived(copy)
    add_into(
        b(half),
        [mine.at[g.here, g.other], buf.at[2 + g.other], buf.at[4 + g.other]],
    )
    s7 = cp.send(b(half), b(over), g.over)
    yield
    cp.arrived(s7)
    add_into(
        out, [mine.at[g.here, g.pair], buf.at[2 + g.pair], buf.at[4 + g.pair], b(over)]
    )
    for copy in (s1, s2, s3, s4, s5, s6, s7):
        cp.sent_off(copy)


def pair_ring_bufs(rows, columns):
    cut = half_columns(columns)
    return [
        pltpu.VMEM((4, rows, columns), BF),
        pltpu.VMEM((2, rows, columns), BF),
        pltpu.VMEM((rows, cut), BF),
        pltpu.VMEM((rows, columns - cut), BF),
    ]


def sum_pair_ring(cp, g, source, mine, bufs, out):
    acc, last, near_lo, near_hi = bufs
    columns = acc.shape[2]
    cut = half_columns(columns)
    lo, hi = pl.ds(0, cut), pl.ds(cut, columns - cut)
    s0 = cp.send(source.at[:, g.other], acc, g.over)
    yield
    cp.arrived(s0)
    for k in range(4):
        add_into(acc.at[k], [acc.at[k], mine.at[k, g.pair]])
    s1 = cp.send(acc.at[g.far, :, lo], near_lo, g.up)
    s2 = cp.send(acc.at[g.far, :, hi], near_hi, g.down)
    s3 = cp.send(acc.at[g.up_at, :, hi], last.at[0, :, hi], g.up)
    s4 = cp.send(acc.at[g.down_at, :, lo], last.at[1, :, lo], g.down)
    yield
    cp.arrived(s1)
    part = acc.at[g.up_at, :, lo]
    add_into(part, [part, near_lo])
    s5 = cp.send(part, last.at[0, :, lo], g.up)
    cp.arrived(s2)
    part = acc.at[g.down_at, :, hi]
    add_into(part, [part, near_hi])
    s6 = cp.send(part, last.at[1, :, hi], g.down)
    yield
    for copy in (s3, s4, s5, s6):
        cp.arrived(copy)
    add_into(out, [acc.at[g.here], last.at[0], last.at[1]])


def gather_expert(cp, place, src, dst, z_first):
    core, y, zl = place.core, place.y, place.zl
    other = 1 - zl
    columns = src.shape[1]
    cut = half_columns(columns)
    lo, hi = pl.ds(0, cut), pl.ds(cut, columns - cut)
    up, down, over, mate = place.to_y(1), place.to_y(-1), place.to_zl(), place.to_core()

    def at(k, z):
        return dst.at[core, (y + k) % 4, z]

    def forward(k, z, to):
        return cp.send(at(k, z), at(k, z), to)

    def ring_halves(z):
        a = cp.send(at(-1, z).at[:, lo], at(-1, z).at[:, lo], up)
        b = cp.send(at(1, z).at[:, hi], at(1, z).at[:, hi], down)
        return a, b

    own = cp.local(src, at(0, zl))
    first = [cp.send(src, at(0, zl), to) for to in (up, down)]
    across = cp.send(src, at(0, zl), over)
    cp.send(src, at(0, zl), mate)
    yield
    if z_first:
        cp.arrived(across)
        second = [forward(0, other, to) for to in (up, down)]
        forward(0, other, mate)
        yield
        halves = []
        for pair, z in ((first, zl), (second, other)):
            for copy in pair:
                cp.arrived(copy)
            halves.append(ring_halves(z))
            forward(-1, z, mate)
            forward(1, z, mate)
            yield
        for pair, z in zip(halves, (zl, other)):
            for copy in pair:
                cp.arrived(copy)
            forward(2, z, mate)
            yield
    else:
        for copy in first:
            cp.arrived(copy)
        halves = ring_halves(zl)
        crossed = [across]
        for k in (-1, 1):
            crossed.append(forward(k, zl, over))
            forward(k, zl, mate)
        yield
        for copy in halves:
            cp.arrived(copy)
        crossed.append(forward(2, zl, over))
        forward(2, zl, mate)
        yield
        for copy, k in zip(crossed, (0, -1, 1, 2)):
            cp.arrived(copy)
            forward(k, other, mate)
            yield
    cp.arrived(own)


def expert_stream(cp, place, grad, tiles, got, bufs, total, dst, ring_first):
    b = cp.send(grad.at[1 - place.core], got, place.to_core())
    places = list(itertools.product(range(4), range(2)))
    load = lambda n: cp.local(grad.at[(place.core,) + places[n]], tiles.at[n % 2])
    yield
    loads = [load(0), load(1)]
    cp.arrived(b)
    for n, at in enumerate(places):
        cp.arrived(loads[n])
        add_into(got.at[at], [got.at[at], tiles.at[n % 2]])
        if n + 2 < len(places):
            loads.append(load(n + 2))
    summed = sum_ring_pair if ring_first else sum_pair_ring
    yield from summed(cp, grid_rep(place), got, got, bufs, total)
    yield from gather_expert(cp, place, total, dst, ring_first)


def dense_stream(cp, place, grad, got, bufs, total, ring_first):
    b = cp.send(grad.at[:, :, 1 - place.core], got, place.to_core())
    yield
    cp.arrived(b)
    own = grad.at[:, :, place.core]
    add_into(got, [got, own])
    summed = sum_ring_pair if ring_first else sum_pair_ring
    yield from summed(cp, grid_rep(place), got, got, bufs, total)


def spread_stream(cp, place, stream, total, padded, result):
    yield from stream
    used = total.shape[0] // 8
    spread = spread_matrix(8 * used, 8, used).astype(BF)
    columns = total.shape[1]
    for c in range(0, columns, 128):
        padded[:, :, c : c + 128] = (
            dot_tn(spread, total[:, c : c + 128]).astype(BF).reshape(8, ROW_PAD, 128)
        )
    cp.local(padded.at[place.ep], result.at[place.ep])
    for k in range(1, 8):
        cp.send(padded.at[(place.ep + k) % 8], result.at[place.ep], place.to_ep(k))


def advance(*streams):
    for stream in streams:
        next(stream, None)


def kernel_back(
    grads, outs, eg, eu, ed, d_shared, d_down, h_probs, h_hidden, h_qkv,
    w_slices, residual, cot, tok, live, probs, attended, w_whole, gain_one, gain_two, cosine, sine,
    out, d_tok, x_gate, x_up, x_down, o_qkv, o_shared, o_whole, o_down,
    m_grads, m_outs, b_grads, b_outs, total_grads, total_hidden,
    e_own, e_got, e_bufs, e_total,
    v_shared, v_whole, v_qkv, v_down, got, bufs, totals, padded,
    g_att, g_heads, g_residual, g_keys, g_values, g_qkv, v_probs, v_hidden, v_qkvs, v_w, g_branch,
    send_sem, recv_sem,
):
    place = Place()
    cp = Copies(send_sem, recv_sem)
    greet(ep_peers(place) + rep_peers(place))
    rows, width = residual.shape
    mine = place.ep
    ge = grid_ep(place)
    wide = width + EXTRA
    cuts = (pl.ds(0, wide // 2 // 128 * 128), pl.ds(wide // 2 // 128 * 128, wide - wide // 2 // 128 * 128))

    def view(ref, c):
        return ref.at[:, :, :, c]

    load = cp.local(grads, m_grads)
    xs = [
        sum_ring_pair(cp, ge, view(grads, c), view(m_grads, c), b, total_grads.at[:, c])
        for c, b in zip(cuts, b_grads)
    ]
    advance(*xs)
    es = [
        expert_stream(cp, place, g, own, got_, b, t, x, first)
        for g, own, got_, b, t, x, first in zip(
            (eg, eu, ed), (e_own[0], e_own[0], e_own[1]), e_got, e_bufs, e_total, (x_gate, x_up, x_down), (True, True, False)
        )
    ]
    advance(*es)
    loads = [
        cp.local(a, b)
        for a, b in (
            (d_shared, v_shared), (d_down, v_down), (h_hidden, v_hidden), (h_qkv, v_qkvs), (h_probs, v_probs),
            (w_slices.at[:, : v_w.shape[1]], v_w),
        )
    ]
    cp.arrived(load)
    advance(es[0], es[1])
    advance(*xs)
    advance(es[2])
    advance(*xs)
    advance(es[0])
    advance(*xs)

    alive = live[...]
    router_grad = total_grads[:, width:] * alive
    prob = probs[...]
    logit_grad = prob * (router_grad - jnp.sum(prob * router_grad, axis=1, keepdims=True))
    step = 256
    squares = jnp.zeros((rows, 1), F32)
    mean_k = jnp.zeros((rows, 1), F32)
    for c in range(0, width, step):
        part = residual[:, c : c + step]
        squares += jnp.sum(part * part, axis=1, keepdims=True)
    scale = lax.rsqrt(squares / width + EPS)
    gain_rows = []
    for c in range(0, width, step):
        k = total_grads[:, c : c + step] + lax.dot_general(
            logit_grad, w_whole[c : c + step, width:].astype(F32), (((1,), (1,)), ((), ())),
            preferred_element_type=F32, precision=HIGH,
        )
        normed = residual[:, c : c + step] * scale
        gain_rows.append(jnp.sum(k * normed, axis=0, keepdims=True))
        k = k * gain_two[:, c : c + step]
        mean_k += jnp.sum(k * normed, axis=1, keepdims=True)
        g_residual[:, c : c + step] = k
    mean_k = mean_k / width
    for c in range(0, width, step):
        normed = residual[:, c : c + step] * scale
        grad = cot[:, c : c + step].astype(F32) + scale * (
            g_residual[:, c : c + step] - normed * mean_k
        )
        g_residual[:, c : c + step] = grad
        g_branch[:, c : c + step] = (alive * grad).astype(BF)
    g_att[...] = jnp.zeros_like(g_att)
    low = g_branch[...]
    for c in range(0, width, step):
        g_att[c // step] = dot_nt(low, w_whole[c : c + step, :width]).astype(BF)
    third = [cp.local(g_att.at[mine], g_heads.at[mine])]
    for k in range(1, 8):
        third.append(cp.send(g_att.at[(mine + k) % 8], g_heads.at[mine], place.to_ep(k)))

    advance(es[1])
    for i in range(2):
        c = slice(i * width // 2, (i + 1) * width // 2)
        v_whole[2 * i : 2 * i + 2, :, :, :, :width] = (
            dot_tn(attended[:, c], low).astype(BF).reshape(2, 2, 2, width // 16, width)
        )
        hid = (residual[:, c] * scale * gain_two[:, c]).astype(BF).astype(F32)
        small = lax.dot_general(
            hid, logit_grad, (((0,), (0,)), ((), ())), preferred_element_type=F32, precision=HIGH
        )
        gain_row = jnp.concatenate(gain_rows, axis=1)[:, c]
        lane = lax.broadcasted_iota(jnp.int32, (width // 2, EXTRA), 1)
        column = jnp.broadcast_to(gain_row, (8, width // 2)).T[:, :1]
        small = jnp.where(lane == EXTRA - 1, column, small)
        v_whole[2 * i : 2 * i + 2, :, :, :, width:] = small.astype(BF).reshape(
            2, 2, 2, width // 16, EXTRA
        )
    for copy in loads:
        cp.arrived(copy)
    dense = [
        dense_stream(cp, place, v, g, b, t, first)
        for v, g, b, t, first in zip(
            (v_whole, v_shared, v_down, v_qkv), got, bufs, totals, (False, True, True, True)
        )
    ]
    ds = [
        spread_stream(cp, place, dense[0], totals[0], padded[0], o_whole),
        spread_stream(cp, place, dense[1], totals[1], padded[1], o_shared),
        dense[2],
        spread_stream(cp, place, dense[3], totals[3], padded[2], o_qkv),
    ]
    advance(*ds[:3])
    load = cp.local(outs, m_outs)
    os = sum_ring_pair(cp, ge, outs, m_outs, b_outs, total_hidden)
    advance(os)
    advance(es[2], es[0])
    for copy in third:
        cp.arrived(copy)

    group = 8 * rows
    span = HEADS_DEV * HD
    for h in range(HEADS_DEV):
        attention_back_head(h, g_heads, v_qkvs, v_probs, cosine, sine, g_keys, g_values, g_qkv)
        if h == 0:
            cp.arrived(load)
        advance(*ds[:3])
        advance(*es)
        advance(os)

    @pl.loop(0, group // BLOCK)
    def _(i):
        at = pl.ds(pl.multiple_of(i * BLOCK, BLOCK), BLOCK)
        part = dot_nt(g_qkv[at, :], v_w[...]).astype(BF)
        m_grads[i, :, :, :width] = part.reshape(2, rows, width)

    half = width // 2 // 128 * 128
    hcuts = (pl.ds(0, half), pl.ds(half, width - half))
    b_hidden = [[b.at[:, :, pl.ds(0, c.size)]] for (b,), c in zip(b_grads, hcuts)]
    advance(os)
    for c in range(0, width, step):
        out[:, c : c + step] = (residual[:, c : c + step] + total_hidden[:, c : c + step]).astype(BF)
    hs = [
        sum_ring_pair(cp, ge, view(m_grads, c), view(m_grads, c), b, total_hidden.at[:, c])
        for c, b in zip(hcuts, b_hidden)
    ]
    advance(*hs)
    for i in range(2):
        c = slice(i * width // 2, (i + 1) * width // 2)
        v_qkv[2 * i : 2 * i + 2] = (
            dot_tn(v_hidden[:, c], g_qkv[...]).astype(BF).reshape(2, 2, 2, width // 16, 3 * span)
        )
    advance(ds[3])
    advance(*es)
    advance(hs[0], ds[3], hs[1], *ds[:3])
    advance(*es)
    advance(hs[0], ds[3], hs[1], *ds[:3])
    advance(*es)
    advance(hs[0], hs[1])
    squares = jnp.zeros((rows, 1), F32)
    mean_k = jnp.zeros((rows, 1), F32)
    for c in range(0, width, step):
        part = tok[:, c : c + step].astype(F32)
        squares += jnp.sum(part * part, axis=1, keepdims=True)
    scale = lax.rsqrt(squares / width + EPS)
    for c in range(0, width, step):
        normed = tok[:, c : c + step].astype(F32) * scale
        k = total_hidden[:, c : c + step] * gain_one[:, c : c + step]
        mean_k += jnp.sum(k * normed, axis=1, keepdims=True)
    mean_k = mean_k / width
    for c in range(0, width, step):
        normed = tok[:, c : c + step].astype(F32) * scale
        k = total_hidden[:, c : c + step] * gain_one[:, c : c + step]
        d_tok[:, c : c + step] = g_residual[:, c : c + step] + scale * (k - normed * mean_k)
    run_streams(ds[3], *ds[:3], *es, os, *hs, *xs)
    o_down[...] = totals[2][...]
    cp.finish()


def call_back(
    grads, outs, eg, eu, ed, d_shared, d_down, h_probs, h_hidden, h_qkv,
    w_slices, residual, cot, tok, live, probs, attended, w_whole, gain_one, gain_two, cosine, sine,
):
    anyspace = pl.BlockSpec(memory_space=pl.ANY)
    vmem = pl.BlockSpec(memory_space=pltpu.VMEM)
    rows, width = residual.shape
    group = rows * 8
    span = HEADS_DEV * HD
    wide = width + EXTRA
    cut = wide // 2 // 128 * 128
    experts = [g.shape[3:] for g in (eg, eu, ed)]
    part = width // 16
    columns = (wide, d_shared.shape[4], width, 3 * span)
    depth = (part, part, ROW_PAD, part)
    orders = (False, True, True, True)
    bufs_of = lambda first, r, c: (ring_pair_bufs if first else pair_ring_bufs)(r, c)
    return pl.pallas_call(
        kernel_back,
        out_shape=(
            jax.ShapeDtypeStruct((rows, width), BF),
            jax.ShapeDtypeStruct((rows, width), F32),
            jax.ShapeDtypeStruct(eg.shape, BF),
            jax.ShapeDtypeStruct(eu.shape, BF),
            jax.ShapeDtypeStruct(ed.shape, BF),
            jax.ShapeDtypeStruct((8, ROW_PAD, 3 * span), BF),
            jax.ShapeDtypeStruct((8, ROW_PAD, columns[1]), BF),
            jax.ShapeDtypeStruct((8, ROW_PAD, wide), BF),
            jax.ShapeDtypeStruct((ROW_PAD, width), BF),
        ),
        in_specs=[anyspace] * 11 + [vmem] * 11,
        out_specs=(vmem, vmem) + (anyspace,) * 6 + (vmem,),
        scratch_shapes=[
            pltpu.VMEM((4, 2, rows, wide), BF),
            pltpu.VMEM((4, 2, rows, width), BF),
            [ring_pair_bufs(rows, c) for c in (cut, wide - cut)],
            ring_pair_bufs(rows, width),
            pltpu.VMEM((rows, wide), F32),
            pltpu.VMEM((rows, width), F32),
            [pltpu.VMEM((2,) + s, BF) for s in experts[1:]],
            [pltpu.VMEM((4, 2) + s, BF) for s in experts],
            [bufs_of(first, *s) for first, s in zip((True, True, False), experts)],
            [pltpu.VMEM(s, BF) for s in experts],
            pltpu.VMEM(d_shared.shape, BF),
            pltpu.VMEM((4, 2, 2, part, wide), BF),
            pltpu.VMEM((4, 2, 2, part, 3 * span), BF),
            pltpu.VMEM(d_down.shape, BF),
            [pltpu.VMEM((4, 2, r, c), BF) for r, c in zip(depth, columns)],
            [bufs_of(first, r, c) for first, r, c in zip(orders, depth, columns)],
            [pltpu.VMEM((r, c), BF) for r, c in zip(depth, columns)],
            [pltpu.VMEM((8, ROW_PAD, columns[i]), BF) for i in (0, 1, 3)],
            pltpu.VMEM((8, rows, span), BF),
            pltpu.VMEM((8, rows, span), BF),
            pltpu.VMEM((rows, width), F32),
            pltpu.VMEM((group, HD), F32),
            pltpu.VMEM((group, HD), F32),
            pltpu.VMEM((group, 3 * span), BF),
            pltpu.VMEM(h_probs.shape, BF),
            pltpu.VMEM(h_hidden.shape, BF),
            pltpu.VMEM(h_qkv.shape, BF),
            pltpu.VMEM((width, 3 * span), BF),
            pltpu.VMEM((rows, width), BF),
            pltpu.SemaphoreType.DMA((320,)),
            pltpu.SemaphoreType.DMA((320,)),
        ],
        compiler_params=pltpu.CompilerParams(
            collective_id=2, has_side_effects=True, vmem_limit_bytes=int(63.9 * 2**20)
        ),
        name="backward",
    )(
        grads, outs, eg, eu, ed, d_shared, d_down, h_probs, h_hidden, h_qkv,
        w_slices, residual, cot, tok, live, probs, attended, w_whole, gain_one, gain_two, cosine, sine,
    )


BLOCK = 256


def turn(values, cosine, sine):
    return values * cosine + pltpu.roll(values, HD // 2, 1) * sine


def attention_forward(tok, gain, w_slices, live, cosine, sine, hidden, qkv, probs, heads):
    group, width = hidden.shape
    span = HEADS_DEV * HD

    @pl.loop(0, group // BLOCK)
    def _(i):
        at = pl.ds(pl.multiple_of(i * BLOCK, BLOCK), BLOCK)
        values = tok[at, :width].astype(F32)
        scale = lax.rsqrt(jnp.sum(values * values, axis=1, keepdims=True) / width + EPS)
        low = (values * scale * gain[...]).astype(BF)
        hidden[at, :] = low
        raw = dot(low, w_slices[:, : 3 * span])
        cos, sin = cosine[at, :], sine[at, :]
        for h in range(2 * HEADS_DEV):
            c = slice(h * HD, (h + 1) * HD)
            qkv[at, c] = turn(raw[:, c], cos, sin).astype(BF)
        qkv[at, 2 * span :] = raw[:, 2 * span :].astype(BF)

    rows = lax.broadcasted_iota(jnp.int32, (BLOCK, BLOCK), 0)
    columns = lax.broadcasted_iota(jnp.int32, (BLOCK, BLOCK), 1)
    for h in range(HEADS_DEV):
        q, k, v = (slice(n * span + h * HD, n * span + (h + 1) * HD) for n in range(3))
        for i in range(group // BLOCK):
            at = slice(i * BLOCK, (i + 1) * BLOCK)
            n = (i + 1) * BLOCK
            scores = dot_nt(qkv[at, q], qkv[:n, k]) * HD**-0.5
            parts = []
            for j in range(i + 1):
                alive = live[:, j * BLOCK : (j + 1) * BLOCK] > 0.5
                if j == i:
                    alive = (alive & (columns < rows)) | (columns == rows)
                parts.append(jnp.where(alive, scores[:, j * BLOCK : (j + 1) * BLOCK], -1e30))
            scores = jnp.concatenate(parts, axis=1) if len(parts) > 1 else parts[0]
            top = jnp.max(scores, axis=1, keepdims=True)
            weights = jnp.exp(scores - top)
            low = (weights * (1.0 / jnp.sum(weights, axis=1, keepdims=True))).astype(BF)
            probs[h, at, :n] = low
            heads[at, h * HD : (h + 1) * HD] = dot(low, qkv[:n, v]).astype(BF)


def call_attention(tok, gain, w_slices, live, cosine, sine, width):
    group = tok.shape[0]
    vmem = pl.BlockSpec(memory_space=pltpu.VMEM)
    span = HEADS_DEV * HD
    return pl.pallas_call(
        attention_forward,
        out_shape=(
            jax.ShapeDtypeStruct((group, width), BF),
            jax.ShapeDtypeStruct((group, 3 * span), BF),
            jax.ShapeDtypeStruct((HEADS_DEV, group, group), BF),
            jax.ShapeDtypeStruct((group, span), BF),
        ),
        in_specs=[vmem] * 6,
        out_specs=(vmem,) * 4,
        compiler_params=pltpu.CompilerParams(vmem_limit_bytes=VMEM_LIMIT),
        name="attention_forward",
    )(tok, gain, w_slices, live, cosine, sine)


def attention_back_head(h, g_heads, qkv, probs, cosine, sine, g_keys, g_values, g_qkv):
    group = qkv.shape[0]
    blocks, rows = g_heads.shape[:2]
    per = BLOCK // rows
    span = HEADS_DEV * HD
    scale = HD**-0.5
    q, k, v = (slice(n * span + h * HD, n * span + (h + 1) * HD) for n in range(3))
    head = slice(h * HD, (h + 1) * HD)
    for i in reversed(range(group // BLOCK)):
        at = slice(i * BLOCK, (i + 1) * BLOCK)
        n = (i + 1) * BLOCK
        g_att = g_heads[i * per : (i + 1) * per, :, head].reshape(BLOCK, HD)
        low = probs[h, at, :n]
        weights = low.astype(F32)
        g_probs = dot_nt(g_att, qkv[:n, v])
        delta = jnp.sum(weights * g_probs, axis=1, keepdims=True)
        g_scores = (weights * (g_probs - delta)).astype(BF)
        g_query = dot(g_scores, qkv[:n, k]) * scale
        g_qkv[at, q] = turn(g_query, cosine[at, :], -sine[at, :]).astype(BF)
        g_key = dot_tn(g_scores, qkv[at, q])
        g_value = dot_tn(low, g_att)
        if i == group // BLOCK - 1:
            g_keys[...] = g_key
            g_values[...] = g_value
        else:
            g_keys[:n, :] += g_key
            g_values[:n, :] += g_value
    g_qkv[:, k] = turn(g_keys[...] * scale, cosine[...], -sine[...]).astype(BF)
    g_qkv[:, v] = g_values[...].astype(BF)


def one_expert(x, g, w_gate, w_up, w_down, weight, mask, wact, g_a, g_b, out, g_x, q_sum, first):
    group, width = g.shape

    @pl.loop(0, group // BLOCK)
    def _(i):
        at = pl.ds(pl.multiple_of(i * BLOCK, BLOCK), BLOCK)
        share = weight(at)
        gate = dot(x[at, :], w_gate[...])
        up = dot(x[at, :], w_up[...])
        raw = dot_nt(g[at, :], w_down[...])
        sig = 1.0 / (1.0 + jnp.exp(-gate))
        silu = gate * sig
        act = silu * up
        if q_sum is not None:
            q_sum(at, jnp.sum(act * raw, axis=1, keepdims=True))
        low = (act * share).astype(BF)
        wact[at, :] = low
        raw = raw * share
        a = (raw * up * (sig + silu * (1.0 - sig))).astype(BF)
        b = (raw * silu).astype(BF)
        g_a[at, :] = a
        g_b[at, :] = b
        part = dot(low, w_down[...])
        back = dot_nt(a, w_gate[...]) + dot_nt(b, w_up[...])
        if first:
            out[at, :] = part.astype(BF)
            g_x[at, :width] = back.astype(BF)
        else:
            out[at, :] = (out[at, :].astype(F32) + part).astype(BF)
            g_x[at, :width] = (g_x[at, :width].astype(F32) + back).astype(BF)


def expert_sums(x, g, wact, g_a, g_b, d_gate, d_up, d_down):
    width = g.shape[1]
    for c in range(0, width, BLOCK):
        left = x[:, c : c + BLOCK]
        d_gate[c : c + BLOCK, :] = dot_tn(left, g_a[...]).astype(BF)
        d_up[c : c + BLOCK, :] = dot_tn(left, g_b[...]).astype(BF)
    hidden = wact.shape[1]
    step = 128
    for c in range(0, hidden, step):
        d_down[c : c + step, :] = dot_tn(wact[:, c : c + step], g[...]).astype(BF)


def experts_kernel(
    experts, top,
    x, g, extra, w_router, s_both, s_padded, e_gate, e_up, e_down,
    out, g_x, probs_own, d_both, d_padded, d_gate, d_up, d_down,
    gates, named, wact, g_a, g_b, swact, sg_a, sg_b, s_down, d_sdown,
):
    step = pl.program_id(0)
    ep = lax.axis_index("ep")
    group, width = g.shape
    exp_dev = pl.num_programs(0)
    expert = ep * exp_dev + step
    lane = lax.broadcasted_iota(jnp.int32, (BLOCK, EXTRA), 1)

    @pl.when(step == 0)
    def _():
        @pl.loop(0, group // BLOCK)
        def _(i):
            at = pl.ds(pl.multiple_of(i * BLOCK, BLOCK), BLOCK)
            logits = jnp.where(lane < experts, dot(x[at, :], w_router[...]), -1e30)
            weights = jnp.exp(logits - jnp.max(logits, axis=1, keepdims=True))
            prob = weights / jnp.sum(weights, axis=1, keepdims=True)
            routes = extra[at, :].astype(F32).astype(jnp.int32)
            chosen = lane == routes[:, 0:1]
            for j in range(1, top):
                chosen = chosen | (lane == routes[:, j : j + 1])
            named[at, :] = jnp.where(chosen, 1.0, 0.0)
            live = extra[at, top : top + 1].astype(F32)
            gates[at, :] = jnp.where(chosen, prob, 0.0) * live
            g_x[at, width:] = jnp.zeros((BLOCK, EXTRA), BF)

        rows = group // 8
        mine = pl.ds(pl.multiple_of(ep * rows, rows), rows)
        own_lane = lane[:rows]
        logits = jnp.where(own_lane < experts, dot(x[mine, :], w_router[...]), -1e30)
        weights = jnp.exp(logits - jnp.max(logits, axis=1, keepdims=True))
        probs_own[...] = weights / jnp.sum(weights, axis=1, keepdims=True)
        shared = s_down.shape[0]
        used = shared // 16 * 7 // 8
        pack = spread_matrix(shared, 16, used).astype(BF)
        s_down[...] = dot(pack, s_padded[...]).astype(BF)
        one_expert(
            x, g, s_both.at[:, :shared], s_both.at[:, shared:], s_down,
            lambda at: extra[at, top : top + 1].astype(F32),
            None, swact, sg_a, sg_b, out, g_x, None, True,
        )
        expert_sums(x, g, swact, sg_a, sg_b, d_both.at[:, :shared], d_both.at[:, shared:], d_sdown)
        d_padded[...] = dot_tn(pack, d_sdown[...]).astype(BF)

    def picked(ref, at):
        return jnp.sum(jnp.where(lane == expert, ref[at, :], 0.0), axis=1, keepdims=True)

    def q_sum(at, value):
        g_x[at, width:] = jnp.where(
            lane == expert, value * named[at, :], g_x[at, width:].astype(F32)
        ).astype(BF)

    one_expert(
        x, g, e_gate.at[0], e_up.at[0], e_down.at[0], lambda at: picked(gates, at),
        None, wact, g_a, g_b, out, g_x, q_sum, False,
    )
    expert_sums(x, g, wact, g_a, g_b, d_gate.at[0], d_up.at[0], d_down.at[0])


def call_experts(x, g, extra, w_router, s_both, s_padded, e_gate, e_up, e_down, experts, top):
    group, width = x.shape
    exp_dev, _, hidden = e_gate.shape
    rows = group // 8
    once = lambda shape: pl.BlockSpec(shape, lambda i: (0,) * len(shape), pipeline_mode=pl.Buffered(1))
    per = lambda a: pl.BlockSpec((1,) + a.shape[1:], lambda i: (i, 0, 0))
    shared = s_both.shape[1] // 2
    return pl.pallas_call(
        functools.partial(experts_kernel, experts, top),
        grid=(exp_dev,),
        out_shape=(
            jax.ShapeDtypeStruct((group, width), BF),
            jax.ShapeDtypeStruct((group, width + EXTRA), BF),
            jax.ShapeDtypeStruct((rows, EXTRA), F32),
            jax.ShapeDtypeStruct((width, 2 * shared), BF),
            jax.ShapeDtypeStruct(s_padded.shape, BF),
            jax.ShapeDtypeStruct(e_gate.shape, BF),
            jax.ShapeDtypeStruct(e_up.shape, BF),
            jax.ShapeDtypeStruct(e_down.shape, BF),
        ),
        in_specs=[once(a.shape) for a in (x, g, extra, w_router, s_both, s_padded)]
        + [per(a) for a in (e_gate, e_up, e_down)],
        out_specs=(
            once((group, width)), once((group, width + EXTRA)), once((rows, EXTRA)),
            once((width, 2 * shared)), once(s_padded.shape),
            per(e_gate), per(e_up), per(e_down),
        ),
        scratch_shapes=[pltpu.VMEM((group, EXTRA), F32)] * 2
        + [pltpu.VMEM((group, hidden), BF)] * 3
        + [pltpu.VMEM((group, shared), BF)] * 3
        + [pltpu.VMEM((shared, width), BF)] * 2,
        compiler_params=pltpu.CompilerParams(
            vmem_limit_bytes=VMEM_LIMIT, dimension_semantics=("arbitrary",)
        ),
        name="experts",
    )(x, g, extra, w_router, s_both, s_padded, e_gate, e_up, e_down)


def pad_rows(values, rows):
    return jnp.pad(values, ((0, rows - values.shape[0]),) + ((0, 0),) * (values.ndim - 1))


def body(
    tokens, cotangent, lengths, token_mask, routes,
    w_query, w_key, w_value, w_output, w_router,
    shared_gate, shared_up, shared_down, norm_attn, norm_ffn,
    expert_gate, expert_up, expert_down,
):
    rows, width = tokens.shape
    top = routes.shape[1]
    used = w_query.shape[0]
    hidden = expert_gate.shape[2]
    experts = w_router.shape[1]
    exp_dev = expert_gate.shape[0]
    ep = lax.axis_index("ep")
    group = rows * 8
    span = HEADS_DEV * HD
    owners = width // span
    down_used = shared_down.shape[0]
    shared_cols = 16 * down_used

    def by_owner(w):
        return jnp.pad(w.reshape(used, owners, span), ((0, 0), (0, 8 - owners), (0, 0)))

    def by_shared(w):
        w = w.reshape(used, 16, 8, down_used).transpose(0, 2, 1, 3).reshape(used, 8, shared_cols)
        return jnp.pad(w, ((0, 0), (0, 0), (0, 128 - shared_cols)))

    slices = jnp.concatenate(
        [by_owner(w_query), by_owner(w_key), by_owner(w_value), by_shared(shared_gate), by_shared(shared_up)],
        axis=2,
    ).transpose(1, 0, 2)
    slices = jnp.pad(slices, ((0, 0), (0, ROW_PAD - used), (0, 0)))
    whole = jnp.concatenate(
        [w_output, w_router, norm_attn[:, None], norm_ffn[:, None]], axis=1
    )
    whole = jnp.pad(whole, ((0, ROW_PAD - used), (0, width + EXTRA - whole.shape[1])))
    down = pad_rows(shared_down, ROW_PAD)
    position = ep * rows + jnp.arange(rows, dtype=jnp.int32)
    live_own = ((position < lengths[0]) & (token_mask == 1)).astype(F32)
    tok_wide = jnp.concatenate(
        [
            tokens,
            jnp.pad(
                jnp.concatenate([routes.astype(BF), live_own[:, None].astype(BF)], axis=1),
                ((0, 0), (0, EXTRA - top - 1)),
            ),
        ],
        axis=1,
    )
    tok_all, cot_all, w_slices, w_whole, w_down = call_a(
        slices, whole, down, tok_wide, cotangent, used
    )
    tok_all = tok_all.reshape(group, width + EXTRA)
    cot_all = cot_all.reshape(group, width)
    w_slices = w_slices.reshape(width, -1)
    w_whole = w_whole.reshape(width, -1)
    w_down = w_down.reshape(-1, width)
    live_row = tok_all[:, width + top].astype(F32)[None]
    gain_one = w_whole[:, width + experts].astype(F32)[None]
    gain_two = w_whole[:, width + experts + 1].astype(F32)[None]
    router = w_whole[:, width:]

    frequency = 10000.0 ** (-(np.arange(HD // 2, dtype=np.float32) * np.float32(2.0) / HD))
    angles = np.arange(group, dtype=np.float32)[:, None] * frequency.astype(np.float32)[None, :]
    cosine = jnp.asarray(np.tile(np.cos(angles), (1, 2)), F32)
    sine = jnp.asarray(np.concatenate([-np.sin(angles), np.sin(angles)], axis=1), F32)
    hidden_one, qkv, attn_probs, heads = call_attention(
        tok_all, gain_one, w_slices, live_row, cosine, sine, width
    )

    live_col = live_own[:, None]
    residual, attended, hidden_all = call_b(
        heads.reshape(8, rows, span), tokens, live_col, w_whole, gain_two
    )
    hidden_all = hidden_all.reshape(group, width)
    out_part, grad_wide, probs_own, d_both, d_down, d_eg, d_eu, d_ed = call_experts(
        hidden_all, cot_all, tok_all[:, width:], router, w_slices[:, 3 * span :], w_down,
        expert_gate, expert_up, expert_down, experts, top,
    )
    part = width // 16
    out, d_tokens, e_gate, e_up, e_down, o_qkv, o_shared, o_whole, o_down = call_back(
        grad_wide.reshape(4, 2, rows, width + EXTRA),
        out_part.reshape(4, 2, rows, width),
        d_eg.reshape(exp_dev, 4, 2, width // 8, hidden),
        d_eu.reshape(exp_dev, 4, 2, width // 8, hidden),
        d_ed.reshape(exp_dev, 4, 2, hidden // 8, width),
        d_both.reshape(4, 2, 2, part, -1),
        d_down.reshape(4, 2, 2, ROW_PAD, width),
        attn_probs, hidden_one, qkv,
        w_slices, residual, cotangent, tokens, live_col, probs_own, attended, w_whole,
        gain_one, gain_two, cosine, sine,
    )
    o_qkv = o_qkv[:owners, :used].astype(F32)
    o_shared = o_shared[:, :used].astype(F32)
    o_whole = jnp.sum(o_whole[:, :used].astype(F32), axis=0)

    def from_owner(i):
        return o_qkv[:, :, i * span : (i + 1) * span].transpose(1, 0, 2).reshape(used, width)

    def from_shared(i):
        return (
            o_shared[:, :, 128 * i : 128 * i + shared_cols]
            .reshape(8, used, 16, down_used)
            .transpose(1, 2, 0, 3)
            .reshape(used, hidden)
        )

    d_query, d_key, d_value = (from_owner(i) for i in range(3))
    d_gain_one = sum(
        jnp.sum(w.astype(F32) * d, axis=1)
        for w, d in ((w_query, d_query), (w_key, d_key), (w_value, d_value))
    ) / norm_attn.astype(F32)
    return (
        out,
        d_tokens,
        d_query,
        d_key,
        d_value,
        o_whole[:, :width],
        o_whole[:, width : width + experts],
        from_shared(0),
        from_shared(1),
        o_down[:down_used].astype(F32),
        d_gain_one,
        o_whole[:, width + EXTRA - 1],
        e_gate.reshape(exp_dev, width, hidden).astype(F32),
        e_up.reshape(exp_dev, width, hidden).astype(F32),
        e_down.reshape(exp_dev, hidden, width).astype(F32),
    )


def solution(mesh):
    both = ("rep", "ep")
    row = P(both, None)
    expert = P("ep", None, None)
    in_specs = (
        row, row, P("rep"), P(both), row, row, row, row, row, row, row, row, row,
        P(both), P(both), expert, expert, expert,
    )
    out_specs = (
        row, row, row, row, row, row, row, row, row, row, P(both), P(both),
        expert, expert, expert,
    )
    return jax.shard_map(body, mesh=mesh, in_specs=in_specs, out_specs=out_specs, check_vma=False)
```

```python
import functools
import itertools
import math

import jax
import jax.numpy as jnp
import numpy as np
from jax import lax
from jax.experimental import pallas as pl
from jax.experimental.pallas import tpu as pltpu
from jax.sharding import PartitionSpec as P

HD = 128
EPS = 1e-6
BF = jnp.bfloat16
F32 = jnp.float32
MESH = pl.DeviceIdType.MESH
HIGH = lax.Precision.HIGHEST
HEADS_DEV = 2
EXTRA = 128
ROW_PAD = 16
VMEM_LIMIT = 60 << 20
LIVE = 7


def dot(a, b):
    return jnp.dot(a, b, preferred_element_type=F32)


def dot_nt(a, b):
    return lax.dot_general(a, b, (((1,), (1,)), ((), ())), preferred_element_type=F32)


def dot_tn(a, b):
    return lax.dot_general(a, b, (((0,), (0,)), ((), ())), preferred_element_type=F32)


class Place:
    def __init__(self):
        self.rep = lax.axis_index("rep")
        self.ep = lax.axis_index("ep")
        self.y = self.rep // 4
        self.zl = (self.rep // 2) % 2
        self.core = self.rep % 2
        self.x = self.ep // 2
        self.zh = self.ep % 2

        self.mate = 1 - self.core
        self.y_at = {k: (self.y + k) % 4 for k in (-1, 0, 1, 2)}
        self._x = {k: (self.rep, self.ep_at(self.x + k, self.zh)) for k in (-1, 1)}
        self._y = {k: (self.rep_at(self.y + k, self.zl, self.core), self.ep) for k in (-1, 1)}
        self._ep = {k: (self.rep, (self.ep + k) % 8) for k in range(1, 8)}
        self._zh = (self.rep, self.ep_at(self.x, 1 - self.zh))
        self._zl = (self.rep_at(self.y, 1 - self.zl, self.core), self.ep)
        self._core = (self.rep_at(self.y, self.zl, self.mate), self.ep)

    def rep_at(self, y, zl, core):
        return (y % 4) * 4 + zl * 2 + core

    def ep_at(self, x, zh):
        return (x % 4) * 2 + zh

    def to_x(self, step):
        return self._x[step]

    def to_zh(self):
        return self._zh

    def to_ep(self, shift):
        return self._ep[shift]

    def to_y(self, step):
        return self._y[step]

    def to_zl(self):
        return self._zl

    def to_core(self):
        return self._core


class Later:
    def __init__(self, ref, path=()):
        self.ref, self.path = ref, path

    @property
    def at(self):
        return LaterAt(self)

    @property
    def shape(self):
        return self.made().shape

    @property
    def dtype(self):
        return self.ref.dtype

    def made(self):
        ref = self.ref
        for index in self.path:
            ref = ref.at[index]
        return ref

    def __getitem__(self, index):
        return self.made()[index]

    def __setitem__(self, index, value):
        self.made()[index] = value


class LaterAt:
    def __init__(self, later):
        self.later = later

    def __getitem__(self, index):
        return Later(self.later.ref, self.later.path + (index,))


def made(ref):
    return ref.made() if isinstance(ref, Later) else ref


class Copies:
    def __init__(self, send_sem, recv_sem):
        self.send_sem, self.recv_sem = send_sem, recv_sem
        self.number = itertools.count()
        self.sent, self.open = [], []

    def send(self, src, dst, device):
        i = next(self.number)

        def copy():
            return pltpu.make_async_remote_copy(
                src_ref=made(src),
                dst_ref=made(dst),
                send_sem=self.send_sem.at[i],
                recv_sem=self.recv_sem.at[i],
                device_id=device,
                device_id_type=MESH,
            )

        copy().start()
        self.sent.append(copy)
        self.open.append(copy)
        return copy

    def local(self, src, dst):
        i = next(self.number)

        def copy():
            return pltpu.make_async_copy(made(src), made(dst), self.recv_sem.at[i])

        copy().start()
        self.open.append(copy)
        return copy

    def arrived(self, copy):
        if any(copy is c for c in self.sent):
            copy().wait_recv()
        else:
            copy().wait()
        self.open = [c for c in self.open if c is not copy]

    def sent_off(self, copy):
        copy().wait_send()
        self.sent = [c for c in self.sent if c is not copy]

    def drain(self, stream):
        for _ in stream:
            pass

    def finish(self):
        for copy in list(self.open):
            self.arrived(copy)
        for copy in list(self.sent):
            self.sent_off(copy)


def greet(devices):
    barrier = pltpu.get_barrier_semaphore()
    for device in devices:
        pl.semaphore_signal(barrier, inc=1, device_id=device, device_id_type=MESH)
    pl.semaphore_wait(barrier, len(devices))


def run_streams(*streams):
    live = list(streams)
    while live:
        for stream in list(live):
            try:
                next(stream)
            except StopIteration:
                live.remove(stream)


def half_columns(columns):
    return (columns // 128 + 1) // 2 * 128


def ep_peers(place):
    return [place.to_ep(k) for k in range(1, 8)]


def rep_peers(place):
    return [place.to_y(1), place.to_y(-1), place.to_zl(), place.to_core()]


def gather_ep(cp, place, src, dst, columns):
    cut = half_columns(columns)
    lo, hi = pl.ds(0, cut), pl.ds(cut, columns - cut)
    mine = place.ep
    own = cp.local(src, dst.at[mine])
    right = cp.send(src, dst.at[mine], place.to_x(1))
    left = cp.send(src, dst.at[mine], place.to_x(-1))
    over = cp.send(src, dst.at[mine], place.to_zh())
    yield
    from_left = place.ep_at(place.x - 1, place.zh)
    from_right = place.ep_at(place.x + 1, place.zh)
    from_over = place.ep_at(place.x, 1 - place.zh)
    far = place.ep_at(place.x + 2, place.zh)
    cp.arrived(right)
    half_a = cp.send(dst.at[from_left, :, lo], dst.at[from_left, :, lo], place.to_x(1))
    cp.arrived(left)
    half_b = cp.send(dst.at[from_right, :, hi], dst.at[from_right, :, hi], place.to_x(-1))
    yield
    cp.arrived(over)
    last = [own]
    last.append(cp.send(dst.at[from_over], dst.at[from_over], place.to_x(1)))
    last.append(cp.send(dst.at[from_over], dst.at[from_over], place.to_x(-1)))
    yield
    cp.arrived(half_a)
    cp.arrived(half_b)
    last.append(cp.send(dst.at[far], dst.at[far], place.to_zh()))
    yield
    for copy in last:
        cp.arrived(copy)


def gather_ring_y(cp, place, src, dst, columns, slot):
    cut = half_columns(columns)
    lo, hi = pl.ds(0, cut), pl.ds(cut, columns - cut)
    up = cp.send(src, dst.at[slot(place.y)], place.to_y(1))
    down = cp.send(src, dst.at[slot(place.y)], place.to_y(-1))
    yield
    cp.arrived(up)
    below = slot(place.y - 1)
    half_a = cp.send(dst.at[below, :, lo], dst.at[below, :, lo], place.to_y(1))
    cp.arrived(down)
    above = slot(place.y + 1)
    half_b = cp.send(dst.at[above, :, hi], dst.at[above, :, hi], place.to_y(-1))
    yield
    cp.arrived(half_a)
    cp.arrived(half_b)


def gather_rep(cp, place, src, dst, columns, z_first):
    mine = place.rep
    last = [cp.local(src, dst.at[mine]), cp.send(src, dst.at[mine], place.to_core())]

    def slot(zl):
        return lambda y: place.rep_at(y, zl, place.core)

    def pass_core(index):
        last.append(cp.send(dst.at[index], dst.at[index], place.to_core()))

    here, there = slot(place.zl), slot(1 - place.zl)
    if z_first:
        over = cp.send(src, dst.at[mine], place.to_zl())
        first = gather_ring_y(cp, place, src, dst, columns, here)
        next(first)
        yield
        cp.arrived(over)
        second = gather_ring_y(
            cp, place, dst.at[there(place.y)], dst, columns, there
        )
        next(second)
        pass_core(there(place.y))
        yield
        next(first)
        for k in (-1, 1):
            pass_core(here(place.y + k))
        yield
        next(second)
        for k in (-1, 1):
            pass_core(there(place.y + k))
        yield
        next(first, None)
        pass_core(here(place.y + 2))
        yield
        next(second, None)
        pass_core(there(place.y + 2))
    else:
        over = [cp.send(src, dst.at[mine], place.to_zl())]
        ring = gather_ring_y(cp, place, src, dst, columns, here)
        next(ring)
        yield
        next(ring)
        for k in (-1, 1):
            block = dst.at[here(place.y + k)]
            over.append(cp.send(block, block, place.to_zl()))
            pass_core(here(place.y + k))
        yield
        next(ring, None)
        block = dst.at[here(place.y + 2)]
        over.append(cp.send(block, block, place.to_zl()))
        pass_core(here(place.y + 2))
        yield
        for copy, k in zip(over, (0, -1, 1, 2)):
            cp.arrived(copy)
            pass_core(there(place.y + k))
            yield
    yield
    for copy in last:
        cp.arrived(copy)


def spread_matrix(rows, blocks, used):
    shape = (rows, blocks * ROW_PAD)
    to = lax.broadcasted_iota(jnp.int32, shape, 0)
    at = lax.broadcasted_iota(jnp.int32, shape, 1)
    return jnp.where((at // ROW_PAD) * used + at % ROW_PAD == to, 1.0, 0.0) * jnp.where(
        at % ROW_PAD < used, 1.0, 0.0
    )


def kernel_front(
    slices, whole, down, tok, cot, live, cosine, sine,
    w_slices, w_both, w_whole, w_router, w_down, cot_all, extra,
    hidden_one, qkv, probs, gains, residual, attended, hidden_all,
    land_slices, land_whole, pack_slices, pack_whole, v_slices, v_whole, v_tok,
    heads, land_heads, hidden, live_row, send_sem, recv_sem,
):
    place = Place()
    cp = Copies(send_sem, recv_sem)
    greet(ep_peers(place) + rep_peers(place))
    rows = tok.shape[0]
    width = cot.shape[1]
    group = 8 * rows
    span = HEADS_DEV * HD
    mine = place.ep

    to_slices = [cp.local(slices.at[mine], land_slices.at[mine])]
    to_whole = [cp.local(whole, land_whole.at[mine])]
    for k in range(1, 8):
        to_slices.append(cp.send(slices.at[(mine + k) % 8], land_slices.at[mine], place.to_ep(k)))
    for k in range(1, 8):
        to_whole.append(cp.send(whole, land_whole.at[mine], place.to_ep(k)))
    toks = gather_ep(cp, place, tok, v_tok, tok.shape[1])
    advance(toks)
    downs = gather_rep(cp, place, down, w_down, down.shape[1], True)
    advance(downs)
    used = pack_slices.shape[0] // 8
    spread = spread_matrix(8 * used, 8, used).astype(BF)

    def pack(land, packed):
        for c in range(0, land.shape[2], 128):
            block = land[:, :, c : c + 128].reshape(8 * ROW_PAD, 128)
            packed[:, c : c + 128] = dot(spread, block).astype(BF)

    for copy in to_slices:
        cp.arrived(copy)
    pack(land_slices, pack_slices)
    sls = gather_rep(cp, place, pack_slices, v_slices, slices.shape[2], True)
    advance(sls)
    for copy in to_whole:
        cp.arrived(copy)
    pack(land_whole, pack_whole)
    advance(toks)
    whs = gather_rep(cp, place, pack_whole, v_whole, whole.shape[1], True)
    advance(sls, whs, toks, sls, toks)
    cots = gather_ep(cp, place, cot, cot_all, width)
    advance(whs, sls)
    cp.drain(toks)
    advance(cots)
    cp.drain(sls)
    outs = [
        cp.local(v_slices, w_slices),
        cp.local(v_slices.at[:, :, pl.ds(3 * span, 256)], w_both),
        cp.local(v_tok.at[:, :, pl.ds(width, EXTRA)], extra),
    ]

    block = v_slices[:, :, 3 * span : 3 * span + 128].reshape(width, 128).astype(F32).T
    gains[...] = block[112:120, :]
    live_row[...] = jnp.concatenate(
        [v_tok[i, :, width:].astype(F32).T[:8, :] for i in range(8)], axis=1
    )
    weights = lambda: v_slices[:, :, : 3 * span].reshape(width, 3 * span)
    per = BLOCK // rows

    @pl.loop(0, group // BLOCK)
    def _(i):
        at = pl.ds(pl.multiple_of(i * BLOCK, BLOCK), BLOCK)
        values = v_tok[pl.ds(i * per, per), :, :width].reshape(BLOCK, width).astype(F32)
        scale = lax.rsqrt(jnp.sum(values * values, axis=1, keepdims=True) / width + EPS)
        low = (values * scale * gains[0:1, :]).astype(BF)
        hidden_one[at, :] = low
        raw = dot(low, weights())
        cos, sin = cosine[at, :], sine[at, :]
        for h in range(2 * HEADS_DEV):
            c = slice(h * HD, (h + 1) * HD)
            qkv[at, c] = turn(raw[:, c], cos, sin).astype(BF)
        qkv[at, 2 * span :] = raw[:, 2 * span :].astype(BF)

    advance(whs, cots)
    for h in range(HEADS_DEV):
        attention_head(h, qkv, live_row, probs, heads)
        advance(whs, cots, downs)
    column = pl.ds(pl.multiple_of(mine * span, 128), span)
    first = [cp.local(heads.at[mine], land_heads.at[:, column])]
    for k in range(1, 8):
        first.append(cp.send(heads.at[(mine + k) % 8], land_heads.at[:, column], place.to_ep(k)))
    cp.drain(whs)
    outs += [
        cp.local(v_whole, w_whole),
        cp.local(v_whole.at[:, :, pl.ds(width, EXTRA)], w_router),
    ]
    advance(cots, downs)
    for copy in first:
        cp.arrived(copy)

    low = land_heads[:, :width]
    attended[...] = low
    step = 256
    squares = jnp.zeros((rows, 1), F32)
    for c in range(0, width, step):
        matrix = v_whole[:, :, c : c + step].reshape(width, step)
        part = tok[:, c : c + step].astype(F32) + live[...] * dot(low, matrix)
        residual[:, c : c + step] = part
        squares += jnp.sum(part * part, axis=1, keepdims=True)
    scale = lax.rsqrt(squares / width + EPS)
    hidden[...] = (residual[...] * scale * gains[1:2, :]).astype(BF)
    run_streams(gather_ep(cp, place, hidden, hidden_all, width), cots, downs)
    cp.finish()


def call_front(slices, whole, down, tok, cot, live, cosine, sine, used):
    anyspace = pl.BlockSpec(memory_space=pl.ANY)
    vmem = pl.BlockSpec(memory_space=pltpu.VMEM)
    rows, width = cot.shape
    group = 8 * rows
    span = HEADS_DEV * HD
    shape = jax.ShapeDtypeStruct
    columns, wide = slices.shape[2], whole.shape[1]
    return pl.pallas_call(
        kernel_front,
        out_shape=(
            shape((16, 8 * used, columns), BF),
            shape((16, 8 * used, columns - 3 * span), BF),
            shape((16, 8 * used, wide), BF),
            shape((16, 8 * used, EXTRA), BF),
            shape((16,) + down.shape, BF),
            shape((8,) + cot.shape, BF),
            shape((8, rows, EXTRA), BF),
            shape((group, width), BF),
            shape((group, 3 * span), BF),
            shape((HEADS_DEV, group, group), BF),
            shape((8, width), F32),
            shape((rows, width), F32),
            shape((rows, width), BF),
            shape((8, rows, width), BF),
        ),
        in_specs=[anyspace] * 3 + [vmem] + [anyspace] + [vmem] * 3,
        out_specs=(anyspace,) * 7 + (vmem,) * 6 + (anyspace,),
        scratch_shapes=[
            pltpu.VMEM((8, ROW_PAD, columns), BF),
            pltpu.VMEM((8, ROW_PAD, wide), BF),
            pltpu.VMEM((8 * used, columns), BF),
            pltpu.VMEM((8 * used, wide), BF),
            pltpu.VMEM((16, 8 * used, columns), BF),
            pltpu.VMEM((16, 8 * used, wide), BF),
            pltpu.VMEM((8,) + tok.shape, BF),
            pltpu.VMEM((8, rows, span), BF),
            pltpu.VMEM((rows, 8 * span), BF),
            pltpu.VMEM((rows, width), BF),
            pltpu.VMEM((8, group), F32),
            pltpu.SemaphoreType.DMA((200,)),
            pltpu.SemaphoreType.DMA((200,)),
        ],
        compiler_params=pltpu.CompilerParams(
            collective_id=0, has_side_effects=True, vmem_limit_bytes=VMEM_LIMIT
        ),
        name="front",
    )(slices, whole, down, tok, cot, live, cosine, sine)


def add_into(out, terms):
    lead = out.shape[:-2]
    count = math.prod(lead)

    def add(index):
        if len(terms) == 2 and out.dtype == BF:
            out[index] = terms[0][index] + terms[1][index]
            return
        total = terms[0][index].astype(F32)
        for term in terms[1:]:
            total += term[index].astype(F32)
        out[index] = total.astype(out.dtype)

    if count == 1:
        add((0,) * len(lead) + (slice(None),))
    else:
        inner = lead[-1] if lead else 1

        @pl.loop(0, count)
        def _(i):
            add(((i // inner, i % inner) if len(lead) == 2 else (i,)) + (slice(None),))


class Grid:
    def __init__(self, ring, pair, up, down, over):
        self.here, self.up_at, self.down_at, self.far = ring, (ring + 1) % 4, (ring + 3) % 4, (ring + 2) % 4
        self.pair, self.other = pair, 1 - pair
        self.up, self.down, self.over = up, down, over


def grid_rep(place):
    return Grid(place.y, place.zl, place.to_y(1), place.to_y(-1), place.to_zl())


def grid_ep(place):
    return Grid(place.x, place.zh, place.to_x(1), place.to_x(-1), place.to_zh())


def ring_pair_bufs(rows, columns):
    return [pltpu.VMEM((7, rows, columns), BF)]


def sum_ring_pair(cp, g, source, mine, bufs, out, more=()):
    (buf,) = bufs
    near, last, half, over = (0, 1), ((2, 3), (4, 5)), 0, 6
    b = lambda i: buf.at[i]
    s1 = cp.send(source.at[g.far, 0], b(near[0]), g.up)
    s2 = cp.send(source.at[g.far, 1], b(near[1]), g.down)
    s3 = cp.send(source.at[g.up_at, 1], b(last[0][1]), g.up)
    s4 = cp.send(source.at[g.down_at, 0], b(last[1][0]), g.down)
    yield
    cp.arrived(s1)
    add_into(mine.at[g.up_at, 0], [mine.at[g.up_at, 0], b(near[0])])
    s5 = cp.send(mine.at[g.up_at, 0], b(last[0][0]), g.up)
    cp.arrived(s2)
    add_into(mine.at[g.down_at, 1], [mine.at[g.down_at, 1], b(near[1])])
    s6 = cp.send(mine.at[g.down_at, 1], b(last[1][1]), g.down)
    yield
    for copy in (s3, s4, s5, s6):
        cp.arrived(copy)
    add_into(
        b(half),
        [mine.at[g.here, g.other], buf.at[2 + g.other], buf.at[4 + g.other]],
    )
    s7 = cp.send(b(half), b(over), g.over)
    yield
    cp.arrived(s7)
    add_into(
        out, [mine.at[g.here, g.pair], buf.at[2 + g.pair], buf.at[4 + g.pair], b(over), *more]
    )
    for copy in (s1, s2, s3, s4, s5, s6, s7):
        cp.sent_off(copy)


def pair_ring_bufs(rows, columns):
    cut = half_columns(columns)
    return [
        pltpu.VMEM((4, rows, columns), BF),
        pltpu.VMEM((2, rows, columns), BF),
        pltpu.VMEM((rows, cut), BF),
        pltpu.VMEM((rows, columns - cut), BF),
    ]


def sum_pair_ring(cp, g, source, mine, bufs, out):
    acc, last, near_lo, near_hi = bufs
    columns = acc.shape[2]
    cut = half_columns(columns)
    lo, hi = pl.ds(0, cut), pl.ds(cut, columns - cut)
    s0 = cp.send(source.at[:, g.other], acc, g.over)
    yield
    cp.arrived(s0)
    add_into(acc, [acc, mine.at[:, g.pair]])
    s1 = cp.send(acc.at[g.far, :, lo], near_lo, g.up)
    s2 = cp.send(acc.at[g.far, :, hi], near_hi, g.down)
    s3 = cp.send(acc.at[g.up_at, :, hi], last.at[0, :, hi], g.up)
    s4 = cp.send(acc.at[g.down_at, :, lo], last.at[1, :, lo], g.down)
    yield
    cp.arrived(s1)
    part = acc.at[g.up_at, :, lo]
    add_into(part, [part, near_lo])
    s5 = cp.send(part, last.at[0, :, lo], g.up)
    cp.arrived(s2)
    part = acc.at[g.down_at, :, hi]
    add_into(part, [part, near_hi])
    s6 = cp.send(part, last.at[1, :, hi], g.down)
    yield
    for copy in (s3, s4, s5, s6):
        cp.arrived(copy)
    add_into(out, [acc.at[g.here], last.at[0], last.at[1]])
    for copy in (s0, s1, s2, s3, s4, s5, s6):
        cp.sent_off(copy)


def gather_expert(cp, place, grid, src, at, z_first):
    zl, other = grid.pair, grid.other
    columns = src.shape[1]
    cut = half_columns(columns)
    lo, hi = pl.ds(0, cut), pl.ds(cut, columns - cut)
    up, down, over, mate = place.to_y(1), place.to_y(-1), place.to_zl(), place.to_core()

    def forward(k, z, to):
        return cp.send(at(k, z), at(k, z), to)

    def ring_halves(z):
        a = cp.send(at(-1, z).at[:, lo], at(-1, z).at[:, lo], up)
        b = cp.send(at(1, z).at[:, hi], at(1, z).at[:, hi], down)
        return a, b

    own = cp.local(src, at(0, zl))
    first = [cp.send(src, at(0, zl), to) for to in (up, down)]
    across = cp.send(src, at(0, zl), over)
    cp.send(src, at(0, zl), mate)
    yield
    if z_first:
        cp.arrived(across)
        second = [forward(0, other, to) for to in (up, down)]
        forward(0, other, mate)
        yield
        halves = []
        for pair, z in ((first, zl), (second, other)):
            for copy in pair:
                cp.arrived(copy)
            halves.append(ring_halves(z))
            forward(-1, z, mate)
            forward(1, z, mate)
            yield
        for pair, z in zip(halves, (zl, other)):
            for copy in pair:
                cp.arrived(copy)
            forward(2, z, mate)
            yield
    else:
        for copy in first:
            cp.arrived(copy)
        halves = ring_halves(zl)
        crossed = [across]
        for k in (-1, 1):
            crossed.append(forward(k, zl, over))
            forward(k, zl, mate)
        yield
        for copy in halves:
            cp.arrived(copy)
        crossed.append(forward(2, zl, over))
        forward(2, zl, mate)
        yield
        for copy, k in zip(crossed, (0, -1, 1, 2)):
            cp.arrived(copy)
            forward(k, other, mate)
            yield
    cp.arrived(own)


def expert_stream(cp, place, grid, sent, kept, got, bufs, total, at, ring_first, free, again):
    neighbours = rep_peers(place)
    if again:
        pl.semaphore_wait(free, len(neighbours))
    b = cp.send(sent, got, place.to_core())
    yield
    cp.arrived(b)
    add_into(got, [got, kept])
    cp.sent_off(b)
    summed = sum_ring_pair if ring_first else sum_pair_ring
    yield from summed(cp, grid, got, got, bufs, total)
    if not again:
        for device in neighbours:
            pl.semaphore_signal(free, inc=1, device_id=device, device_id_type=MESH)
    yield from gather_expert(cp, place, grid, total, at, True)


def dense_stream(cp, place, grid, grad, got, bufs, total, ring_first):
    b = cp.send(grad.at[:, :, 1 - place.core], got, place.to_core())
    yield
    cp.arrived(b)
    own = grad.at[:, :, place.core]
    add_into(got, [got, own])
    summed = sum_ring_pair if ring_first else sum_pair_ring
    yield from summed(cp, grid, got, got, bufs, total)


def spread_stream(cp, place, stream, total, padded, result):
    yield from stream
    used = total.shape[0] // 8
    spread = spread_matrix(8 * used, 8, used).astype(BF)
    columns = total.shape[1]
    for c in range(0, columns, 128):
        padded[:, :, c : c + 128] = (
            dot_tn(spread, total[:, c : c + 128]).astype(BF).reshape(8, ROW_PAD, 128)
        )
    cp.local(padded.at[place.ep], result.at[place.ep])
    for k in range(1, 8):
        cp.send(padded.at[(place.ep + k) % 8], result.at[place.ep], place.to_ep(k))


def advance(*streams):
    for stream in streams:
        next(stream, None)


BLOCK = 256


def turn(values, cosine, sine):
    return values * cosine + pltpu.roll(values, HD // 2, 1) * sine


def attention_head(h, qkv, live, probs, heads):
    group = qkv.shape[0]
    span = HEADS_DEV * HD
    per = BLOCK // heads.shape[1]
    rows = lax.broadcasted_iota(jnp.int32, (BLOCK, BLOCK), 0)
    columns = lax.broadcasted_iota(jnp.int32, (BLOCK, BLOCK), 1)
    q, k, v = (slice(n * span + h * HD, n * span + (h + 1) * HD) for n in range(3))
    for i in range(group // BLOCK):
        at = slice(i * BLOCK, (i + 1) * BLOCK)
        n = (i + 1) * BLOCK
        scores = dot_nt(qkv[at, q], qkv[:n, k]) * HD**-0.5
        parts = []
        for j in range(i + 1):
            alive = live[LIVE : LIVE + 1, j * BLOCK : (j + 1) * BLOCK] > 0.5
            if j == i:
                alive = (alive & (columns < rows)) | (columns == rows)
            parts.append(jnp.where(alive, scores[:, j * BLOCK : (j + 1) * BLOCK], -1e30))
        scores = jnp.concatenate(parts, axis=1) if len(parts) > 1 else parts[0]
        top = jnp.max(scores, axis=1, keepdims=True)
        weights = jnp.exp(scores - top)
        low = (weights * (1.0 / jnp.sum(weights, axis=1, keepdims=True))).astype(BF)
        probs[h, at, :n] = low
        heads[i * per : (i + 1) * per, :, h * HD : (h + 1) * HD] = (
            dot(low, qkv[:n, v]).astype(BF).reshape(per, BLOCK // per, HD)
        )


def attention_back_head(h, g_heads, qkv, probs, cosine, sine, g_keys, g_values, g_qkv):
    group = qkv.shape[0]
    blocks, rows = g_heads.shape[:2]
    per = BLOCK // rows
    span = HEADS_DEV * HD
    scale = HD**-0.5
    q, k, v = (slice(n * span + h * HD, n * span + (h + 1) * HD) for n in range(3))
    head = slice(h * HD, (h + 1) * HD)
    for i in reversed(range(group // BLOCK)):
        at = slice(i * BLOCK, (i + 1) * BLOCK)
        n = (i + 1) * BLOCK
        g_att = g_heads[i * per : (i + 1) * per, :, head].reshape(BLOCK, HD)
        low = probs[h, at, :n]
        weights = low.astype(F32)
        g_probs = dot_nt(g_att, qkv[:n, v])
        delta = jnp.sum(weights * g_probs, axis=1, keepdims=True)
        g_scores = (weights * (g_probs - delta)).astype(BF)
        g_query = dot(g_scores, qkv[:n, k]) * scale
        g_qkv[at, q] = turn(g_query, cosine[at, :], -sine[at, :]).astype(BF)
        g_key = dot_tn(g_scores, qkv[at, q])
        g_value = dot_tn(low, g_att)
        if i == group // BLOCK - 1:
            g_keys[...] = g_key
            g_values[...] = g_value
        else:
            g_keys[:n, :] += g_key
            g_values[:n, :] += g_value
    g_qkv[:, k] = turn(g_keys[...] * scale, cosine[...], -sine[...]).astype(BF)
    g_qkv[:, v] = g_values[...].astype(BF)


def store_rows(ref, lead, columns, row, value):
    depth = ref.shape[len(lead)]
    done = 0
    while done < value.shape[0]:
        block, offset = divmod(row + done, depth)
        take = min(depth - offset, value.shape[0] - done)
        at = tuple(int(i) for i in np.unravel_index(block, lead))
        ref[at + (slice(offset, offset + take), columns)] = value[done : done + take]
        done += take


def one_expert(blocks, x, g, w_gate, w_up, w_down, weight, wact, g_a, g_b, outs, grads, q_sum, first):
    width = g.shape[1]

    @pl.loop(*blocks)
    def _(i):
        at = pl.ds(pl.multiple_of(i * BLOCK, BLOCK), BLOCK)
        share = weight(at)
        gate = dot(x[at, :], w_gate[...])
        up = dot(x[at, :], w_up[...])
        raw = dot_nt(g[at, :], w_down[...])
        sig = 1.0 / (1.0 + jnp.exp(-gate))
        silu = gate * sig
        act = silu * up
        if q_sum is not None:
            q_sum(i, at, jnp.sum(act * raw, axis=1, keepdims=True))
        low = (act * share).astype(BF)
        wact[at, :] = low
        raw = raw * share
        a = (raw * up * (sig + silu * (1.0 - sig))).astype(BF)
        b = (raw * silu).astype(BF)
        g_a[at, :] = a
        g_b[at, :] = b
        shape = (2, BLOCK // 2, width)
        part = dot(low, w_down[...]).reshape(shape)
        back = (dot_nt(a, w_gate[...]) + dot_nt(b, w_up[...])).reshape(shape)
        if not first:
            part += outs[i].astype(F32)
            back += grads[i, :, :, :width].astype(F32)
        outs[i] = part.astype(BF)
        grads[i, :, :, :width] = back.astype(BF)


ORDER_A = (
    "p0", "g0", "u0", "d0", "G0", "sp", "G0", "U0", "D0", "q1", "G0", "U0", "r1", "G0",
    "U0", "D0", "x", "g1", "G0", "G0", "X0", "D0", "U0", "u1", "G0", "G0", "G1", "U0",
    "X1", "D0", "d1", "U0", "U1", "G0", "G0", "D0", "ss", "X0", "G1", "D1",
)
ORDER_B = (
    "X1", "U0", "X0", "D0", "U0", "U1", "D1", "D0", "G1", "X1", "n2", "U0", "U0", "D0",
    "G1", "U1", "dw", "D1", "sn", "D0", "D0", "G1", "o", "G1", "U1", "D1", "h0", "G1",
    "G1", "U1", "U1", "D1", "W", "S", "D1", "N", "O", "h1", "G1", "G1", "U1", "U1",
    "D1", "O", "hp", "D1", "S", "dq", "N", "U1", "U1", "H0", "D1", "D1", "S", "N",
    "Q", "W", "H1", "Q", "O", "S", "W", "N", "H0", "Q", "H1", "H0", "W", "Q",
    "H1", "n1",
)


def kernel_rest(
    experts, top,
    x_all, g_all, e_gate, e_up, e_down, h_probs, h_hidden, h_qkv, w_slices, h_whole,
    h_residual, h_cot, h_tok, h_attended, h_cosine, h_sine,
    extra, w_router, s_both, s_padded, live, gains,
    out, d_tok, x_gate, x_up, x_down, o_qkv, o_shared, o_whole, o_down,
    m_grads, m_outs, b_grads, b_outs, total_grads, total_hidden, e_got, e_bufs, e_total,
    v_shared, v_down, got, bufs, g_heads, probs, free, send_sem, recv_sem,
):
    place = Place()
    cp = Copies(send_sem, recv_sem)
    group, width = x_all.shape
    rows = group // 8
    mine, core = place.ep, place.core
    ge, gr = grid_ep(place), grid_rep(place)
    wide = width + EXTRA
    exp_dev, _, hidden = e_gate.shape
    span = HEADS_DEV * HD
    cut = wide // 2 // 128 * 128
    cuts = (pl.ds(0, cut), pl.ds(cut, wide - cut))
    m_grads, m_outs, total_grads, total_hidden, x_gate, x_up, x_down = (
        Later(ref) for ref in (m_grads, m_outs, total_grads, total_hidden, x_gate, x_up, x_down)
    )
    later = lambda refs: [Later(ref) if hasattr(ref, "at") else later(ref) for ref in refs]
    b_grads, b_outs, e_got, e_bufs, e_total = (
        later(refs) for refs in (b_grads, b_outs, e_got, e_bufs, e_total)
    )
    half_part = width // 16
    half = width // 2
    ours = pl.ds(pl.multiple_of(core * half, 128), half)
    theirs = pl.ds(pl.multiple_of(place.mate * half, 128), half)
    streams = {}

    def view(ref, c):
        return ref.at[:, :, :, c]

    def phase_a(
        x, g, w_gate, w_up, w_down, wact, g_a, g_b, gates, named,
        swact, sg_a, sg_b, s_down, d_sdown, d_gate, d_up, d_down,
    ):
        first = [cp.local(a, b) for a, b in ((x_all, x), (g_all, g))]
        weights = ((e_gate, w_gate), (e_up, w_up), (e_down, w_down))
        loads = [cp.local(a.at[0], b) for a, b in weights]
        greet(ep_peers(place) + rep_peers(place))
        for copy in first:
            cp.arrived(copy)
        lane = lax.broadcasted_iota(jnp.int32, (BLOCK, EXTRA), 1)

        def router(at, lanes):
            logits = jnp.where(lanes < experts, dot(x[at, :], w_router[...]), -1e30)
            weights = jnp.exp(logits - jnp.max(logits, axis=1, keepdims=True))
            return weights / jnp.sum(weights, axis=1, keepdims=True)

        @pl.loop(0, group // BLOCK)
        def _(i):
            at = pl.ds(pl.multiple_of(i * BLOCK, BLOCK), BLOCK)
            prob = router(at, lane)
            routes = extra[at, :].astype(F32).astype(jnp.int32)
            chosen = lane == routes[:, 0:1]
            for j in range(1, top):
                chosen = chosen | (lane == routes[:, j : j + 1])
            named[at, :] = jnp.where(chosen, 1.0, 0.0)
            alive = extra[at, top : top + 1].astype(F32)
            gates[at, :] = jnp.where(chosen, prob, 0.0) * alive
            m_grads[i, :, :, width:] = jnp.zeros((2, BLOCK // 2, EXTRA), BF)

        probs[...] = router(pl.ds(pl.multiple_of(mine * rows, rows), rows), lane[:rows])

        shared = s_down.shape[0]
        used = s_padded.shape[0] // ROW_PAD * 7 // 16
        steps = group // BLOCK

        def shared_pass():
            pack = spread_matrix(shared, 16, used).astype(BF)
            s_down[...] = dot(pack, s_padded[...]).astype(BF)
            one_expert(
                (0, steps), x, g, s_both.at[:, :shared], s_both.at[:, shared:], s_down,
                lambda at: extra[at, top : top + 1].astype(F32),
                swact, sg_a, sg_b, m_outs, m_grads, None, False,
            )

        def shared_sums():
            for c in range(0, width, BLOCK):
                left = x[:, c : c + BLOCK]
                for n, back in enumerate((sg_a, sg_b)):
                    store_rows(
                        v_shared, (4, 2, 2), slice(n * shared, (n + 1) * shared), c,
                        dot_tn(left, back[...]).astype(BF),
                    )
            d_sdown[...] = dot_tn(swact[...], g[...]).astype(BF)
            pack = spread_matrix(shared, 16, used).astype(BF)
            for c in range(0, s_padded.shape[0], BLOCK):
                store_rows(
                    v_down, (4, 2, 2), slice(0, width), c,
                    dot_tn(pack[:, c : c + BLOCK], d_sdown[...]).astype(BF),
                )

        def expert_pass(e, part):
            expert = mine * exp_dev + e

            def picked(at):
                return jnp.sum(jnp.where(lane == expert, gates[at, :], 0.0), axis=1, keepdims=True)

            def q_sum(i, at, value):
                old = m_grads[i, :, :, width:].reshape(BLOCK, EXTRA).astype(F32)
                new = jnp.where(lane == expert, value * named[at, :], old)
                m_grads[i, :, :, width:] = new.astype(BF).reshape(2, BLOCK // 2, EXTRA)

            if part[0] == 0:
                for copy in loads:
                    cp.arrived(copy)
                loads.clear()
            one_expert(
                part, x, g, w_gate, w_up, w_down, picked,
                wact, g_a, g_b, m_outs, m_grads, q_sum, e == 0,
            )
            if part[1] == steps and e + 1 < exp_dev:
                loads.extend(cp.local(a.at[e + 1], b) for a, b in weights)

        def stream(e, n, sent, kept, at, ring_first):
            streams["GUD"[n] + str(e)] = one = expert_stream(
                cp, place, gr, sent, kept, e_got[n], e_bufs[n], e_total[e][n], at, ring_first,
                free.at[n], e > 0,
            )
            next(one)

        def expert_sums(e, n):
            if n < 2:
                d, back, x_out = ((d_gate, g_a, x_gate), (d_up, g_b, x_up))[n]
                for c in range(0, width, BLOCK):
                    store_rows(
                        d, (2, 4, 2), slice(0, hidden), c, dot_tn(x[:, c : c + BLOCK], back[...]).astype(BF)
                    )
                stream(
                    e, n, d.at[place.mate], d.at[core],
                    lambda k, z: x_out.at[e, core, place.y_at[k], z], True,
                )
            else:
                for c in range(0, hidden, 128):
                    store_rows(
                        d_down, (4, 2), slice(0, width), c, dot_tn(wact[:, c : c + 128], g[...]).astype(BF)
                    )
                stream(
                    e, n, d_down.at[:, :, :, theirs], d_down.at[:, :, :, ours],
                    lambda k, z: x_down.at[e, place.y_at[k], z, :, ours], False,
                )

        def start_x():
            for n, (c, b) in enumerate(zip(cuts, b_grads)):
                streams["X" + str(n)] = one = sum_ring_pair(
                    cp, ge, view(m_grads, c), view(m_grads, c), b, total_grads.at[:, c]
                )
                next(one)

        pieces = {"sp": shared_pass, "ss": shared_sums, "x": start_x}
        for e in range(exp_dev):
            half_steps = steps // 2
            pieces["p" + str(e)] = functools.partial(expert_pass, e, (0, steps))
            pieces["q" + str(e)] = functools.partial(expert_pass, e, (0, half_steps))
            pieces["r" + str(e)] = functools.partial(expert_pass, e, (half_steps, steps))
            for n in range(3):
                pieces["gud"[n] + str(e)] = functools.partial(expert_sums, e, n)
        follow(ORDER_A, pieces)

    def follow(order, pieces):
        for name in order:
            if name in pieces:
                pieces[name]()
            else:
                next(streams[name], None)

    pl.run_scoped(
        phase_a,
        pltpu.VMEM((group, width), BF),
        pltpu.VMEM((group, width), BF),
        pltpu.VMEM((width, hidden), BF),
        pltpu.VMEM((width, hidden), BF),
        pltpu.VMEM((hidden, width), BF),
        *[pltpu.VMEM((group, hidden), BF)] * 3,
        *[pltpu.VMEM((group, EXTRA), F32)] * 2,
        *[pltpu.VMEM((group, s_both.shape[1] // 2), BF)] * 3,
        *[pltpu.VMEM((s_both.shape[1] // 2, width), BF)] * 2,
        pltpu.VMEM((2, 4, 2, half_part, hidden), BF),
        pltpu.VMEM((2, 4, 2, half_part, hidden), BF),
        pltpu.VMEM((4, 2, hidden // 8, width), BF),
    )

    def phase_b(
        v_probs, v_hidden, v_qkvs, v_w, w_whole, residual, cot, tok, attended, cosine, sine,
        v_whole, v_qkv, totals, padded, g_att, g_residual, g_keys, g_values, g_qkv, g_branch,
    ):
        loads = [
            cp.local(a, b)
            for a, b in (
                (h_residual, residual), (h_cot, cot), (h_whole, w_whole), (h_attended, attended),
                (h_qkv, v_qkvs), (h_probs, v_probs), (h_cosine, cosine), (h_sine, sine),
                (w_slices.at[:, : v_w.shape[1]], v_w), (h_hidden, v_hidden), (h_tok, tok),
            )
        ]
        alive = live[...]
        kept = {}

        step = 256

        def second_norm():
            for copy in loads:
                cp.arrived(copy)
            router_grad = total_grads[:, width:] * alive
            prob = probs[...]
            logit_grad = prob * (router_grad - jnp.sum(prob * router_grad, axis=1, keepdims=True))
            squares = jnp.zeros((rows, 1), F32)
            mean_k = jnp.zeros((rows, 1), F32)
            for c in range(0, width, step):
                part = residual[:, c : c + step]
                squares += jnp.sum(part * part, axis=1, keepdims=True)
            scale = lax.rsqrt(squares / width + EPS)
            gain_rows = []
            for c in range(0, width, step):
                k = total_grads[:, c : c + step] + lax.dot_general(
                    logit_grad, w_whole[c : c + step, width:].astype(F32), (((1,), (1,)), ((), ())),
                    preferred_element_type=F32, precision=HIGH,
                )
                normed = residual[:, c : c + step] * scale
                gain_rows.append(jnp.sum(k * normed, axis=0, keepdims=True))
                k = k * gains[1:2, c : c + step]
                mean_k += jnp.sum(k * normed, axis=1, keepdims=True)
                g_residual[:, c : c + step] = k
            mean_k = mean_k / width
            for c in range(0, width, step):
                normed = residual[:, c : c + step] * scale
                grad = cot[:, c : c + step].astype(F32) + scale * (
                    g_residual[:, c : c + step] - normed * mean_k
                )
                g_residual[:, c : c + step] = grad
                g_branch[:, c : c + step] = (alive * grad).astype(BF)
            for c in range(0, width, step):
                g_att[c // step] = dot_nt(g_branch[...], w_whole[c : c + step, :width]).astype(BF)
            for c in range(width // step, 8):
                g_att[c] = jnp.zeros((rows, span), BF)
            kept["third"] = [cp.local(g_att.at[mine], g_heads.at[mine])] + [
                cp.send(g_att.at[(mine + k) % 8], g_heads.at[mine], place.to_ep(k)) for k in range(1, 8)
            ]
            kept["norm"] = logit_grad, scale, gain_rows

        def whole_sums():
            logit_grad, scale, gain_rows = kept["norm"]
            for i in range(2):
                c = slice(i * width // 2, (i + 1) * width // 2)
                v_whole[2 * i : 2 * i + 2, :, :, :, :width] = (
                    dot_tn(attended[:, c], g_branch[...]).astype(BF).reshape(2, 2, 2, width // 16, width)
                )
                hid = (residual[:, c] * scale * gains[1:2, c]).astype(BF).astype(F32)
                small = lax.dot_general(
                    hid, logit_grad, (((0,), (0,)), ((), ())), preferred_element_type=F32, precision=HIGH
                )
                gain_row = jnp.concatenate(gain_rows, axis=1)[:, c]
                lane = lax.broadcasted_iota(jnp.int32, (width // 2, EXTRA), 1)
                column = jnp.broadcast_to(gain_row, (8, width // 2)).T[:, :1]
                small = jnp.where(lane == EXTRA - 1, column, small)
                v_whole[2 * i : 2 * i + 2, :, :, :, width:] = small.astype(BF).reshape(
                    2, 2, 2, width // 16, EXTRA
                )
            dense("W", 0, v_whole, False, 0, o_whole)

        def dense(name, i, v, ring_first, spread, result):
            one = dense_stream(cp, place, gr, v, got[i], bufs[i], totals[i], ring_first)
            if spread is not None:
                one = spread_stream(cp, place, one, totals[i], padded[spread], result)
            streams[name] = one
            next(one)

        def small_dense():
            dense("S", 1, v_shared, True, 1, o_shared)
            dense("N", 2, v_down, True, None, None)

        def start_out():
            streams["O"] = sum_ring_pair(cp, ge, m_outs, m_outs, b_outs, out, (residual,))
            next(streams["O"])

        def head(h):
            if h == 0:
                for copy in kept["third"]:
                    cp.arrived(copy)
            attention_back_head(h, g_heads, v_qkvs, v_probs, cosine, sine, g_keys, g_values, g_qkv)

        def hidden_part():
            @pl.loop(0, group // BLOCK)
            def _(i):
                at = pl.ds(pl.multiple_of(i * BLOCK, BLOCK), BLOCK)
                part = dot_nt(g_qkv[at, :], v_w[...]).astype(BF)
                m_grads[i, :, :, :width] = part.reshape(2, rows, width)

            hcuts = (pl.ds(0, half), pl.ds(half, width - half))
            for n, ((b,), c) in enumerate(zip(b_grads, hcuts)):
                streams["H" + str(n)] = one = sum_ring_pair(
                    cp, ge, view(m_grads, c), view(m_grads, c), [b.at[:, :, pl.ds(0, c.size)]],
                    total_hidden.at[:, c],
                )
                next(one)

        def qkv_sums():
            for i in range(2):
                c = slice(i * width // 2, (i + 1) * width // 2)
                v_qkv[2 * i : 2 * i + 2] = (
                    dot_tn(v_hidden[:, c], g_qkv[...]).astype(BF).reshape(2, 2, 2, width // 16, 3 * span)
                )
            dense("Q", 3, v_qkv, True, 2, o_qkv)

        def first_norm():
            squares = jnp.zeros((rows, 1), F32)
            mean_k = jnp.zeros((rows, 1), F32)
            for c in range(0, width, step):
                part = tok[:, c : c + step].astype(F32)
                squares += jnp.sum(part * part, axis=1, keepdims=True)
            scale = lax.rsqrt(squares / width + EPS)
            for c in range(0, width, step):
                normed = tok[:, c : c + step].astype(F32) * scale
                k = total_hidden[:, c : c + step] * gains[0:1, c : c + step]
                mean_k += jnp.sum(k * normed, axis=1, keepdims=True)
            mean_k = mean_k / width
            for c in range(0, width, step):
                normed = tok[:, c : c + step].astype(F32) * scale
                k = total_hidden[:, c : c + step] * gains[0:1, c : c + step]
                d_tok[:, c : c + step] = g_residual[:, c : c + step] + scale * (k - normed * mean_k)

        follow(
            ORDER_B,
            {
                "n2": second_norm, "dw": whole_sums, "sn": small_dense, "o": start_out,
                "h0": functools.partial(head, 0), "h1": functools.partial(head, 1),
                "hp": hidden_part, "dq": qkv_sums, "n1": first_norm,
            },
        )
        run_streams(*streams.values())
        o_down[...] = totals[2][...]
        cp.finish()

    columns = (wide, s_both.shape[1], width, 3 * span)
    depth = (half_part, half_part, ROW_PAD, half_part)
    pl.run_scoped(
        phase_b,
        pltpu.VMEM(h_probs.shape, BF),
        pltpu.VMEM(h_hidden.shape, BF),
        pltpu.VMEM(h_qkv.shape, BF),
        pltpu.VMEM((width, 3 * span), BF),
        pltpu.VMEM(h_whole.shape, BF),
        pltpu.VMEM((rows, width), F32),
        *[pltpu.VMEM((rows, width), BF)] * 3,
        *[pltpu.VMEM((group, HD), F32)] * 2,
        pltpu.VMEM((4, 2, 2, half_part, wide), BF),
        pltpu.VMEM((4, 2, 2, half_part, 3 * span), BF),
        [pltpu.VMEM((r, c), BF) for r, c in zip(depth, columns)],
        [pltpu.VMEM((8, ROW_PAD, columns[i]), BF) for i in (0, 1, 3)],
        pltpu.VMEM((8, rows, span), BF),
        pltpu.VMEM((rows, width), F32),
        *[pltpu.VMEM((group, HD), F32)] * 2,
        pltpu.VMEM((group, 3 * span), BF),
        pltpu.VMEM((rows, width), BF),
    )


def call_rest(
    experts, top, x_all, g_all, e_gate, e_up, e_down, h_probs, h_hidden, h_qkv, w_slices, h_whole,
    h_residual, h_cot, h_tok, h_attended, h_cosine, h_sine,
    extra, w_router, s_both, s_padded, live, gains,
):
    anyspace = pl.BlockSpec(memory_space=pl.ANY)
    vmem = pl.BlockSpec(memory_space=pltpu.VMEM)
    rows, width = h_cot.shape
    span = HEADS_DEV * HD
    wide = width + EXTRA
    cut = wide // 2 // 128 * 128
    exp_dev, _, hidden = e_gate.shape
    part = width // 16
    columns = (wide, s_both.shape[1], width, 3 * span)
    depth = (part, part, ROW_PAD, part)
    orders = (False, True, True, True)
    halves = ((part, hidden), (part, hidden), (hidden // 8, width // 2))
    bufs_of = lambda first, r, c: (ring_pair_bufs if first else pair_ring_bufs)(r, c)
    shape = jax.ShapeDtypeStruct
    return pl.pallas_call(
        functools.partial(kernel_rest, experts, top),
        out_shape=(
            shape((rows, width), BF),
            shape((rows, width), F32),
            shape((exp_dev, 2, 4, 2, part, hidden), BF),
            shape((exp_dev, 2, 4, 2, part, hidden), BF),
            shape((exp_dev, 4, 2, hidden // 8, width), BF),
            shape((8, ROW_PAD, 3 * span), BF),
            shape((8, ROW_PAD, columns[1]), BF),
            shape((8, ROW_PAD, wide), BF),
            shape((ROW_PAD, width), BF),
        ),
        in_specs=[anyspace] * 16 + [vmem] * 6,
        out_specs=(vmem, vmem) + (anyspace,) * 6 + (vmem,),
        scratch_shapes=[
            pltpu.VMEM((4, 2, rows, wide), BF),
            pltpu.VMEM((4, 2, rows, width), BF),
            [ring_pair_bufs(rows, c) for c in (cut, wide - cut)],
            ring_pair_bufs(rows, width),
            pltpu.VMEM((rows, wide), F32),
            pltpu.VMEM((rows, width), F32),
            [pltpu.VMEM((4, 2) + h, BF) for h in halves],
            [bufs_of(first, *h) for first, h in zip((True, True, False), halves)],
            [[pltpu.VMEM(h, BF) for h in halves] for _ in range(exp_dev)],
            pltpu.VMEM((4, 2, 2, part, columns[1]), BF),
            pltpu.VMEM((4, 2, 2, ROW_PAD, width), BF),
            [pltpu.VMEM((4, 2, r, c), BF) for r, c in zip(depth, columns)],
            [bufs_of(first, r, c) for first, r, c in zip(orders, depth, columns)],
            pltpu.VMEM((8, rows, span), BF),
            pltpu.VMEM((rows, EXTRA), F32),
            pltpu.SemaphoreType.REGULAR((3,)),
            pltpu.SemaphoreType.DMA((440,)),
            pltpu.SemaphoreType.DMA((440,)),
        ],
        compiler_params=pltpu.CompilerParams(
            collective_id=2, has_side_effects=True, vmem_limit_bytes=int(63.9 * 2**20)
        ),
        name="rest",
    )(
        x_all, g_all, e_gate, e_up, e_down, h_probs, h_hidden, h_qkv, w_slices, h_whole,
        h_residual, h_cot, h_tok, h_attended, h_cosine, h_sine,
        extra, w_router, s_both, s_padded, live, gains,
    )


def pad_rows(values, rows):
    return jnp.pad(values, ((0, rows - values.shape[0]),) + ((0, 0),) * (values.ndim - 1))


def body(
    tokens, cotangent, lengths, token_mask, routes,
    w_query, w_key, w_value, w_output, w_router,
    shared_gate, shared_up, shared_down, norm_attn, norm_ffn,
    expert_gate, expert_up, expert_down,
):
    rows, width = tokens.shape
    top = routes.shape[1]
    used = w_query.shape[0]
    hidden = expert_gate.shape[2]
    experts = w_router.shape[1]
    exp_dev = expert_gate.shape[0]
    ep = lax.axis_index("ep")
    group = rows * 8
    span = HEADS_DEV * HD
    owners = width // span
    down_used = shared_down.shape[0]
    shared_cols = 16 * down_used

    def by_owner(w):
        return jnp.pad(w.reshape(used, owners, span), ((0, 0), (0, 8 - owners), (0, 0)))

    def by_shared(w):
        w = w.reshape(used, 16, 8, down_used).transpose(0, 2, 1, 3).reshape(used, 8, shared_cols)
        return w

    gains = jnp.broadcast_to(jnp.stack([norm_attn, norm_ffn], axis=1)[:, None], (used, 8, 2))
    zeros = lambda n: jnp.zeros((used, 8, n), BF)
    slices = jnp.concatenate(
        [
            by_owner(w_query), by_owner(w_key), by_owner(w_value),
            by_shared(shared_gate), gains, zeros(126 - shared_cols),
            by_shared(shared_up), zeros(128 - shared_cols),
        ],
        axis=2,
    ).transpose(1, 0, 2)
    slices = jnp.pad(slices, ((0, 0), (0, ROW_PAD - used), (0, 0)))
    whole = jnp.concatenate([w_output, w_router], axis=1)
    whole = jnp.pad(whole, ((0, ROW_PAD - used), (0, width + EXTRA - whole.shape[1])))
    down = pad_rows(shared_down, ROW_PAD)
    position = ep * rows + jnp.arange(rows, dtype=jnp.int32)
    live_own = ((position < lengths[0]) & (token_mask == 1)).astype(F32)
    tok_wide = jnp.concatenate(
        [
            tokens,
            jnp.pad(
                jnp.concatenate([routes.astype(BF), live_own[:, None].astype(BF)], axis=1),
                ((0, 0), (0, EXTRA - top - 1)),
            ),
        ],
        axis=1,
    )
    frequency = 10000.0 ** (-(np.arange(HD // 2, dtype=np.float32) * np.float32(2.0) / HD))
    angles = np.arange(group, dtype=np.float32)[:, None] * frequency.astype(np.float32)[None, :]
    cosine = jnp.asarray(np.tile(np.cos(angles), (1, 2)), F32)
    sine = jnp.asarray(np.concatenate([-np.sin(angles), np.sin(angles)], axis=1), F32)
    live_col = live_own[:, None]
    (
        w_slices, w_both, w_whole, w_router_all, w_down, cot_all, extra,
        hidden_one, qkv, attn_probs, gain_rows, residual, attended, hidden_all,
    ) = call_front(slices, whole, down, tok_wide, cotangent, live_col, cosine, sine, used)
    w_slices = w_slices.reshape(width, -1)
    w_whole = w_whole.reshape(width, -1)
    out, d_tokens, e_gate, e_up, e_down, o_qkv, o_shared, o_whole, o_down = call_rest(
        experts, top,
        hidden_all.reshape(group, width), cot_all.reshape(group, width),
        expert_gate, expert_up, expert_down, attn_probs, hidden_one, qkv, w_slices, w_whole,
        residual, cotangent, tokens, attended, cosine, sine,
        extra.reshape(group, EXTRA), w_router_all.reshape(width, EXTRA),
        w_both.reshape(width, -1), w_down.reshape(-1, width), live_col, gain_rows,
    )
    o_qkv = o_qkv[:owners, :used].astype(F32)
    o_shared = o_shared[:, :used].astype(F32)
    o_whole = jnp.sum(o_whole[:, :used].astype(F32), axis=0)

    def from_owner(i):
        return o_qkv[:, :, i * span : (i + 1) * span].transpose(1, 0, 2).reshape(used, width)

    def from_shared(i):
        return (
            o_shared[:, :, 128 * i : 128 * i + shared_cols]
            .reshape(8, used, 16, down_used)
            .transpose(1, 2, 0, 3)
            .reshape(used, hidden)
        )

    d_query, d_key, d_value = (from_owner(i) for i in range(3))
    d_gain_one = sum(
        jnp.sum(w.astype(F32) * d, axis=1)
        for w, d in ((w_query, d_query), (w_key, d_key), (w_value, d_value))
    ) / norm_attn.astype(F32)
    return (
        out,
        d_tokens,
        d_query,
        d_key,
        d_value,
        o_whole[:, :width],
        o_whole[:, width : width + experts],
        from_shared(0),
        from_shared(1),
        o_down[:down_used].astype(F32),
        d_gain_one,
        o_whole[:, width + EXTRA - 1],
        e_gate.reshape(exp_dev, width, hidden).astype(F32),
        e_up.reshape(exp_dev, width, hidden).astype(F32),
        e_down.reshape(exp_dev, hidden, width).astype(F32),
    )


def solution(mesh):
    both = ("rep", "ep")
    row = P(both, None)
    expert = P("ep", None, None)
    in_specs = (
        row, row, P("rep"), P(both), row, row, row, row, row, row, row, row, row,
        P(both), P(both), expert, expert, expert,
    )
    out_specs = (
        row, row, row, row, row, row, row, row, row, row, P(both), P(both),
        expert, expert, expert,
    )
    return jax.shard_map(body, mesh=mesh, in_specs=in_specs, out_specs=out_specs, check_vma=False)
```

```python
import functools
import itertools
import math

import jax
import jax.numpy as jnp
import numpy as np
from jax import lax
from jax.experimental import pallas as pl
from jax.experimental.pallas import tpu as pltpu
from jax.sharding import PartitionSpec as P

HD = 128
EPS = 1e-6
BF = jnp.bfloat16
F32 = jnp.float32
MESH = pl.DeviceIdType.MESH
HIGH = lax.Precision.HIGHEST
HEADS_DEV = 2
EXTRA = 128
ROW_PAD = 16
VMEM_LIMIT = 60 << 20
LIVE = 7


def dot(a, b):
    return jnp.dot(a, b, preferred_element_type=F32)


def dot_nt(a, b):
    return lax.dot_general(a, b, (((1,), (1,)), ((), ())), preferred_element_type=F32)


def dot_tn(a, b):
    return lax.dot_general(a, b, (((0,), (0,)), ((), ())), preferred_element_type=F32)


class Place:
    def __init__(self):
        self.rep = lax.axis_index("rep")
        self.ep = lax.axis_index("ep")
        self.y = self.rep // 4
        self.zl = (self.rep // 2) % 2
        self.core = self.rep % 2
        self.x = self.ep // 2
        self.zh = self.ep % 2

        self.mate = 1 - self.core
        self.y_at = {k: (self.y + k) % 4 for k in (-1, 0, 1, 2)}
        self.from_x = {k: self.ep_at(self.x + k, self.zh) for k in (-1, 1, 2)}
        self.from_z = {k: self.ep_at(self.x + k, 1 - self.zh) for k in (-1, 0, 1, 2)}
        self._x = {k: (self.rep, self.ep_at(self.x + k, self.zh)) for k in (-1, 1)}
        self._y = {k: (self.rep_at(self.y + k, self.zl, self.core), self.ep) for k in (-1, 1)}
        self._ep = {k: (self.rep, (self.ep + k) % 8) for k in range(1, 8)}
        self._zh = (self.rep, self.ep_at(self.x, 1 - self.zh))
        self._zl = (self.rep_at(self.y, 1 - self.zl, self.core), self.ep)
        self._core = (self.rep_at(self.y, self.zl, self.mate), self.ep)

    def rep_at(self, y, zl, core):
        return (y % 4) * 4 + zl * 2 + core

    def ep_at(self, x, zh):
        return (x % 4) * 2 + zh

    def to_x(self, step):
        return self._x[step]

    def to_zh(self):
        return self._zh

    def to_ep(self, shift):
        return self._ep[shift]

    def to_y(self, step):
        return self._y[step]

    def to_zl(self):
        return self._zl

    def to_core(self):
        return self._core


class Later:
    def __init__(self, ref, path=()):
        self.ref, self.path = ref, path

    @property
    def at(self):
        return LaterAt(self)

    @property
    def shape(self):
        return self.made().shape

    @property
    def dtype(self):
        return self.ref.dtype

    def made(self):
        ref = self.ref
        for index in self.path:
            ref = ref.at[index]
        return ref

    def __getitem__(self, index):
        return self.made()[index]

    def __setitem__(self, index, value):
        self.made()[index] = value


class LaterAt:
    def __init__(self, later):
        self.later = later

    def __getitem__(self, index):
        return Later(self.later.ref, self.later.path + (index,))


def made(ref):
    return ref.made() if isinstance(ref, Later) else ref


class Copies:
    def __init__(self, send_sem, recv_sem):
        self.send_sem, self.recv_sem = send_sem, recv_sem
        self.number = itertools.count()
        self.sent, self.open = [], []

    def send(self, src, dst, device):
        i = next(self.number)

        def copy():
            return pltpu.make_async_remote_copy(
                src_ref=made(src),
                dst_ref=made(dst),
                send_sem=self.send_sem.at[i],
                recv_sem=self.recv_sem.at[i],
                device_id=device,
                device_id_type=MESH,
            )

        copy().start()
        self.sent.append(copy)
        self.open.append(copy)
        return copy

    def local(self, src, dst):
        i = next(self.number)

        def copy():
            return pltpu.make_async_copy(made(src), made(dst), self.recv_sem.at[i])

        copy().start()
        self.open.append(copy)
        return copy

    def arrived(self, copy):
        if any(copy is c for c in self.sent):
            copy().wait_recv()
        else:
            copy().wait()
        self.open = [c for c in self.open if c is not copy]

    def sent_off(self, copy):
        copy().wait_send()
        self.sent = [c for c in self.sent if c is not copy]

    def drain(self, stream):
        for _ in stream:
            pass

    def finish(self):
        for copy in list(self.open):
            self.arrived(copy)
        for copy in list(self.sent):
            self.sent_off(copy)


def greet(devices, meanwhile=lambda: None):
    barrier = pltpu.get_barrier_semaphore()
    for device in devices:
        pl.semaphore_signal(barrier, inc=1, device_id=device, device_id_type=MESH)
    meanwhile()
    pl.semaphore_wait(barrier, len(devices))


def as_column(row):
    shape = (row.shape[1],) * 2
    same = lax.broadcasted_iota(jnp.int32, shape, 0) == lax.broadcasted_iota(jnp.int32, shape, 1)
    return jnp.sum(jnp.where(same, row, 0.0), axis=1, keepdims=True)


def as_row(column):
    shape = (column.shape[0],) * 2
    same = lax.broadcasted_iota(jnp.int32, shape, 0) == lax.broadcasted_iota(jnp.int32, shape, 1)
    return jnp.sum(jnp.where(same, column, 0.0), axis=0, keepdims=True)


def shared_columns(owner, hidden, used):
    shape = (hidden, 128)
    unit = lax.broadcasted_iota(jnp.int32, shape, 0)
    k = lax.broadcasted_iota(jnp.int32, shape, 1)
    taken = (k < 16 * used) & (unit == (k // used) * 8 * used + owner * used + k % used)
    return jnp.where(taken, 1.0, 0.0).astype(BF)


def run_streams(*streams):
    live = list(streams)
    while live:
        for stream in list(live):
            try:
                next(stream)
            except StopIteration:
                live.remove(stream)


def half_columns(columns):
    return (columns // 128 + 1) // 2 * 128


def ep_peers(place):
    return [place.to_ep(k) for k in range(1, 8)]


def rep_peers(place):
    return [place.to_y(1), place.to_y(-1), place.to_zl(), place.to_core()]


def gather_ep(cp, place, src, dst, columns):
    cut = half_columns(columns)
    lo, hi = pl.ds(0, cut), pl.ds(cut, columns - cut)
    mine = place.ep
    own = cp.local(src, dst.at[mine])
    right = cp.send(src, dst.at[mine], place.to_x(1))
    left = cp.send(src, dst.at[mine], place.to_x(-1))
    over = cp.send(src, dst.at[mine], place.to_zh())
    yield
    from_left, from_right, far = (place.from_x[k] for k in (-1, 1, 2))
    from_over = place.from_z[0]
    cp.arrived(own)
    cp.arrived(right)
    half_a = cp.send(dst.at[from_left, :, lo], dst.at[from_left, :, lo], place.to_x(1))
    cp.arrived(left)
    half_b = cp.send(dst.at[from_right, :, hi], dst.at[from_right, :, hi], place.to_x(-1))
    yield
    cp.arrived(over)
    last = []
    last.append(cp.send(dst.at[from_over], dst.at[from_over], place.to_x(1)))
    last.append(cp.send(dst.at[from_over], dst.at[from_over], place.to_x(-1)))
    yield
    cp.arrived(half_a)
    cp.arrived(half_b)
    last.append(cp.send(dst.at[far], dst.at[far], place.to_zh()))
    yield
    for copy in last:
        cp.arrived(copy)
    for copy in [right, left, over, half_a, half_b] + last:
        cp.sent_off(copy)


def gather_ring_y(cp, place, src, dst, columns, slot):
    cut = half_columns(columns)
    lo, hi = pl.ds(0, cut), pl.ds(cut, columns - cut)
    up = cp.send(src, dst.at[slot(place.y)], place.to_y(1))
    down = cp.send(src, dst.at[slot(place.y)], place.to_y(-1))
    yield
    cp.arrived(up)
    below = slot(place.y - 1)
    half_a = cp.send(dst.at[below, :, lo], dst.at[below, :, lo], place.to_y(1))
    cp.arrived(down)
    above = slot(place.y + 1)
    half_b = cp.send(dst.at[above, :, hi], dst.at[above, :, hi], place.to_y(-1))
    yield
    cp.arrived(half_a)
    cp.arrived(half_b)


def gather_rep(cp, place, src, dst, columns, z_first):
    mine = place.rep
    last = [cp.local(src, dst.at[mine]), cp.send(src, dst.at[mine], place.to_core())]

    def slot(zl):
        return lambda y: place.rep_at(y, zl, place.core)

    def pass_core(index):
        last.append(cp.send(dst.at[index], dst.at[index], place.to_core()))

    here, there = slot(place.zl), slot(1 - place.zl)
    if z_first:
        over = cp.send(src, dst.at[mine], place.to_zl())
        first = gather_ring_y(cp, place, src, dst, columns, here)
        next(first)
        yield
        cp.arrived(over)
        second = gather_ring_y(
            cp, place, dst.at[there(place.y)], dst, columns, there
        )
        next(second)
        pass_core(there(place.y))
        yield
        next(first)
        for k in (-1, 1):
            pass_core(here(place.y + k))
        yield
        next(second)
        for k in (-1, 1):
            pass_core(there(place.y + k))
        yield
        next(first, None)
        pass_core(here(place.y + 2))
        yield
        next(second, None)
        pass_core(there(place.y + 2))
    else:
        over = [cp.send(src, dst.at[mine], place.to_zl())]
        ring = gather_ring_y(cp, place, src, dst, columns, here)
        next(ring)
        yield
        next(ring)
        for k in (-1, 1):
            block = dst.at[here(place.y + k)]
            over.append(cp.send(block, block, place.to_zl()))
            pass_core(here(place.y + k))
        yield
        next(ring, None)
        block = dst.at[here(place.y + 2)]
        over.append(cp.send(block, block, place.to_zl()))
        pass_core(here(place.y + 2))
        yield
        for copy, k in zip(over, (0, -1, 1, 2)):
            cp.arrived(copy)
            pass_core(there(place.y + k))
            yield
    yield
    for copy in last:
        cp.arrived(copy)


def spread_matrix(rows, blocks, used):
    shape = (rows, blocks * ROW_PAD)
    to = lax.broadcasted_iota(jnp.int32, shape, 0)
    at = lax.broadcasted_iota(jnp.int32, shape, 1)
    return jnp.where((at // ROW_PAD) * used + at % ROW_PAD == to, 1.0, 0.0) * jnp.where(
        at % ROW_PAD < used, 1.0, 0.0
    )


ORDER_F = (
    "a", "k1", "T", "T", "L", "L", "T", "L", "k2", "L", "c", "L", "L", "T",
    "pr", "W", "h0", "h1", "W", "W", "C", "C", "W", "C", "D", "D", "W", "D",
    "D", "W", "D", "D", "op", "C",
)


def kernel_front(
    tok, cot, length, mask, routes, w_query, w_key, w_value, w_output, w_route,
    shared_gate, shared_up, shared_down, norm_attn, norm_ffn, cosine, sine,
    w_slices, w_both, w_whole, w_router, w_down, cot_all, extra,
    hidden_one, qkv, probs, gains, residual, attended, hidden, live,
    slices, whole, down, wide_tok,
    land_slices, land_whole, pack_slices, pack_whole, v_slices, v_whole, v_tok,
    heads, land_heads, live_row, send_sem, recv_sem,
):
    place = Place()
    cp = Copies(send_sem, recv_sem)
    rows, width = tok.shape
    group = 8 * rows
    span = HEADS_DEV * HD
    mine = place.ep
    top = routes.shape[0]

    def own_inputs():
        position = mine * rows + lax.broadcasted_iota(jnp.int32, (1, rows), 1)
        alive = jnp.where((position < length[...]) & (mask[...] == 1), 1.0, 0.0)
        live[...] = as_column(alive)
        block = jnp.concatenate(
            [routes[...].astype(F32), alive, jnp.zeros((EXTRA - top - 1, rows), F32)], axis=0
        )
        wide_tok[:, :width] = tok[...]
        wide_tok[:, width:] = block.T.astype(BF)
        for ref in (slices, whole, down):
            ref[...] = jnp.zeros_like(ref)
        rows_of = slice(0, w_query.shape[0])
        whole[rows_of, :width] = w_output[...]
        whole[rows_of, width : width + w_route.shape[1]] = w_route[...]
        down[: shared_down.shape[0], :] = shared_down[...]
        gains_of = [as_column(g[...].astype(F32)) for g in (norm_attn, norm_ffn)]
        lane = lax.broadcasted_iota(jnp.int32, (w_query.shape[0], 128), 1)
        spare = 16 * shared_down.shape[0]
        for owner in range(8):
            if owner * span < width:
                for n, w in enumerate((w_query, w_key, w_value)):
                    slices[owner, rows_of, n * span : (n + 1) * span] = w[:, owner * span : (owner + 1) * span]
            pick = shared_columns(owner, shared_gate.shape[1], shared_down.shape[0])
            gate = dot(shared_gate[...], pick)
            gate = jnp.where(lane == spare, gains_of[0], jnp.where(lane == spare + 1, gains_of[1], gate))
            slices[owner, rows_of, 3 * span : 3 * span + 128] = gate.astype(BF)
            slices[owner, rows_of, 3 * span + 128 :] = dot(shared_up[...], pick).astype(BF)

    greet(ep_peers(place) + rep_peers(place), own_inputs)
    streams, kept = {}, {}
    used = pack_slices.shape[0] // 8
    per = BLOCK // rows

    def pack(land, packed):
        spread = spread_matrix(8 * used, 8, used).astype(BF)
        for c in range(0, land.shape[2], 128):
            block = land[:, :, c : c + 128].reshape(8 * ROW_PAD, 128)
            packed[:, c : c + 128] = dot(spread, block).astype(BF)

    def start(name, stream):
        streams[name] = stream
        next(stream)

    def to_owners():
        kept["slices"] = [cp.local(slices.at[mine], land_slices.at[mine])] + [
            cp.send(slices.at[(mine + k) % 8], land_slices.at[mine], place.to_ep(k)) for k in range(1, 8)
        ]
        kept["whole"] = [cp.local(whole, land_whole.at[mine])] + [
            cp.send(whole, land_whole.at[mine], place.to_ep(k)) for k in range(1, 8)
        ]
        start("T", gather_ep(cp, place, wide_tok, v_tok, wide_tok.shape[1]))

    def pack_first():
        for copy in kept["slices"]:
            cp.arrived(copy)
        pack(land_slices, pack_slices)
        start("L", gather_rep(cp, place, pack_slices, v_slices, slices.shape[2], True))

    def pack_second():
        for copy in kept["whole"]:
            cp.arrived(copy)
        pack(land_whole, pack_whole)
        start("W", gather_rep(cp, place, pack_whole, v_whole, whole.shape[1], True))
        start("D", gather_rep(cp, place, down, w_down, down.shape[1], True))

    def start_cot():
        start("C", gather_ep(cp, place, cot, cot_all, width))

    def projections():
        cp.local(v_slices, w_slices)
        cp.local(v_slices.at[:, :, pl.ds(3 * span, 256)], w_both)
        cp.local(v_tok.at[:, :, pl.ds(width, EXTRA)], extra)
        block = v_slices[:, :, 3 * span : 3 * span + 128].reshape(width, 128).astype(F32).T
        gains[...] = block[112:120, :]
        live_row[...] = jnp.concatenate(
            [v_tok[i, :, width:].astype(F32).T[:8, :] for i in range(8)], axis=1
        )

        @pl.loop(0, group // BLOCK)
        def _(i):
            at = pl.ds(pl.multiple_of(i * BLOCK, BLOCK), BLOCK)
            values = v_tok[pl.ds(i * per, per), :, :width].reshape(BLOCK, width).astype(F32)
            scale = lax.rsqrt(jnp.sum(values * values, axis=1, keepdims=True) / width + EPS)
            low = (values * scale * gains[0:1, :]).astype(BF)
            hidden_one[at, :] = low
            raw = dot(low, v_slices[:, :, : 3 * span].reshape(width, 3 * span))
            cos, sin = cosine[at, :], sine[at, :]
            for h in range(2 * HEADS_DEV):
                c = slice(h * HD, (h + 1) * HD)
                qkv[at, c] = turn(raw[:, c], cos, sin).astype(BF)
            qkv[at, 2 * span :] = raw[:, 2 * span :].astype(BF)

    def head(h):
        attention_head(h, qkv, live_row, probs, heads)
        if h == HEADS_DEV - 1:
            column = pl.ds(pl.multiple_of(mine * span, 128), span)
            kept["heads"] = [cp.local(heads.at[mine], land_heads.at[:, column])] + [
                cp.send(heads.at[(mine + k) % 8], land_heads.at[:, column], place.to_ep(k))
                for k in range(1, 8)
            ]

    def output():
        cp.local(v_whole, w_whole)
        cp.local(v_whole.at[:, :, pl.ds(width, EXTRA)], w_router)
        for copy in kept["heads"]:
            cp.arrived(copy)
        low = land_heads[:, :width]
        attended[...] = low
        step = 256
        squares = jnp.zeros((rows, 1), F32)
        for c in range(0, width, step):
            matrix = v_whole[:, :, c : c + step].reshape(width, step)
            part = tok[:, c : c + step].astype(F32) + live[...] * dot(low, matrix)
            residual[:, c : c + step] = part
            squares += jnp.sum(part * part, axis=1, keepdims=True)
        scale = lax.rsqrt(squares / width + EPS)
        hidden[...] = (residual[...] * scale * gains[1:2, :]).astype(BF)

    pieces = {
        "a": to_owners, "k1": pack_first, "k2": pack_second, "c": start_cot, "pr": projections,
        "h0": functools.partial(head, 0), "h1": functools.partial(head, 1), "op": output,
    }
    for name in ORDER_F:
        if name in pieces:
            pieces[name]()
        else:
            next(streams[name], None)
    run_streams(*streams.values())
    cp.finish()


def call_front(
    tok, cot, length, mask, routes, w_query, w_key, w_value, w_output, w_route,
    shared_gate, shared_up, shared_down, norm_attn, norm_ffn, cosine, sine,
):
    anyspace = pl.BlockSpec(memory_space=pl.ANY)
    vmem = pl.BlockSpec(memory_space=pltpu.VMEM)
    rows, width = cot.shape
    used = w_query.shape[0]
    group = 8 * rows
    span = HEADS_DEV * HD
    shape = jax.ShapeDtypeStruct
    columns, wide = 3 * span + 256, width + EXTRA
    return pl.pallas_call(
        kernel_front,
        out_shape=(
            shape((16, 8 * used, columns), BF),
            shape((16, 8 * used, columns - 3 * span), BF),
            shape((16, 8 * used, wide), BF),
            shape((16, 8 * used, EXTRA), BF),
            shape((16, ROW_PAD, width), BF),
            shape((8,) + cot.shape, BF),
            shape((8, rows, EXTRA), BF),
            shape((group, width), BF),
            shape((group, 3 * span), BF),
            shape((HEADS_DEV, group, group), BF),
            shape((8, width), F32),
            shape((rows, width), F32),
            shape((rows, width), BF),
            shape((rows, width), BF),
            shape((rows, 1), F32),
        ),
        in_specs=[vmem, anyspace] + [vmem] * 15,
        out_specs=(anyspace,) * 7 + (vmem,) * 8,
        scratch_shapes=[
            pltpu.VMEM((8, ROW_PAD, columns), BF),
            pltpu.VMEM((ROW_PAD, wide), BF),
            pltpu.VMEM((ROW_PAD, width), BF),
            pltpu.VMEM((rows, wide), BF),
            pltpu.VMEM((8, ROW_PAD, columns), BF),
            pltpu.VMEM((8, ROW_PAD, wide), BF),
            pltpu.VMEM((8 * used, columns), BF),
            pltpu.VMEM((8 * used, wide), BF),
            pltpu.VMEM((16, 8 * used, columns), BF),
            pltpu.VMEM((16, 8 * used, wide), BF),
            pltpu.VMEM((8, rows, wide), BF),
            pltpu.VMEM((8, rows, span), BF),
            pltpu.VMEM((rows, 8 * span), BF),
            pltpu.VMEM((8, group), F32),
            pltpu.SemaphoreType.DMA((200,)),
            pltpu.SemaphoreType.DMA((200,)),
        ],
        compiler_params=pltpu.CompilerParams(
            collective_id=0, has_side_effects=True, vmem_limit_bytes=VMEM_LIMIT
        ),
        name="front",
    )(
        tok, cot, length, mask, routes, w_query, w_key, w_value, w_output, w_route,
        shared_gate, shared_up, shared_down, norm_attn, norm_ffn, cosine, sine,
    )


def add_into(out, terms):
    lead = out.shape[:-2]
    count = math.prod(lead)

    def add(index):
        if len(terms) == 2 and out.dtype == BF:
            out[index] = terms[0][index] + terms[1][index]
            return
        total = terms[0][index].astype(F32)
        for term in terms[1:]:
            total += term[index].astype(F32)
        out[index] = total.astype(out.dtype)

    if count == 1:
        add((0,) * len(lead) + (slice(None),))
    else:
        inner = lead[-1] if lead else 1

        @pl.loop(0, count)
        def _(i):
            add(((i // inner, i % inner) if len(lead) == 2 else (i,)) + (slice(None),))


class Grid:
    def __init__(self, ring, pair, up, down, over):
        self.here, self.up_at, self.down_at, self.far = ring, (ring + 1) % 4, (ring + 3) % 4, (ring + 2) % 4
        self.pair, self.other = pair, 1 - pair
        self.up, self.down, self.over = up, down, over


def grid_rep(place):
    return Grid(place.y, place.zl, place.to_y(1), place.to_y(-1), place.to_zl())


def grid_ep(place):
    return Grid(place.x, place.zh, place.to_x(1), place.to_x(-1), place.to_zh())


def ring_pair_bufs(rows, columns):
    return [pltpu.VMEM((7, rows, columns), BF)]


def sum_ring_pair(cp, g, source, mine, bufs, out, more=()):
    (buf,) = bufs
    near, last, half, over = (0, 1), ((2, 3), (4, 5)), 0, 6
    b = lambda i: buf.at[i]
    s1 = cp.send(source.at[g.far, 0], b(near[0]), g.up)
    s2 = cp.send(source.at[g.far, 1], b(near[1]), g.down)
    s3 = cp.send(source.at[g.up_at, 1], b(last[0][1]), g.up)
    s4 = cp.send(source.at[g.down_at, 0], b(last[1][0]), g.down)
    yield
    cp.arrived(s1)
    add_into(mine.at[g.up_at, 0], [mine.at[g.up_at, 0], b(near[0])])
    s5 = cp.send(mine.at[g.up_at, 0], b(last[0][0]), g.up)
    cp.arrived(s2)
    add_into(mine.at[g.down_at, 1], [mine.at[g.down_at, 1], b(near[1])])
    s6 = cp.send(mine.at[g.down_at, 1], b(last[1][1]), g.down)
    yield
    for copy in (s3, s4, s5, s6):
        cp.arrived(copy)
    add_into(
        b(half),
        [mine.at[g.here, g.other], buf.at[2 + g.other], buf.at[4 + g.other]],
    )
    s7 = cp.send(b(half), b(over), g.over)
    yield
    cp.arrived(s7)
    add_into(
        out, [mine.at[g.here, g.pair], buf.at[2 + g.pair], buf.at[4 + g.pair], b(over), *more]
    )
    for copy in (s1, s2, s3, s4, s5, s6, s7):
        cp.sent_off(copy)


def pair_ring_bufs(rows, columns):
    cut = half_columns(columns)
    return [
        pltpu.VMEM((4, rows, columns), BF),
        pltpu.VMEM((2, rows, columns), BF),
        pltpu.VMEM((rows, cut), BF),
        pltpu.VMEM((rows, columns - cut), BF),
    ]


def sum_pair_ring(cp, g, source, mine, bufs, out):
    acc, last, near_lo, near_hi = bufs
    columns = acc.shape[2]
    cut = half_columns(columns)
    lo, hi = pl.ds(0, cut), pl.ds(cut, columns - cut)
    s0 = cp.send(source.at[:, g.other], acc, g.over)
    yield
    cp.arrived(s0)
    add_into(acc, [acc, mine.at[:, g.pair]])
    s1 = cp.send(acc.at[g.far, :, lo], near_lo, g.up)
    s2 = cp.send(acc.at[g.far, :, hi], near_hi, g.down)
    s3 = cp.send(acc.at[g.up_at, :, hi], last.at[0, :, hi], g.up)
    s4 = cp.send(acc.at[g.down_at, :, lo], last.at[1, :, lo], g.down)
    yield
    cp.arrived(s1)
    part = acc.at[g.up_at, :, lo]
    add_into(part, [part, near_lo])
    s5 = cp.send(part, last.at[0, :, lo], g.up)
    cp.arrived(s2)
    part = acc.at[g.down_at, :, hi]
    add_into(part, [part, near_hi])
    s6 = cp.send(part, last.at[1, :, hi], g.down)
    yield
    for copy in (s3, s4, s5, s6):
        cp.arrived(copy)
    add_into(out, [acc.at[g.here], last.at[0], last.at[1]])
    for copy in (s0, s1, s2, s3, s4, s5, s6):
        cp.sent_off(copy)


def gather_expert(cp, place, grid, src, at, z_first):
    zl, other = grid.pair, grid.other
    columns = src.shape[1]
    cut = half_columns(columns)
    lo, hi = pl.ds(0, cut), pl.ds(cut, columns - cut)
    up, down, over, mate = place.to_y(1), place.to_y(-1), place.to_zl(), place.to_core()

    def forward(k, z, to):
        return cp.send(at(k, z), at(k, z), to)

    def ring_halves(z):
        a = cp.send(at(-1, z).at[:, lo], at(-1, z).at[:, lo], up)
        b = cp.send(at(1, z).at[:, hi], at(1, z).at[:, hi], down)
        return a, b

    own = cp.local(src, at(0, zl))
    first = [cp.send(src, at(0, zl), to) for to in (up, down)]
    across = cp.send(src, at(0, zl), over)
    cp.send(src, at(0, zl), mate)
    yield
    if z_first:
        cp.arrived(across)
        second = [forward(0, other, to) for to in (up, down)]
        forward(0, other, mate)
        yield
        halves = []
        for pair, z in ((first, zl), (second, other)):
            for copy in pair:
                cp.arrived(copy)
            halves.append(ring_halves(z))
            forward(-1, z, mate)
            forward(1, z, mate)
            yield
        for pair, z in zip(halves, (zl, other)):
            for copy in pair:
                cp.arrived(copy)
            forward(2, z, mate)
            yield
    else:
        for copy in first:
            cp.arrived(copy)
        halves = ring_halves(zl)
        crossed = [across]
        for k in (-1, 1):
            crossed.append(forward(k, zl, over))
            forward(k, zl, mate)
        yield
        for copy in halves:
            cp.arrived(copy)
        crossed.append(forward(2, zl, over))
        forward(2, zl, mate)
        yield
        for copy, k in zip(crossed, (0, -1, 1, 2)):
            cp.arrived(copy)
            forward(k, other, mate)
            yield
    cp.arrived(own)


def expert_stream(cp, place, grid, sent, kept, got, bufs, total, at, ring_first, z_first, free, again):
    neighbours = rep_peers(place)
    if again:
        pl.semaphore_wait(free, len(neighbours))
    b = cp.send(sent, got, place.to_core())
    yield
    cp.arrived(b)
    add_into(got, [got, kept])
    cp.sent_off(b)
    summed = sum_ring_pair if ring_first else sum_pair_ring
    yield from summed(cp, grid, got, got, bufs, total)
    if not again:
        for device in neighbours:
            pl.semaphore_signal(free, inc=1, device_id=device, device_id_type=MESH)
    yield from gather_expert(cp, place, grid, total, at, z_first)


def dense_stream(cp, place, grid, grad, got, bufs, total, ring_first):
    b = cp.send(grad.at[:, :, 1 - place.core], got, place.to_core())
    yield
    cp.arrived(b)
    own = grad.at[:, :, place.core]
    add_into(got, [got, own])
    summed = sum_ring_pair if ring_first else sum_pair_ring
    yield from summed(cp, grid, got, got, bufs, total)


def spread_stream(cp, place, stream, total, padded, result):
    yield from stream
    used = total.shape[0] // 8
    spread = spread_matrix(8 * used, 8, used).astype(BF)
    columns = total.shape[1]
    for c in range(0, columns, 128):
        padded[:, :, c : c + 128] = (
            dot_tn(spread, total[:, c : c + 128]).astype(BF).reshape(8, ROW_PAD, 128)
        )
    cp.local(padded.at[place.ep], result.at[place.ep])
    for k in range(1, 8):
        cp.send(padded.at[(place.ep + k) % 8], result.at[place.ep], place.to_ep(k))


def advance(*streams):
    for stream in streams:
        next(stream, None)


BLOCK = 256


def turn(values, cosine, sine):
    return values * cosine + pltpu.roll(values, HD // 2, 1) * sine


def attention_head(h, qkv, live, probs, heads):
    group = qkv.shape[0]
    span = HEADS_DEV * HD
    per = BLOCK // heads.shape[1]
    rows = lax.broadcasted_iota(jnp.int32, (BLOCK, BLOCK), 0)
    columns = lax.broadcasted_iota(jnp.int32, (BLOCK, BLOCK), 1)
    q, k, v = (slice(n * span + h * HD, n * span + (h + 1) * HD) for n in range(3))
    for i in range(group // BLOCK):
        at = slice(i * BLOCK, (i + 1) * BLOCK)
        n = (i + 1) * BLOCK
        scores = dot_nt(qkv[at, q], qkv[:n, k]) * HD**-0.5
        parts = []
        for j in range(i + 1):
            alive = live[LIVE : LIVE + 1, j * BLOCK : (j + 1) * BLOCK] > 0.5
            if j == i:
                alive = (alive & (columns < rows)) | (columns == rows)
            parts.append(jnp.where(alive, scores[:, j * BLOCK : (j + 1) * BLOCK], -1e30))
        scores = jnp.concatenate(parts, axis=1) if len(parts) > 1 else parts[0]
        top = jnp.max(scores, axis=1, keepdims=True)
        weights = jnp.exp(scores - top)
        low = (weights * (1.0 / jnp.sum(weights, axis=1, keepdims=True))).astype(BF)
        probs[h, at, :n] = low
        heads[i * per : (i + 1) * per, :, h * HD : (h + 1) * HD] = (
            dot(low, qkv[:n, v]).astype(BF).reshape(per, BLOCK // per, HD)
        )


def attention_back_head(h, g_heads, qkv, probs, cosine, sine, g_keys, g_values, g_qkv):
    group = qkv.shape[0]
    blocks, rows = g_heads.shape[:2]
    per = BLOCK // rows
    span = HEADS_DEV * HD
    scale = HD**-0.5
    q, k, v = (slice(n * span + h * HD, n * span + (h + 1) * HD) for n in range(3))
    head = slice(h * HD, (h + 1) * HD)
    for i in reversed(range(group // BLOCK)):
        at = slice(i * BLOCK, (i + 1) * BLOCK)
        n = (i + 1) * BLOCK
        g_att = g_heads[i * per : (i + 1) * per, :, head].reshape(BLOCK, HD)
        low = probs[h, at, :n]
        weights = low.astype(F32)
        g_probs = dot_nt(g_att, qkv[:n, v])
        delta = jnp.sum(weights * g_probs, axis=1, keepdims=True)
        g_scores = (weights * (g_probs - delta)).astype(BF)
        g_query = dot(g_scores, qkv[:n, k]) * scale
        g_qkv[at, q] = turn(g_query, cosine[at, :], -sine[at, :]).astype(BF)
        g_key = dot_tn(g_scores, qkv[at, q])
        g_value = dot_tn(low, g_att)
        if i == group // BLOCK - 1:
            g_keys[...] = g_key
            g_values[...] = g_value
        else:
            g_keys[:n, :] += g_key
            g_values[:n, :] += g_value
    g_qkv[:, k] = turn(g_keys[...] * scale, cosine[...], -sine[...]).astype(BF)
    g_qkv[:, v] = g_values[...].astype(BF)


def store_rows(ref, lead, columns, row, value):
    depth = ref.shape[len(lead)]
    done = 0
    while done < value.shape[0]:
        block, offset = divmod(row + done, depth)
        take = min(depth - offset, value.shape[0] - done)
        at = tuple(int(i) for i in np.unravel_index(block, lead))
        ref[at + (slice(offset, offset + take), columns)] = value[done : done + take]
        done += take


def one_expert(
    loop, blocks, x, g, w_gate, w_up, w_down, weight, wact, g_a, g_b, outs, grads, before, q_sum, first
):
    width = g.shape[2]

    @pl.loop(*loop)
    def _(i):
        pair = blocks(i)

        def load(ref):
            return jnp.concatenate([ref[b] for b in pair], axis=0)

        def store(ref, value):
            for n, b in enumerate(pair):
                ref[b] = value[n * (BLOCK // 2) : (n + 1) * (BLOCK // 2)]

        if before is not None:
            before(pair, load, store)
        share = weight(load)
        rows = load(x)
        gate = dot(rows, w_gate[...])
        up = dot(rows, w_up[...])
        raw = dot_nt(load(g), w_down[...])
        sig = 1.0 / (1.0 + jnp.exp(-gate))
        silu = gate * sig
        act = silu * up
        if q_sum is not None:
            q_sum(pair, load, jnp.sum(act * raw, axis=1, keepdims=True))
        low = (act * share).astype(BF)
        store(wact, low)
        raw = raw * share
        a = (raw * up * (sig + silu * (1.0 - sig))).astype(BF)
        b = (raw * silu).astype(BF)
        store(g_a, a)
        store(g_b, b)
        part = dot(low, w_down[...])
        back = dot_nt(a, w_gate[...]) + dot_nt(b, w_up[...])
        for n, k in enumerate(pair):
            at = slice(n * (BLOCK // 2), (n + 1) * (BLOCK // 2))
            more, behind = part[at], back[at]
            if not first:
                more += outs[k // 2, k % 2].astype(F32)
                behind += grads[k // 2, k % 2, :, :width].astype(F32)
            outs[k // 2, k % 2] = more.astype(BF)
            grads[k // 2, k % 2, :, :width] = behind.astype(BF)


ORDER_A = (
    "A", "A", "p0", "A", "p1", "A", "p2", "p3", "g0", "d0", "u0", "G0", "sp", "G0",
    "U0", "D0", "w1", "q1", "G0", "U0", "r1", "G0", "U0", "D0", "pr", "x", "g1", "G0",
    "X0", "D0", "U0", "u1", "G1", "G0", "G0", "G0", "ss", "G0", "X1", "U1", "G1", "D0",
    "d1", "X0", "U0", "U0", "U1", "G0", "G0", "X1", "D1",
)
ORDER_B = (
    "sn", "o", "G1", "S", "N", "X0", "D0", "X1", "n2", "O", "U1", "G1", "U0", "U0",
    "dw", "D1", "S", "U1", "N", "O", "G1", "D0", "h0", "D1", "U1", "G1", "W", "O",
    "S", "U0", "U0", "h1", "D1", "G1", "hp", "dq", "U1", "U1", "H0", "U1", "G1", "G1",
    "G1", "Q", "U1", "U1", "Q", "H1", "W", "S", "Q", "H0", "W", "Q", "D1", "D1",
    "H1", "N", "W", "H0", "D0", "D0", "D0", "D0", "D0", "D1", "H1", "n1", "N", "D1",
    "D1", "D1",
)
Y_FIRST = ((0, 0), (0, 2))


def kernel_rest(
    experts, top,
    x_own, g_all, e_gate, e_up, e_down, h_probs, h_hidden, h_qkv, w_slices, h_whole,
    h_residual, h_cot, h_tok, h_attended, h_cosine, h_sine,
    extra, w_router, s_both, s_padded, live, gains,
    out, d_tok, x_gate, x_up, x_down, o_qkv, o_shared, o_whole, o_down,
    x, m_grads, m_outs, b_grads, b_outs, total_grads, total_hidden, e_got, e_bufs, e_total,
    v_shared, v_down, got, bufs, g_heads, probs, free, send_sem, recv_sem,
):
    place = Place()
    cp = Copies(send_sem, recv_sem)
    rows, width = x_own.shape
    group = 8 * rows
    mine, core = place.ep, place.core
    ge, gr = grid_ep(place), grid_rep(place)
    wide = width + EXTRA
    exp_dev, _, hidden = e_gate.shape
    span = HEADS_DEV * HD
    cut = wide // 2 // 128 * 128
    cuts = (pl.ds(0, cut), pl.ds(cut, wide - cut))
    m_grads, m_outs, total_grads, total_hidden, x_gate, x_up, x_down = (
        Later(ref) for ref in (m_grads, m_outs, total_grads, total_hidden, x_gate, x_up, x_down)
    )
    later = lambda refs: [Later(ref) if hasattr(ref, "at") else later(ref) for ref in refs]
    b_grads, b_outs, e_got, e_bufs, e_total = (
        later(refs) for refs in (b_grads, b_outs, e_got, e_bufs, e_total)
    )
    half_part = width // 16
    half = width // 2
    ours = pl.ds(pl.multiple_of(core * half, 128), half)
    theirs = pl.ds(pl.multiple_of(place.mate * half, 128), half)
    streams = {}
    from_x, from_z = place.from_x, place.from_z

    def view(ref, c):
        return ref.at[:, :, :, c]

    def phase_a(
        g, w_gate, w_up, w_down, wact, g_a, g_b, gates, named,
        swact, sg_a, sg_b, s_down, d_sdown, d_gate, d_up, d_down,
    ):
        first = [cp.local(g_all, g)]
        weights = ((e_gate, w_gate), (e_up, w_up), (e_down, w_down))
        loads = [cp.local(a.at[0], b) for a, b in weights]
        greet(ep_peers(place) + rep_peers(place))
        streams["A"] = gather_ep(cp, place, x_own, Later(x), width)
        next(streams["A"])
        for copy in first:
            cp.arrived(copy)
        lane = lax.broadcasted_iota(jnp.int32, (BLOCK, EXTRA), 1)

        def router(values, lanes):
            logits = jnp.where(lanes < experts, dot(values, w_router[...]), -1e30)
            weights = jnp.exp(logits - jnp.max(logits, axis=1, keepdims=True))
            return weights / jnp.sum(weights, axis=1, keepdims=True)

        def route(pair, load, store):
            prob = router(load(x), lane)
            routes = load(extra)
            whole = routes.astype(F32).astype(jnp.int32)
            chosen = lane == whole[:, 0:1]
            for j in range(1, top):
                chosen = chosen | (lane == whole[:, j : j + 1])
            store(named, jnp.where(chosen, 1.0, 0.0))
            store(gates, jnp.where(chosen, prob, 0.0) * routes[:, top : top + 1].astype(F32))
            for b in pair:
                m_grads[b // 2, b % 2, :, width:] = jnp.zeros((BLOCK // 2, EXTRA), BF)

        shared = s_down.shape[0]
        used = s_padded.shape[0] // ROW_PAD * 7 // 16
        steps = group // BLOCK
        in_turn = lambda i: (2 * i, 2 * i + 1)
        flat = lambda ref: ref[...].reshape(group, ref.shape[2])
        columns_of = lambda ref, c: ref[:, :, c : c + BLOCK].reshape(group, BLOCK)
        arrivals = (
            (place.ep, from_x[-1]), (from_x[1], from_z[0]), (from_x[2], from_z[-1]), (from_z[1], from_z[2]),
        )

        def shared_pass():
            pack = spread_matrix(shared, 16, used).astype(BF)
            s_down[...] = dot(pack, s_padded[...]).astype(BF)
            one_expert(
                (0, steps), in_turn, x, g, s_both.at[:, :shared], s_both.at[:, shared:], s_down,
                lambda load: load(extra)[:, top : top + 1].astype(F32),
                swact, sg_a, sg_b, m_outs, m_grads, None, None, False,
            )

        def shared_sums():
            for c in range(0, width, BLOCK):
                left = columns_of(x, c)
                for n, back in enumerate((sg_a, sg_b)):
                    store_rows(
                        v_shared, (4, 2, 2), slice(n * shared, (n + 1) * shared), c,
                        dot_tn(left, flat(back)).astype(BF),
                    )
            d_sdown[...] = dot_tn(flat(swact), flat(g)).astype(BF)
            pack = spread_matrix(shared, 16, used).astype(BF)
            for c in range(0, s_padded.shape[0], BLOCK):
                store_rows(
                    v_down, (4, 2, 2), slice(0, width), c,
                    dot_tn(pack[:, c : c + BLOCK], d_sdown[...]).astype(BF),
                )

        def expert_pass(e, loop, blocks):
            expert = mine * exp_dev + e

            def picked(load):
                return jnp.sum(jnp.where(lane == expert, load(gates), 0.0), axis=1, keepdims=True)

            def q_sum(pair, load, value):
                value = value * load(named)
                for n, b in enumerate(pair):
                    at = slice(n * (BLOCK // 2), (n + 1) * (BLOCK // 2))
                    old = m_grads[b // 2, b % 2, :, width:].astype(F32)
                    new = jnp.where(lane[: BLOCK // 2] == expert, value[at], old)
                    m_grads[b // 2, b % 2, :, width:] = new.astype(BF)

            for copy in loads:
                cp.arrived(copy)
            loads.clear()
            one_expert(
                loop, blocks, x, g, w_gate, w_up, w_down, picked,
                wact, g_a, g_b, m_outs, m_grads, route if e == 0 else None, q_sum, e == 0,
            )

        def next_weights(e):
            loads.extend(cp.local(a.at[e], b) for a, b in weights)

        def stream(e, n, sent, kept, at, ring_first):
            streams["GUD"[n] + str(e)] = one = expert_stream(
                cp, place, gr, sent, kept, e_got[n], e_bufs[n], e_total[e][n], at, ring_first,
                (e, n) not in Y_FIRST, free.at[n], e > 0,
            )
            next(one)

        def expert_sums(e, n):
            if n < 2:
                d, back, x_out = ((d_gate, g_a, x_gate), (d_up, g_b, x_up))[n]
                for c in range(0, width, BLOCK):
                    store_rows(
                        d, (2, 4, 2), slice(0, hidden), c, dot_tn(columns_of(x, c), flat(back)).astype(BF)
                    )
                stream(
                    e, n, d.at[place.mate], d.at[core],
                    lambda k, z: x_out.at[e, core, place.y_at[k], z], True,
                )
            else:
                for c in range(0, hidden, 128):
                    left = wact[:, :, c : c + 128].reshape(group, 128)
                    store_rows(d_down, (4, 2), slice(0, width), c, dot_tn(left, flat(g)).astype(BF))
                stream(
                    e, n, d_down.at[:, :, :, theirs], d_down.at[:, :, :, ours],
                    lambda k, z: x_down.at[e, place.y_at[k], z, :, ours], True,
                )

        def own_probs():
            probs[...] = router(x[mine], lane[:rows])

        def start_x():
            for n, (c, b) in enumerate(zip(cuts, b_grads)):
                streams["X" + str(n)] = one = sum_ring_pair(
                    cp, ge, view(m_grads, c), view(m_grads, c), b, total_grads.at[:, c]
                )
                next(one)

        pieces = {"sp": shared_pass, "ss": shared_sums, "x": start_x, "w1": functools.partial(next_weights, 1)}
        for n, pair in enumerate(arrivals):
            pieces["p" + str(n)] = functools.partial(expert_pass, 0, (0, 1), lambda i, pair=pair: pair)
        pieces["q1"] = functools.partial(expert_pass, 1, (0, steps // 2), in_turn)
        pieces["r1"] = functools.partial(expert_pass, 1, (steps // 2, steps), in_turn)
        pieces["pr"] = own_probs
        for e in range(exp_dev):
            for n in range(3):
                pieces["gud"[n] + str(e)] = functools.partial(expert_sums, e, n)
        follow(ORDER_A, pieces)

    def follow(order, pieces):
        for name in order:
            if name in pieces:
                pieces[name]()
            else:
                next(streams[name], None)

    pl.run_scoped(
        phase_a,
        pltpu.VMEM((8, rows, width), BF),
        pltpu.VMEM((width, hidden), BF),
        pltpu.VMEM((width, hidden), BF),
        pltpu.VMEM((hidden, width), BF),
        *[pltpu.VMEM((8, rows, hidden), BF)] * 3,
        *[pltpu.VMEM((8, rows, EXTRA), F32)] * 2,
        *[pltpu.VMEM((8, rows, s_both.shape[1] // 2), BF)] * 3,
        *[pltpu.VMEM((s_both.shape[1] // 2, width), BF)] * 2,
        pltpu.VMEM((2, 4, 2, half_part, hidden), BF),
        pltpu.VMEM((2, 4, 2, half_part, hidden), BF),
        pltpu.VMEM((4, 2, hidden // 8, width), BF),
    )

    def phase_b(
        v_probs, v_qkvs, v_w, w_whole, residual, cot, tok, attended, cosine, sine,
        v_whole, v_qkv, totals, padded, g_att, g_residual, g_keys, g_values, g_qkv, g_branch,
    ):
        loads = [
            cp.local(a, b)
            for a, b in (
                (h_residual, residual), (h_cot, cot), (h_whole, w_whole), (h_attended, attended),
                (h_qkv, v_qkvs), (h_probs, v_probs), (h_cosine, cosine), (h_sine, sine),
                (w_slices.at[:, : v_w.shape[1]], v_w), (h_hidden, x), (h_tok, tok),
            )
        ]
        alive = live[...]
        kept = {}

        step = 256

        def second_norm():
            for copy in loads:
                cp.arrived(copy)
            router_grad = total_grads[:, width:] * alive
            prob = probs[...]
            logit_grad = prob * (router_grad - jnp.sum(prob * router_grad, axis=1, keepdims=True))
            squares = jnp.zeros((rows, 1), F32)
            mean_k = jnp.zeros((rows, 1), F32)
            for c in range(0, width, step):
                part = residual[:, c : c + step]
                squares += jnp.sum(part * part, axis=1, keepdims=True)
            scale = lax.rsqrt(squares / width + EPS)
            gain_rows = []
            for c in range(0, width, step):
                k = total_grads[:, c : c + step] + lax.dot_general(
                    logit_grad, w_whole[c : c + step, width:].astype(F32), (((1,), (1,)), ((), ())),
                    preferred_element_type=F32, precision=HIGH,
                )
                normed = residual[:, c : c + step] * scale
                gain_rows.append(jnp.sum(k * normed, axis=0, keepdims=True))
                k = k * gains[1:2, c : c + step]
                mean_k += jnp.sum(k * normed, axis=1, keepdims=True)
                g_residual[:, c : c + step] = k
            mean_k = mean_k / width
            for c in range(0, width, step):
                normed = residual[:, c : c + step] * scale
                grad = cot[:, c : c + step].astype(F32) + scale * (
                    g_residual[:, c : c + step] - normed * mean_k
                )
                g_residual[:, c : c + step] = grad
                g_branch[:, c : c + step] = (alive * grad).astype(BF)
            for c in range(0, width, step):
                g_att[c // step] = dot_nt(g_branch[...], w_whole[c : c + step, :width]).astype(BF)
            for c in range(width // step, 8):
                g_att[c] = jnp.zeros((rows, span), BF)
            kept["third"] = [cp.local(g_att.at[mine], g_heads.at[mine])] + [
                cp.send(g_att.at[(mine + k) % 8], g_heads.at[mine], place.to_ep(k)) for k in range(1, 8)
            ]
            kept["norm"] = logit_grad, scale, gain_rows

        def whole_sums():
            logit_grad, scale, gain_rows = kept["norm"]
            for i in range(2):
                c = slice(i * width // 2, (i + 1) * width // 2)
                v_whole[2 * i : 2 * i + 2, :, :, :, :width] = (
                    dot_tn(attended[:, c], g_branch[...]).astype(BF).reshape(2, 2, 2, width // 16, width)
                )
                hid = (residual[:, c] * scale * gains[1:2, c]).astype(BF).astype(F32)
                small = lax.dot_general(
                    hid, logit_grad, (((0,), (0,)), ((), ())), preferred_element_type=F32, precision=HIGH
                )
                gain_row = jnp.concatenate(gain_rows, axis=1)[:, c]
                lane = lax.broadcasted_iota(jnp.int32, (width // 2, EXTRA), 1)
                column = jnp.broadcast_to(gain_row, (8, width // 2)).T[:, :1]
                small = jnp.where(lane == EXTRA - 1, column, small)
                v_whole[2 * i : 2 * i + 2, :, :, :, width:] = small.astype(BF).reshape(
                    2, 2, 2, width // 16, EXTRA
                )
            dense("W", 0, v_whole, False, 0, o_whole)

        def dense(name, i, v, ring_first, spread, result):
            one = dense_stream(cp, place, gr, v, got[i], bufs[i], totals[i], ring_first)
            if spread is not None:
                one = spread_stream(cp, place, one, totals[i], padded[spread], result)
            streams[name] = one
            next(one)

        def small_dense():
            dense("S", 1, v_shared, True, 1, o_shared)
            dense("N", 2, v_down, True, None, None)

        def start_out():
            streams["O"] = sum_ring_pair(cp, ge, m_outs, m_outs, b_outs, out, (residual,))
            next(streams["O"])

        def head(h):
            if h == 0:
                for copy in kept["third"]:
                    cp.arrived(copy)
            attention_back_head(h, g_heads, v_qkvs, v_probs, cosine, sine, g_keys, g_values, g_qkv)

        def hidden_part():
            @pl.loop(0, group // BLOCK)
            def _(i):
                at = pl.ds(pl.multiple_of(i * BLOCK, BLOCK), BLOCK)
                part = dot_nt(g_qkv[at, :], v_w[...]).astype(BF)
                m_grads[i, :, :, :width] = part.reshape(2, rows, width)

            hcuts = (pl.ds(0, half), pl.ds(half, width - half))
            for n, ((b,), c) in enumerate(zip(b_grads, hcuts)):
                streams["H" + str(n)] = one = sum_ring_pair(
                    cp, ge, view(m_grads, c), view(m_grads, c), [b.at[:, :, pl.ds(0, c.size)]],
                    total_hidden.at[:, c],
                )
                next(one)

        def qkv_sums():
            for i in range(2):
                c = slice(i * width // 2, (i + 1) * width // 2)
                v_qkv[2 * i : 2 * i + 2] = (
                    dot_tn(x[:, :, c].reshape(group, width // 2), g_qkv[...]).astype(BF).reshape(2, 2, 2, width // 16, 3 * span)
                )
            dense("Q", 3, v_qkv, True, 2, o_qkv)

        def first_norm():
            squares = jnp.zeros((rows, 1), F32)
            mean_k = jnp.zeros((rows, 1), F32)
            for c in range(0, width, step):
                part = tok[:, c : c + step].astype(F32)
                squares += jnp.sum(part * part, axis=1, keepdims=True)
            scale = lax.rsqrt(squares / width + EPS)
            for c in range(0, width, step):
                normed = tok[:, c : c + step].astype(F32) * scale
                k = total_hidden[:, c : c + step] * gains[0:1, c : c + step]
                mean_k += jnp.sum(k * normed, axis=1, keepdims=True)
            mean_k = mean_k / width
            for c in range(0, width, step):
                normed = tok[:, c : c + step].astype(F32) * scale
                k = total_hidden[:, c : c + step] * gains[0:1, c : c + step]
                d_tok[:, c : c + step] = g_residual[:, c : c + step] + scale * (k - normed * mean_k)

        follow(
            ORDER_B,
            {
                "n2": second_norm, "dw": whole_sums, "sn": small_dense, "o": start_out,
                "h0": functools.partial(head, 0), "h1": functools.partial(head, 1),
                "hp": hidden_part, "dq": qkv_sums, "n1": first_norm,
            },
        )
        run_streams(*streams.values())
        o_down[...] = totals[2][...]
        cp.finish()

    columns = (wide, s_both.shape[1], width, 3 * span)
    depth = (half_part, half_part, ROW_PAD, half_part)
    pl.run_scoped(
        phase_b,
        pltpu.VMEM(h_probs.shape, BF),
        pltpu.VMEM(h_qkv.shape, BF),
        pltpu.VMEM((width, 3 * span), BF),
        pltpu.VMEM(h_whole.shape, BF),
        pltpu.VMEM((rows, width), F32),
        *[pltpu.VMEM((rows, width), BF)] * 3,
        *[pltpu.VMEM((group, HD), F32)] * 2,
        pltpu.VMEM((4, 2, 2, half_part, wide), BF),
        pltpu.VMEM((4, 2, 2, half_part, 3 * span), BF),
        [pltpu.VMEM((r, c), BF) for r, c in zip(depth, columns)],
        [pltpu.VMEM((8, ROW_PAD, columns[i]), BF) for i in (0, 1, 3)],
        pltpu.VMEM((8, rows, span), BF),
        pltpu.VMEM((rows, width), F32),
        *[pltpu.VMEM((group, HD), F32)] * 2,
        pltpu.VMEM((group, 3 * span), BF),
        pltpu.VMEM((rows, width), BF),
    )


def call_rest(
    experts, top, x_own, g_all, e_gate, e_up, e_down, h_probs, h_hidden, h_qkv, w_slices, h_whole,
    h_residual, h_cot, h_tok, h_attended, h_cosine, h_sine,
    extra, w_router, s_both, s_padded, live, gains,
):
    anyspace = pl.BlockSpec(memory_space=pl.ANY)
    vmem = pl.BlockSpec(memory_space=pltpu.VMEM)
    rows, width = h_cot.shape
    span = HEADS_DEV * HD
    wide = width + EXTRA
    cut = wide // 2 // 128 * 128
    exp_dev, _, hidden = e_gate.shape
    part = width // 16
    columns = (wide, s_both.shape[1], width, 3 * span)
    depth = (part, part, ROW_PAD, part)
    orders = (False, True, True, True)
    halves = ((part, hidden), (part, hidden), (hidden // 8, width // 2))
    bufs_of = lambda first, r, c: (ring_pair_bufs if first else pair_ring_bufs)(r, c)
    shape = jax.ShapeDtypeStruct
    return pl.pallas_call(
        functools.partial(kernel_rest, experts, top),
        out_shape=(
            shape((rows, width), BF),
            shape((rows, width), F32),
            shape((exp_dev, 2, 4, 2, part, hidden), BF),
            shape((exp_dev, 2, 4, 2, part, hidden), BF),
            shape((exp_dev, 4, 2, hidden // 8, width), BF),
            shape((8, ROW_PAD, 3 * span), BF),
            shape((8, ROW_PAD, columns[1]), BF),
            shape((8, ROW_PAD, wide), BF),
            shape((ROW_PAD, width), BF),
        ),
        in_specs=[anyspace] * 16 + [vmem] * 6,
        out_specs=(vmem, vmem) + (anyspace,) * 6 + (vmem,),
        scratch_shapes=[
            pltpu.VMEM((8, rows, width), BF),
            pltpu.VMEM((4, 2, rows, wide), BF),
            pltpu.VMEM((4, 2, rows, width), BF),
            [ring_pair_bufs(rows, c) for c in (cut, wide - cut)],
            ring_pair_bufs(rows, width),
            pltpu.VMEM((rows, wide), F32),
            pltpu.VMEM((rows, width), F32),
            [pltpu.VMEM((4, 2) + h, BF) for h in halves],
            [ring_pair_bufs(*h) for h in halves],
            [[pltpu.VMEM(h, BF) for h in halves] for _ in range(exp_dev)],
            pltpu.VMEM((4, 2, 2, part, columns[1]), BF),
            pltpu.VMEM((4, 2, 2, ROW_PAD, width), BF),
            [pltpu.VMEM((4, 2, r, c), BF) for r, c in zip(depth, columns)],
            [bufs_of(first, r, c) for first, r, c in zip(orders, depth, columns)],
            pltpu.VMEM((8, rows, span), BF),
            pltpu.VMEM((rows, EXTRA), F32),
            pltpu.SemaphoreType.REGULAR((3,)),
            pltpu.SemaphoreType.DMA((440,)),
            pltpu.SemaphoreType.DMA((440,)),
        ],
        compiler_params=pltpu.CompilerParams(
            collective_id=2, has_side_effects=True, vmem_limit_bytes=int(63.9 * 2**20)
        ),
        name="rest",
    )(
        x_own, g_all, e_gate, e_up, e_down, h_probs, h_hidden, h_qkv, w_slices, h_whole,
        h_residual, h_cot, h_tok, h_attended, h_cosine, h_sine,
        extra, w_router, s_both, s_padded, live, gains,
    )


def kernel_finish(
    o_qkv, o_shared, o_whole, o_down, w_query, w_key, w_value, norm_attn, b_gate, b_up, b_down,
    d_query, d_key, d_value, d_output, d_router, d_sgate, d_sup, d_sdown, d_norm_one, d_norm_two,
    d_gate, d_up, d_down,
):
    used, width = w_query.shape
    hidden = d_sgate.shape[1]
    span = HEADS_DEV * HD
    for low, full in ((b_gate, d_gate), (b_up, d_up), (b_down, d_down)):
        full[...] = low[...].astype(F32)

    step = pl.program_id(0)

    @pl.when(step == 1)
    def _():
        gain = jnp.zeros((used, 1), F32)
        for n, (w, d) in enumerate(((w_query, d_query), (w_key, d_key), (w_value, d_value))):
            for owner in range(width // span):
                c = slice(owner * span, (owner + 1) * span)
                part = o_qkv[owner, :used, n * span : (n + 1) * span].astype(F32)
                d[:, c] = part
                gain += jnp.sum(part * w[:, c].astype(F32), axis=1, keepdims=True)
        d_norm_one[...] = as_row(gain) / norm_attn[...].astype(F32)

    for n, d in enumerate((d_sgate, d_sup)):
        for half in range(2):

            @pl.when(step == 3 + 4 * n + 2 * half)
            def _(n=n, d=d, half=half):
                total = jnp.zeros((ROW_PAD, hidden), F32)
                for owner in range(4 * half, 4 * half + 4):
                    pick = shared_columns(owner, hidden, d_sdown.shape[0])
                    total += dot_nt(o_shared[owner, :, n * 128 : (n + 1) * 128], pick)
                d[...] = total[:used] if half == 0 else d[...] + total[:used]

    @pl.when(step == 11)
    def _():
        total = o_whole[0].astype(F32)
        for i in range(1, 8):
            total += o_whole[i].astype(F32)
        d_output[...] = total[:used, :width]
        d_router[...] = total[:used, width : width + d_router.shape[1]]
        d_norm_two[...] = as_row(total[:used, width + EXTRA - 1 :])
        d_sdown[...] = o_down[: d_sdown.shape[0]].astype(F32)


def call_finish(
    o_qkv, o_shared, o_whole, o_down, w_query, w_key, w_value, norm_attn, b_gate, b_up, b_down,
    experts, hidden,
):
    used, width = w_query.shape
    down_used = hidden // 128
    shape = jax.ShapeDtypeStruct
    steps = 16
    fixed = lambda a: pl.BlockSpec(a.shape, lambda i: (0,) * len(a.shape))
    part = lambda a: pl.BlockSpec((a.shape[0] // steps, a.shape[1]), lambda i: (i, 0))
    small = (
        [shape((used, width), F32)] * 4
        + [shape((used, experts), F32)]
        + [shape((used, hidden), F32)] * 2
        + [shape((down_used, width), F32)]
        + [shape((1, used), F32)] * 2
    )
    large = [shape(a.shape, F32) for a in (b_gate, b_up, b_down)]
    operands = (o_qkv, o_shared, o_whole, o_down, w_query, w_key, w_value, norm_attn)
    return pl.pallas_call(
        kernel_finish,
        grid=(steps,),
        out_shape=tuple(small + large),
        in_specs=[fixed(a) for a in operands] + [part(a) for a in (b_gate, b_up, b_down)],
        out_specs=tuple([fixed(a) for a in small] + [part(a) for a in large]),
        compiler_params=pltpu.CompilerParams(
            vmem_limit_bytes=VMEM_LIMIT, dimension_semantics=("arbitrary",)
        ),
        name="finish",
    )(*operands, b_gate, b_up, b_down)


def body(
    tokens, cotangent, lengths, token_mask, routes,
    w_query, w_key, w_value, w_output, w_router,
    shared_gate, shared_up, shared_down, norm_attn, norm_ffn,
    expert_gate, expert_up, expert_down,
):
    rows, width = tokens.shape
    used = w_query.shape[0]
    exp_dev, _, hidden = expert_gate.shape
    experts = w_router.shape[1]
    group = rows * 8
    frequency = 10000.0 ** (-(np.arange(HD // 2, dtype=np.float32) * np.float32(2.0) / HD))
    angles = np.arange(group, dtype=np.float32)[:, None] * frequency.astype(np.float32)[None, :]
    cosine = jnp.asarray(np.tile(np.cos(angles), (1, 2)), F32)
    sine = jnp.asarray(np.concatenate([-np.sin(angles), np.sin(angles)], axis=1), F32)
    (
        w_slices, w_both, w_whole, w_router_all, w_down, cot_all, extra,
        hidden_one, qkv, attn_probs, gain_rows, residual, attended, hidden_two, live,
    ) = call_front(
        tokens, cotangent, lengths[None], token_mask[None], routes.T,
        w_query, w_key, w_value, w_output, w_router,
        shared_gate, shared_up, shared_down, norm_attn[None], norm_ffn[None], cosine, sine,
    )
    out, d_tokens, e_gate, e_up, e_down, o_qkv, o_shared, o_whole, o_down = call_rest(
        experts, routes.shape[1],
        hidden_two, cot_all, expert_gate, expert_up, expert_down,
        attn_probs, hidden_one.reshape(8, rows, width), qkv,
        w_slices.reshape(width, -1), w_whole.reshape(width, -1),
        residual, cotangent, tokens, attended, cosine, sine,
        extra, w_router_all.reshape(width, EXTRA),
        w_both.reshape(width, -1), w_down.reshape(-1, width), live, gain_rows,
    )
    (
        d_query, d_key, d_value, d_output, d_router, d_sgate, d_sup, d_sdown, d_norm_one, d_norm_two,
        d_gate, d_up, d_down,
    ) = call_finish(
        o_qkv, o_shared, o_whole, o_down, w_query, w_key, w_value, norm_attn[None],
        e_gate.reshape(-1, hidden), e_up.reshape(-1, hidden), e_down.reshape(-1, width),
        experts, hidden,
    )
    return (
        out, d_tokens, d_query, d_key, d_value, d_output, d_router, d_sgate, d_sup, d_sdown,
        d_norm_one.reshape(used), d_norm_two.reshape(used),
        d_gate.reshape(exp_dev, width, hidden), d_up.reshape(exp_dev, width, hidden),
        d_down.reshape(exp_dev, hidden, width),
    )


def solution(mesh):
    both = ("rep", "ep")
    row = P(both, None)
    expert = P("ep", None, None)
    in_specs = (
        row, row, P("rep"), P(both), row, row, row, row, row, row, row, row, row,
        P(both), P(both), expert, expert, expert,
    )
    out_specs = (
        row, row, row, row, row, row, row, row, row, row, P(both), P(both),
        expert, expert, expert,
    )
    return jax.shard_map(body, mesh=mesh, in_specs=in_specs, out_specs=out_specs, check_vma=False)
```

```python
import functools
import itertools
import math

import jax
import jax.numpy as jnp
import numpy as np
from jax import lax
from jax.experimental import pallas as pl
from jax.experimental.pallas import tpu as pltpu
from jax.sharding import PartitionSpec as P

HD = 128
EPS = 1e-6
BF = jnp.bfloat16
F32 = jnp.float32
MESH = pl.DeviceIdType.MESH
HIGH = lax.Precision.HIGHEST
HEADS_DEV = 2
EXTRA = 128
ROW_PAD = 16
VMEM_LIMIT = 60 << 20
LIVE = 7


def dot(a, b):
    return jnp.dot(a, b, preferred_element_type=F32)


def dot_nt(a, b):
    return lax.dot_general(a, b, (((1,), (1,)), ((), ())), preferred_element_type=F32)


def dot_tn(a, b):
    return lax.dot_general(a, b, (((0,), (0,)), ((), ())), preferred_element_type=F32)


class Place:
    def __init__(self):
        self.rep = lax.axis_index("rep")
        self.ep = lax.axis_index("ep")
        self.y = self.rep // 4
        self.zl = (self.rep // 2) % 2
        self.core = self.rep % 2
        self.x = self.ep // 2
        self.zh = self.ep % 2

        self.mate = 1 - self.core
        self.y_at = {k: (self.y + k) % 4 for k in (-1, 0, 1, 2)}
        self.from_x = {k: self.ep_at(self.x + k, self.zh) for k in (-1, 1, 2)}
        self.from_z = {k: self.ep_at(self.x + k, 1 - self.zh) for k in (-1, 0, 1, 2)}
        self._x = {k: (self.rep, self.ep_at(self.x + k, self.zh)) for k in (-1, 1)}
        self._y = {k: (self.rep_at(self.y + k, self.zl, self.core), self.ep) for k in (-1, 1)}
        self._ep = {k: (self.rep, (self.ep + k) % 8) for k in range(1, 8)}
        self._zh = (self.rep, self.ep_at(self.x, 1 - self.zh))
        self._zl = (self.rep_at(self.y, 1 - self.zl, self.core), self.ep)
        self._core = (self.rep_at(self.y, self.zl, self.mate), self.ep)

    def rep_at(self, y, zl, core):
        return (y % 4) * 4 + zl * 2 + core

    def ep_at(self, x, zh):
        return (x % 4) * 2 + zh

    def to_x(self, step):
        return self._x[step]

    def to_zh(self):
        return self._zh

    def to_ep(self, shift):
        return self._ep[shift]

    def to_y(self, step):
        return self._y[step]

    def to_zl(self):
        return self._zl

    def to_core(self):
        return self._core


class Later:
    def __init__(self, ref, path=()):
        self.ref, self.path = ref, path

    @property
    def at(self):
        return LaterAt(self)

    @property
    def shape(self):
        return self.made().shape

    @property
    def dtype(self):
        return self.ref.dtype

    def made(self):
        ref = self.ref
        for index in self.path:
            ref = ref.at[index]
        return ref

    def __getitem__(self, index):
        return self.made()[index]

    def __setitem__(self, index, value):
        self.made()[index] = value


class LaterAt:
    def __init__(self, later):
        self.later = later

    def __getitem__(self, index):
        return Later(self.later.ref, self.later.path + (index,))


def made(ref):
    return ref.made() if isinstance(ref, Later) else ref


class Copies:
    def __init__(self, send_sem, recv_sem):
        self.send_sem, self.recv_sem = send_sem, recv_sem
        self.number = itertools.count()
        self.sent, self.open = [], []

    def send(self, src, dst, device):
        i = next(self.number)

        def copy():
            return pltpu.make_async_remote_copy(
                src_ref=made(src),
                dst_ref=made(dst),
                send_sem=self.send_sem.at[i],
                recv_sem=self.recv_sem.at[i],
                device_id=device,
                device_id_type=MESH,
            )

        copy().start()
        self.sent.append(copy)
        self.open.append(copy)
        return copy

    def local(self, src, dst):
        i = next(self.number)

        def copy():
            return pltpu.make_async_copy(made(src), made(dst), self.recv_sem.at[i])

        copy().start()
        self.open.append(copy)
        return copy

    def arrived(self, copy):
        if any(copy is c for c in self.sent):
            copy().wait_recv()
        else:
            copy().wait()
        self.open = [c for c in self.open if c is not copy]

    def sent_off(self, copy):
        copy().wait_send()
        self.sent = [c for c in self.sent if c is not copy]

    def drain(self, stream):
        for _ in stream:
            pass

    def finish(self):
        for copy in list(self.open):
            self.arrived(copy)
        for copy in list(self.sent):
            self.sent_off(copy)


def greet(devices, meanwhile=lambda: None):
    barrier = pltpu.get_barrier_semaphore()
    for device in devices:
        pl.semaphore_signal(barrier, inc=1, device_id=device, device_id_type=MESH)
    meanwhile()
    pl.semaphore_wait(barrier, len(devices))


def as_column(row):
    shape = (row.shape[1],) * 2
    same = lax.broadcasted_iota(jnp.int32, shape, 0) == lax.broadcasted_iota(jnp.int32, shape, 1)
    return jnp.sum(jnp.where(same, row, 0.0), axis=1, keepdims=True)


def as_row(column):
    shape = (column.shape[0],) * 2
    same = lax.broadcasted_iota(jnp.int32, shape, 0) == lax.broadcasted_iota(jnp.int32, shape, 1)
    return jnp.sum(jnp.where(same, column, 0.0), axis=0, keepdims=True)


def shared_columns(owner, hidden, used):
    shape = (hidden, 128)
    unit = lax.broadcasted_iota(jnp.int32, shape, 0)
    k = lax.broadcasted_iota(jnp.int32, shape, 1)
    taken = (k < 16 * used) & (unit == (k // used) * 8 * used + owner * used + k % used)
    return jnp.where(taken, 1.0, 0.0).astype(BF)


def run_streams(*streams):
    live = list(streams)
    while live:
        for stream in list(live):
            try:
                next(stream)
            except StopIteration:
                live.remove(stream)


def half_columns(columns):
    return (columns // 128 + 1) // 2 * 128


def ep_peers(place):
    return [place.to_ep(k) for k in range(1, 8)]


def rep_peers(place):
    return [place.to_y(1), place.to_y(-1), place.to_zl(), place.to_core()]


def gather_ep(cp, place, src, dst, columns):
    cut = half_columns(columns)
    lo, hi = pl.ds(0, cut), pl.ds(cut, columns - cut)
    mine = place.ep
    own = cp.local(src, dst.at[mine])
    right = cp.send(src, dst.at[mine], place.to_x(1))
    left = cp.send(src, dst.at[mine], place.to_x(-1))
    over = cp.send(src, dst.at[mine], place.to_zh())
    yield
    from_left, from_right, far = (place.from_x[k] for k in (-1, 1, 2))
    from_over = place.from_z[0]
    cp.arrived(own)
    cp.arrived(right)
    half_a = cp.send(dst.at[from_left, :, lo], dst.at[from_left, :, lo], place.to_x(1))
    cp.arrived(left)
    half_b = cp.send(dst.at[from_right, :, hi], dst.at[from_right, :, hi], place.to_x(-1))
    yield
    cp.arrived(over)
    last = []
    last.append(cp.send(dst.at[from_over], dst.at[from_over], place.to_x(1)))
    last.append(cp.send(dst.at[from_over], dst.at[from_over], place.to_x(-1)))
    yield
    cp.arrived(half_a)
    cp.arrived(half_b)
    last.append(cp.send(dst.at[far], dst.at[far], place.to_zh()))
    yield
    for copy in last:
        cp.arrived(copy)
    for copy in [right, left, over, half_a, half_b] + last:
        cp.sent_off(copy)


def gather_ring_y(cp, place, src, dst, columns, slot):
    cut = half_columns(columns)
    lo, hi = pl.ds(0, cut), pl.ds(cut, columns - cut)
    up = cp.send(src, dst.at[slot(place.y)], place.to_y(1))
    down = cp.send(src, dst.at[slot(place.y)], place.to_y(-1))
    yield
    cp.arrived(up)
    below = slot(place.y - 1)
    half_a = cp.send(dst.at[below, :, lo], dst.at[below, :, lo], place.to_y(1))
    cp.arrived(down)
    above = slot(place.y + 1)
    half_b = cp.send(dst.at[above, :, hi], dst.at[above, :, hi], place.to_y(-1))
    yield
    cp.arrived(half_a)
    cp.arrived(half_b)


def gather_rep(cp, place, src, dst, columns, z_first):
    mine = place.rep
    last = [cp.local(src, dst.at[mine]), cp.send(src, dst.at[mine], place.to_core())]

    def slot(zl):
        return lambda y: place.rep_at(y, zl, place.core)

    def pass_core(index):
        last.append(cp.send(dst.at[index], dst.at[index], place.to_core()))

    here, there = slot(place.zl), slot(1 - place.zl)
    if z_first:
        over = cp.send(src, dst.at[mine], place.to_zl())
        first = gather_ring_y(cp, place, src, dst, columns, here)
        next(first)
        yield
        cp.arrived(over)
        second = gather_ring_y(
            cp, place, dst.at[there(place.y)], dst, columns, there
        )
        next(second)
        pass_core(there(place.y))
        yield
        next(first)
        for k in (-1, 1):
            pass_core(here(place.y + k))
        yield
        next(second)
        for k in (-1, 1):
            pass_core(there(place.y + k))
        yield
        next(first, None)
        pass_core(here(place.y + 2))
        yield
        next(second, None)
        pass_core(there(place.y + 2))
    else:
        over = [cp.send(src, dst.at[mine], place.to_zl())]
        ring = gather_ring_y(cp, place, src, dst, columns, here)
        next(ring)
        yield
        next(ring)
        for k in (-1, 1):
            block = dst.at[here(place.y + k)]
            over.append(cp.send(block, block, place.to_zl()))
            pass_core(here(place.y + k))
        yield
        next(ring, None)
        block = dst.at[here(place.y + 2)]
        over.append(cp.send(block, block, place.to_zl()))
        pass_core(here(place.y + 2))
        yield
        for copy, k in zip(over, (0, -1, 1, 2)):
            cp.arrived(copy)
            pass_core(there(place.y + k))
            yield
    yield
    for copy in last:
        cp.arrived(copy)


def spread_matrix(rows, blocks, used):
    shape = (rows, blocks * ROW_PAD)
    to = lax.broadcasted_iota(jnp.int32, shape, 0)
    at = lax.broadcasted_iota(jnp.int32, shape, 1)
    return jnp.where((at // ROW_PAD) * used + at % ROW_PAD == to, 1.0, 0.0) * jnp.where(
        at % ROW_PAD < used, 1.0, 0.0
    )


ORDER_F = (
    "a", "k1", "wa", "T", "T", "L", "L", "T", "L", "k2", "L", "c", "L", "L",
    "T", "pr", "W", "h0", "C", "h1", "W", "W", "C", "W", "C", "D", "D", "W",
    "D", "D", "W", "D", "D", "op", "C",
)


def kernel_front(
    tok, cot, length, mask, routes, w_query, w_key, w_value, w_output, w_route,
    shared_gate, shared_up, shared_down, norm_attn, norm_ffn, h_cosine, h_sine,
    w_slices, w_both, w_whole, w_router, w_down, cot_all, extra,
    o_hidden, o_qkv, o_probs, gains, residual, attended, hidden, live,
    hidden_one, qkv, probs, cosine, sine, slices, whole, down, wide_tok,
    land_slices, land_whole, pack_slices, pack_whole, v_slices, v_whole, v_tok,
    heads, land_heads, live_row, send_sem, recv_sem,
):
    place = Place()
    cp = Copies(send_sem, recv_sem)
    rows, width = tok.shape
    group = 8 * rows
    span = HEADS_DEV * HD
    mine = place.ep
    top = routes.shape[0]

    def own_inputs():
        position = mine * rows + lax.broadcasted_iota(jnp.int32, (1, rows), 1)
        alive = jnp.where((position < length[...]) & (mask[...] == 1), 1.0, 0.0)
        live[...] = as_column(alive)
        block = jnp.concatenate(
            [routes[...].astype(F32), alive, jnp.zeros((EXTRA - top - 1, rows), F32)], axis=0
        )
        wide_tok[:, :width] = tok[...]
        wide_tok[:, width:] = block.T.astype(BF)
        for ref in (slices, whole, down):
            ref[...] = jnp.zeros_like(ref)
        rows_of = slice(0, w_query.shape[0])
        whole[rows_of, :width] = w_output[...]
        whole[rows_of, width : width + w_route.shape[1]] = w_route[...]
        down[: shared_down.shape[0], :] = shared_down[...]
        gains_of = [as_column(g[...].astype(F32)) for g in (norm_attn, norm_ffn)]
        lane = lax.broadcasted_iota(jnp.int32, (w_query.shape[0], 128), 1)
        spare = 16 * shared_down.shape[0]
        for owner in range(8):
            if owner * span < width:
                for n, w in enumerate((w_query, w_key, w_value)):
                    slices[owner, rows_of, n * span : (n + 1) * span] = w[:, owner * span : (owner + 1) * span]
            pick = shared_columns(owner, shared_gate.shape[1], shared_down.shape[0])
            gate = dot(shared_gate[...], pick)
            gate = jnp.where(lane == spare, gains_of[0], jnp.where(lane == spare + 1, gains_of[1], gate))
            slices[owner, rows_of, 3 * span : 3 * span + 128] = gate.astype(BF)
            slices[owner, rows_of, 3 * span + 128 :] = dot(shared_up[...], pick).astype(BF)

    tables = [cp.local(h_cosine, cosine), cp.local(h_sine, sine)]
    greet(ep_peers(place) + rep_peers(place), own_inputs)
    streams, kept = {}, {}
    used = pack_slices.shape[0] // 8
    per = BLOCK // rows

    def pack(land, packed):
        spread = spread_matrix(8 * used, 8, used).astype(BF)
        for c in range(0, land.shape[2], 128):
            block = land[:, :, c : c + 128].reshape(8 * ROW_PAD, 128)
            packed[:, c : c + 128] = dot(spread, block).astype(BF)

    def start(name, stream):
        streams[name] = stream
        next(stream)

    def to_owners():
        kept["slices"] = [cp.local(slices.at[mine], land_slices.at[mine])] + [
            cp.send(slices.at[(mine + k) % 8], land_slices.at[mine], place.to_ep(k)) for k in range(1, 8)
        ]
        start("T", gather_ep(cp, place, wide_tok, v_tok, wide_tok.shape[1]))

    def to_all():
        kept["whole"] = [cp.local(whole, land_whole.at[mine])] + [
            cp.send(whole, land_whole.at[mine], place.to_ep(k)) for k in range(1, 8)
        ]

    def pack_first():
        for copy in kept["slices"]:
            cp.arrived(copy)
        pack(land_slices, pack_slices)
        start("L", gather_rep(cp, place, pack_slices, v_slices, slices.shape[2], True))

    def pack_second():
        for copy in kept["whole"]:
            cp.arrived(copy)
        pack(land_whole, pack_whole)
        start("W", gather_rep(cp, place, pack_whole, v_whole, whole.shape[1], True))
        start("D", gather_rep(cp, place, down, w_down, down.shape[1], True))

    def start_cot():
        start("C", gather_ep(cp, place, cot, cot_all, width))

    def projections():
        cp.local(v_slices, w_slices)
        cp.local(v_slices.at[:, :, pl.ds(3 * span, 256)], w_both)
        cp.local(v_tok.at[:, :, pl.ds(width, EXTRA)], extra)
        block = v_slices[:, :, 3 * span : 3 * span + 128].reshape(width, 128).astype(F32).T
        gains[...] = block[112:120, :]
        live_row[...] = jnp.concatenate(
            [v_tok[i, :, width:].astype(F32).T[:8, :] for i in range(8)], axis=1
        )

        for copy in tables:
            cp.arrived(copy)

        @pl.loop(0, group // BLOCK)
        def _(i):
            at = pl.ds(pl.multiple_of(i * BLOCK, BLOCK), BLOCK)
            values = v_tok[pl.ds(i * per, per), :, :width].reshape(BLOCK, width).astype(F32)
            scale = lax.rsqrt(jnp.sum(values * values, axis=1, keepdims=True) / width + EPS)
            low = (values * scale * gains[0:1, :]).astype(BF)
            hidden_one[at, :] = low
            raw = dot(low, v_slices[:, :, : 3 * span].reshape(width, 3 * span))
            cos, sin = cosine[at, :], sine[at, :]
            for h in range(2 * HEADS_DEV):
                c = slice(h * HD, (h + 1) * HD)
                qkv[at, c] = turn(raw[:, c], cos, sin).astype(BF)
            qkv[at, 2 * span :] = raw[:, 2 * span :].astype(BF)

        cp.local(hidden_one, o_hidden)
        cp.local(qkv, o_qkv)

    def head(h):
        attention_head(h, qkv, live_row, probs, heads)
        cp.local(probs.at[h], o_probs.at[h])
        if h == HEADS_DEV - 1:
            column = pl.ds(pl.multiple_of(mine * span, 128), span)
            kept["heads"] = [cp.local(heads.at[mine], land_heads.at[:, column])] + [
                cp.send(heads.at[(mine + k) % 8], land_heads.at[:, column], place.to_ep(k))
                for k in range(1, 8)
            ]

    def output():
        cp.local(v_whole, w_whole)
        cp.local(v_whole.at[:, :, pl.ds(width, EXTRA)], w_router)
        for copy in kept["heads"]:
            cp.arrived(copy)
        low = land_heads[:, :width]
        attended[...] = low
        step = 256
        squares = jnp.zeros((rows, 1), F32)
        for c in range(0, width, step):
            matrix = v_whole[:, :, c : c + step].reshape(width, step)
            part = tok[:, c : c + step].astype(F32) + live[...] * dot(low, matrix)
            residual[:, c : c + step] = part
            squares += jnp.sum(part * part, axis=1, keepdims=True)
        scale = lax.rsqrt(squares / width + EPS)
        hidden[...] = (residual[...] * scale * gains[1:2, :]).astype(BF)

    pieces = {
        "a": to_owners, "wa": to_all, "k1": pack_first, "k2": pack_second, "c": start_cot, "pr": projections,
        "h0": functools.partial(head, 0), "h1": functools.partial(head, 1), "op": output,
    }
    for name in ORDER_F:
        if name in pieces:
            pieces[name]()
        else:
            next(streams[name], None)
    run_streams(*streams.values())
    cp.finish()


def call_front(
    tok, cot, length, mask, routes, w_query, w_key, w_value, w_output, w_route,
    shared_gate, shared_up, shared_down, norm_attn, norm_ffn, cosine, sine,
):
    anyspace = pl.BlockSpec(memory_space=pl.ANY)
    vmem = pl.BlockSpec(memory_space=pltpu.VMEM)
    rows, width = cot.shape
    used = w_query.shape[0]
    group = 8 * rows
    span = HEADS_DEV * HD
    shape = jax.ShapeDtypeStruct
    columns, wide = 3 * span + 256, width + EXTRA
    return pl.pallas_call(
        kernel_front,
        out_shape=(
            shape((16, 8 * used, columns), BF),
            shape((16, 8 * used, columns - 3 * span), BF),
            shape((16, 8 * used, wide), BF),
            shape((16, 8 * used, EXTRA), BF),
            shape((16, ROW_PAD, width), BF),
            shape((8,) + cot.shape, BF),
            shape((8, rows, EXTRA), BF),
            shape((group, width), BF),
            shape((group, 3 * span), BF),
            shape((HEADS_DEV, group, group), BF),
            shape((8, width), F32),
            shape((rows, width), F32),
            shape((rows, width), BF),
            shape((rows, width), BF),
            shape((rows, 1), F32),
        ),
        in_specs=[vmem, anyspace] + [vmem] * 13 + [anyspace] * 2,
        out_specs=(anyspace,) * 10 + (vmem,) * 5,
        scratch_shapes=[
            pltpu.VMEM((group, width), BF),
            pltpu.VMEM((group, 3 * span), BF),
            pltpu.VMEM((HEADS_DEV, group, group), BF),
            pltpu.VMEM((group, HD), F32),
            pltpu.VMEM((group, HD), F32),
            pltpu.VMEM((8, ROW_PAD, columns), BF),
            pltpu.VMEM((ROW_PAD, wide), BF),
            pltpu.VMEM((ROW_PAD, width), BF),
            pltpu.VMEM((rows, wide), BF),
            pltpu.VMEM((8, ROW_PAD, columns), BF),
            pltpu.VMEM((8, ROW_PAD, wide), BF),
            pltpu.VMEM((8 * used, columns), BF),
            pltpu.VMEM((8 * used, wide), BF),
            pltpu.VMEM((16, 8 * used, columns), BF),
            pltpu.VMEM((16, 8 * used, wide), BF),
            pltpu.VMEM((8, rows, wide), BF),
            pltpu.VMEM((8, rows, span), BF),
            pltpu.VMEM((rows, 8 * span), BF),
            pltpu.VMEM((8, group), F32),
            pltpu.SemaphoreType.DMA((200,)),
            pltpu.SemaphoreType.DMA((200,)),
        ],
        compiler_params=pltpu.CompilerParams(
            collective_id=0, has_side_effects=True, vmem_limit_bytes=VMEM_LIMIT
        ),
        name="front",
    )(
        tok, cot, length, mask, routes, w_query, w_key, w_value, w_output, w_route,
        shared_gate, shared_up, shared_down, norm_attn, norm_ffn, cosine, sine,
    )


def add_into(out, terms):
    lead = out.shape[:-2]
    count = math.prod(lead)

    def add(index):
        if len(terms) == 2 and out.dtype == BF:
            out[index] = terms[0][index] + terms[1][index]
            return
        total = terms[0][index].astype(F32)
        for term in terms[1:]:
            total += term[index].astype(F32)
        out[index] = total.astype(out.dtype)

    if count == 1:
        add((0,) * len(lead) + (slice(None),))
    else:
        inner = lead[-1] if lead else 1

        @pl.loop(0, count)
        def _(i):
            add(((i // inner, i % inner) if len(lead) == 2 else (i,)) + (slice(None),))


class Grid:
    def __init__(self, ring, pair, up, down, over):
        self.here, self.up_at, self.down_at, self.far = ring, (ring + 1) % 4, (ring + 3) % 4, (ring + 2) % 4
        self.pair, self.other = pair, 1 - pair
        self.up, self.down, self.over = up, down, over


def grid_rep(place):
    return Grid(place.y, place.zl, place.to_y(1), place.to_y(-1), place.to_zl())


def grid_ep(place):
    return Grid(place.x, place.zh, place.to_x(1), place.to_x(-1), place.to_zh())


def ring_pair_bufs(rows, columns):
    return [pltpu.VMEM((7, rows, columns), BF)]


def sum_ring_pair(cp, g, source, mine, bufs, out, more=()):
    (buf,) = bufs
    near, last, half, over = (0, 1), ((2, 3), (4, 5)), 0, 6
    b = lambda i: buf.at[i]
    s1 = cp.send(source.at[g.far, 0], b(near[0]), g.up)
    s2 = cp.send(source.at[g.far, 1], b(near[1]), g.down)
    s3 = cp.send(source.at[g.up_at, 1], b(last[0][1]), g.up)
    s4 = cp.send(source.at[g.down_at, 0], b(last[1][0]), g.down)
    yield
    cp.arrived(s1)
    add_into(mine.at[g.up_at, 0], [mine.at[g.up_at, 0], b(near[0])])
    s5 = cp.send(mine.at[g.up_at, 0], b(last[0][0]), g.up)
    cp.arrived(s2)
    add_into(mine.at[g.down_at, 1], [mine.at[g.down_at, 1], b(near[1])])
    s6 = cp.send(mine.at[g.down_at, 1], b(last[1][1]), g.down)
    yield
    for copy in (s3, s4, s5, s6):
        cp.arrived(copy)
    add_into(
        b(half),
        [mine.at[g.here, g.other], buf.at[2 + g.other], buf.at[4 + g.other]],
    )
    s7 = cp.send(b(half), b(over), g.over)
    yield
    cp.arrived(s7)
    add_into(
        out, [mine.at[g.here, g.pair], buf.at[2 + g.pair], buf.at[4 + g.pair], b(over), *more]
    )
    for copy in (s1, s2, s3, s4, s5, s6, s7):
        cp.sent_off(copy)


def pair_ring_bufs(rows, columns):
    cut = half_columns(columns)
    return [
        pltpu.VMEM((4, rows, columns), BF),
        pltpu.VMEM((2, rows, columns), BF),
        pltpu.VMEM((rows, cut), BF),
        pltpu.VMEM((rows, columns - cut), BF),
    ]


def sum_pair_ring(cp, g, source, mine, bufs, out):
    acc, last, near_lo, near_hi = bufs
    columns = acc.shape[2]
    cut = half_columns(columns)
    lo, hi = pl.ds(0, cut), pl.ds(cut, columns - cut)
    s0 = cp.send(source.at[:, g.other], acc, g.over)
    yield
    cp.arrived(s0)
    add_into(acc, [acc, mine.at[:, g.pair]])
    s1 = cp.send(acc.at[g.far, :, lo], near_lo, g.up)
    s2 = cp.send(acc.at[g.far, :, hi], near_hi, g.down)
    s3 = cp.send(acc.at[g.up_at, :, hi], last.at[0, :, hi], g.up)
    s4 = cp.send(acc.at[g.down_at, :, lo], last.at[1, :, lo], g.down)
    yield
    cp.arrived(s1)
    part = acc.at[g.up_at, :, lo]
    add_into(part, [part, near_lo])
    s5 = cp.send(part, last.at[0, :, lo], g.up)
    cp.arrived(s2)
    part = acc.at[g.down_at, :, hi]
    add_into(part, [part, near_hi])
    s6 = cp.send(part, last.at[1, :, hi], g.down)
    yield
    for copy in (s3, s4, s5, s6):
        cp.arrived(copy)
    add_into(out, [acc.at[g.here], last.at[0], last.at[1]])
    for copy in (s0, s1, s2, s3, s4, s5, s6):
        cp.sent_off(copy)


def gather_expert(cp, place, grid, src, at, z_first):
    zl, other = grid.pair, grid.other
    columns = src.shape[1]
    cut = half_columns(columns)
    lo, hi = pl.ds(0, cut), pl.ds(cut, columns - cut)
    up, down, over, mate = place.to_y(1), place.to_y(-1), place.to_zl(), place.to_core()

    def forward(k, z, to):
        return cp.send(at(k, z), at(k, z), to)

    def ring_halves(z):
        a = cp.send(at(-1, z).at[:, lo], at(-1, z).at[:, lo], up)
        b = cp.send(at(1, z).at[:, hi], at(1, z).at[:, hi], down)
        return a, b

    own = cp.local(src, at(0, zl))
    first = [cp.send(src, at(0, zl), to) for to in (up, down)]
    across = cp.send(src, at(0, zl), over)
    cp.send(src, at(0, zl), mate)
    yield
    if z_first:
        cp.arrived(across)
        second = [forward(0, other, to) for to in (up, down)]
        forward(0, other, mate)
        yield
        halves = []
        for pair, z in ((first, zl), (second, other)):
            for copy in pair:
                cp.arrived(copy)
            halves.append(ring_halves(z))
            forward(-1, z, mate)
            forward(1, z, mate)
            yield
        for pair, z in zip(halves, (zl, other)):
            for copy in pair:
                cp.arrived(copy)
            forward(2, z, mate)
            yield
    else:
        for copy in first:
            cp.arrived(copy)
        halves = ring_halves(zl)
        crossed = [across]
        for k in (-1, 1):
            crossed.append(forward(k, zl, over))
            forward(k, zl, mate)
        yield
        for copy in halves:
            cp.arrived(copy)
        crossed.append(forward(2, zl, over))
        forward(2, zl, mate)
        yield
        for copy, k in zip(crossed, (0, -1, 1, 2)):
            cp.arrived(copy)
            forward(k, other, mate)
            yield
    cp.arrived(own)


def expert_stream(cp, place, grid, sent, kept, got, bufs, total, at, ring_first, z_first, free, again):
    neighbours = rep_peers(place)
    if again:
        pl.semaphore_wait(free, len(neighbours))
    b = cp.send(sent, got, place.to_core())
    yield
    cp.arrived(b)
    add_into(got, [got, kept])
    cp.sent_off(b)
    summed = sum_ring_pair if ring_first else sum_pair_ring
    yield from summed(cp, grid, got, got, bufs, total)
    if not again:
        for device in neighbours:
            pl.semaphore_signal(free, inc=1, device_id=device, device_id_type=MESH)
    yield from gather_expert(cp, place, grid, total, at, z_first)


def dense_stream(cp, place, grid, grad, got, bufs, total, ring_first):
    b = cp.send(grad.at[:, :, 1 - place.core], got, place.to_core())
    yield
    cp.arrived(b)
    own = grad.at[:, :, place.core]
    add_into(got, [got, own])
    summed = sum_ring_pair if ring_first else sum_pair_ring
    yield from summed(cp, grid, got, got, bufs, total)


def spread_stream(cp, place, stream, total, padded, result):
    yield from stream
    used = total.shape[0] // 8
    spread = spread_matrix(8 * used, 8, used).astype(BF)
    columns = total.shape[1]
    for c in range(0, columns, 128):
        padded[:, :, c : c + 128] = (
            dot_tn(spread, total[:, c : c + 128]).astype(BF).reshape(8, ROW_PAD, 128)
        )
    cp.local(padded.at[place.ep], result.at[place.ep])
    for k in range(1, 8):
        cp.send(padded.at[(place.ep + k) % 8], result.at[place.ep], place.to_ep(k))


def advance(*streams):
    for stream in streams:
        next(stream, None)


BLOCK = 256


def turn(values, cosine, sine):
    return values * cosine + pltpu.roll(values, HD // 2, 1) * sine


def attention_head(h, qkv, live, probs, heads):
    group = qkv.shape[0]
    span = HEADS_DEV * HD
    per = BLOCK // heads.shape[1]
    rows = lax.broadcasted_iota(jnp.int32, (BLOCK, BLOCK), 0)
    columns = lax.broadcasted_iota(jnp.int32, (BLOCK, BLOCK), 1)
    q, k, v = (slice(n * span + h * HD, n * span + (h + 1) * HD) for n in range(3))
    for i in range(group // BLOCK):
        at = slice(i * BLOCK, (i + 1) * BLOCK)
        n = (i + 1) * BLOCK
        scores = dot_nt(qkv[at, q], qkv[:n, k]) * HD**-0.5
        parts = []
        for j in range(i + 1):
            alive = live[LIVE : LIVE + 1, j * BLOCK : (j + 1) * BLOCK] > 0.5
            if j == i:
                alive = (alive & (columns < rows)) | (columns == rows)
            parts.append(jnp.where(alive, scores[:, j * BLOCK : (j + 1) * BLOCK], -1e30))
        scores = jnp.concatenate(parts, axis=1) if len(parts) > 1 else parts[0]
        top = jnp.max(scores, axis=1, keepdims=True)
        weights = jnp.exp(scores - top)
        low = (weights * (1.0 / jnp.sum(weights, axis=1, keepdims=True))).astype(BF)
        probs[h, at, :n] = low
        heads[i * per : (i + 1) * per, :, h * HD : (h + 1) * HD] = (
            dot(low, qkv[:n, v]).astype(BF).reshape(per, BLOCK // per, HD)
        )


def attention_back_head(h, g_heads, qkv, probs, cosine, sine, g_keys, g_values, g_qkv):
    group = qkv.shape[0]
    blocks, rows = g_heads.shape[:2]
    per = BLOCK // rows
    span = HEADS_DEV * HD
    scale = HD**-0.5
    q, k, v = (slice(n * span + h * HD, n * span + (h + 1) * HD) for n in range(3))
    head = slice(h * HD, (h + 1) * HD)
    for i in reversed(range(group // BLOCK)):
        at = slice(i * BLOCK, (i + 1) * BLOCK)
        n = (i + 1) * BLOCK
        g_att = g_heads[i * per : (i + 1) * per, :, head].reshape(BLOCK, HD)
        low = probs[h, at, :n]
        weights = low.astype(F32)
        g_probs = dot_nt(g_att, qkv[:n, v])
        delta = jnp.sum(weights * g_probs, axis=1, keepdims=True)
        g_scores = (weights * (g_probs - delta)).astype(BF)
        g_query = dot(g_scores, qkv[:n, k]) * scale
        g_qkv[at, q] = turn(g_query, cosine[at, :], -sine[at, :]).astype(BF)
        g_key = dot_tn(g_scores, qkv[at, q])
        g_value = dot_tn(low, g_att)
        if i == group // BLOCK - 1:
            g_keys[...] = g_key
            g_values[...] = g_value
        else:
            g_keys[:n, :] += g_key
            g_values[:n, :] += g_value
    g_qkv[:, k] = turn(g_keys[...] * scale, cosine[...], -sine[...]).astype(BF)
    g_qkv[:, v] = g_values[...].astype(BF)


def store_rows(ref, lead, columns, row, value):
    depth = ref.shape[len(lead)]
    done = 0
    while done < value.shape[0]:
        block, offset = divmod(row + done, depth)
        take = min(depth - offset, value.shape[0] - done)
        at = tuple(int(i) for i in np.unravel_index(block, lead))
        ref[at + (slice(offset, offset + take), columns)] = value[done : done + take]
        done += take


def one_expert(
    loop, blocks, x, g, w_gate, w_up, w_down, weight, wact, g_a, g_b, outs, grads, before, q_sum, first
):
    width = g.shape[2]

    @pl.loop(*loop)
    def _(i):
        pair = blocks(i)

        def load(ref):
            return jnp.concatenate([ref[b] for b in pair], axis=0)

        def store(ref, value):
            for n, b in enumerate(pair):
                ref[b] = value[n * (BLOCK // 2) : (n + 1) * (BLOCK // 2)]

        if before is not None:
            before(pair, load, store)
        share = weight(load)
        rows = load(x)
        gate = dot(rows, w_gate[...])
        up = dot(rows, w_up[...])
        raw = dot_nt(load(g), w_down[...])
        sig = 1.0 / (1.0 + jnp.exp(-gate))
        silu = gate * sig
        act = silu * up
        if q_sum is not None:
            q_sum(pair, load, jnp.sum(act * raw, axis=1, keepdims=True))
        low = (act * share).astype(BF)
        store(wact, low)
        raw = raw * share
        a = (raw * up * (sig + silu * (1.0 - sig))).astype(BF)
        b = (raw * silu).astype(BF)
        store(g_a, a)
        store(g_b, b)
        part = dot(low, w_down[...])
        back = dot_nt(a, w_gate[...]) + dot_nt(b, w_up[...])
        for n, k in enumerate(pair):
            at = slice(n * (BLOCK // 2), (n + 1) * (BLOCK // 2))
            more, behind = part[at], back[at]
            if not first:
                more += outs[k // 2, k % 2].astype(F32)
                behind += grads[k // 2, k % 2, :, :width].astype(F32)
            outs[k // 2, k % 2] = more.astype(BF)
            grads[k // 2, k % 2, :, :width] = behind.astype(BF)


ORDER_A = (
    "A", "A", "p0", "A", "p1", "A", "p2", "p3", "w1", "pr", "g0", "u0", "d0", "G0",
    "sp", "G0", "U0", "D0", "q1", "G0", "U0", "r1", "G0", "U0", "D0", "x", "g1", "G0",
    "G0", "X0", "D0", "U0", "u1", "G1", "G0", "G0", "D0", "X1", "d1", "U1", "G1", "U0",
    "U0", "D0", "ss", "X0", "D1",
)
ORDER_B = (
    "G0", "G0", "X1", "D0", "X0", "U1", "X1", "n2", "G1", "U0", "dw", "U0", "sn", "D0",
    "o", "G1", "D1", "G1", "W", "h0", "O", "S", "N", "U1", "U0", "U0", "D0", "D0",
    "D0", "h1", "O", "S", "G1", "G1", "D1", "N", "hp", "W", "S", "G1", "dq", "N",
    "G1", "G1", "U1", "H0", "W", "Q", "O", "H1", "D1", "W", "S", "N", "Q", "U1",
    "U1", "H0", "D1", "D1", "H1", "Q", "H0", "U1", "H1", "n1", "U1", "Q", "D1", "D1",
    "U1", "U1", "D1", "D1",
)
Y_FIRST = ()


def kernel_rest(
    experts, top,
    x_own, g_all, e_gate, e_up, e_down, h_probs, h_hidden, h_qkv, w_slices, h_whole,
    h_residual, h_cot, h_tok, h_attended, h_cosine, h_sine,
    h_extra, h_router, h_both, h_padded, live, gains,
    out, d_tok, x_gate, x_up, x_down, o_qkv, o_shared, o_whole, o_down,
    x, m_grads, m_outs, b_grads, b_outs, total_grads, total_hidden, e_got, e_bufs, e_total,
    v_shared, v_down, got, bufs, g_heads, probs, free, send_sem, recv_sem,
):
    place = Place()
    cp = Copies(send_sem, recv_sem)
    rows, width = x_own.shape
    group = 8 * rows
    mine, core = place.ep, place.core
    ge, gr = grid_ep(place), grid_rep(place)
    wide = width + EXTRA
    exp_dev, _, hidden = e_gate.shape
    span = HEADS_DEV * HD
    cut = wide // 2 // 128 * 128
    cuts = (pl.ds(0, cut), pl.ds(cut, wide - cut))
    m_grads, m_outs, total_grads, total_hidden, x_gate, x_up, x_down = (
        Later(ref) for ref in (m_grads, m_outs, total_grads, total_hidden, x_gate, x_up, x_down)
    )
    later = lambda refs: [Later(ref) if hasattr(ref, "at") else later(ref) for ref in refs]
    b_grads, b_outs, e_got, e_bufs, e_total = (
        later(refs) for refs in (b_grads, b_outs, e_got, e_bufs, e_total)
    )
    half_part = width // 16
    half = width // 2
    ours = pl.ds(pl.multiple_of(core * half, 128), half)
    theirs = pl.ds(pl.multiple_of(place.mate * half, 128), half)
    streams = {}
    from_x, from_z = place.from_x, place.from_z

    def view(ref, c):
        return ref.at[:, :, :, c]

    def phase_a(
        g, extra, w_router, s_both, s_padded, w_gate, w_up, w_down, wact, g_a, g_b, gates, named,
        swact, sg_a, sg_b, s_down, d_sdown, d_gate, d_up, d_down,
    ):
        first = [cp.local(h_extra, extra), cp.local(h_router, w_router), cp.local(g_all, g)]
        small = [cp.local(h_both, s_both), cp.local(h_padded, s_padded)]
        weights = ((e_gate, w_gate), (e_up, w_up), (e_down, w_down))
        loads = [cp.local(a.at[0], b) for a, b in weights]
        greet(ep_peers(place) + rep_peers(place))
        streams["A"] = gather_ep(cp, place, x_own, Later(x), width)
        next(streams["A"])
        for copy in first:
            cp.arrived(copy)
        lane = lax.broadcasted_iota(jnp.int32, (BLOCK, EXTRA), 1)

        def router(values, lanes):
            logits = jnp.where(lanes < experts, dot(values, w_router[...]), -1e30)
            weights = jnp.exp(logits - jnp.max(logits, axis=1, keepdims=True))
            return weights / jnp.sum(weights, axis=1, keepdims=True)

        def route(pair, load, store):
            prob = router(load(x), lane)
            routes = load(extra)
            whole = routes.astype(F32).astype(jnp.int32)
            chosen = lane == whole[:, 0:1]
            for j in range(1, top):
                chosen = chosen | (lane == whole[:, j : j + 1])
            store(named, jnp.where(chosen, 1.0, 0.0))
            store(gates, jnp.where(chosen, prob, 0.0) * routes[:, top : top + 1].astype(F32))
            for b in pair:
                m_grads[b // 2, b % 2, :, width:] = jnp.zeros((BLOCK // 2, EXTRA), BF)

        shared = s_down.shape[0]
        used = s_padded.shape[0] // ROW_PAD * 7 // 16
        steps = group // BLOCK
        in_turn = lambda i: (2 * i, 2 * i + 1)
        flat = lambda ref: ref[...].reshape(group, ref.shape[2])
        columns_of = lambda ref, c: ref[:, :, c : c + BLOCK].reshape(group, BLOCK)
        arrivals = (
            (place.ep, from_x[-1]), (from_x[1], from_z[0]), (from_x[2], from_z[-1]), (from_z[1], from_z[2]),
        )

        def shared_pass():
            for copy in small:
                cp.arrived(copy)
            pack = spread_matrix(shared, 16, used).astype(BF)
            s_down[...] = dot(pack, s_padded[...]).astype(BF)
            one_expert(
                (0, steps), in_turn, x, g, s_both.at[:, :shared], s_both.at[:, shared:], s_down,
                lambda load: load(extra)[:, top : top + 1].astype(F32),
                swact, sg_a, sg_b, m_outs, m_grads, None, None, False,
            )

        def shared_sums():
            for c in range(0, width, BLOCK):
                left = columns_of(x, c)
                for n, back in enumerate((sg_a, sg_b)):
                    store_rows(
                        v_shared, (4, 2, 2), slice(n * shared, (n + 1) * shared), c,
                        dot_tn(left, flat(back)).astype(BF),
                    )
            d_sdown[...] = dot_tn(flat(swact), flat(g)).astype(BF)
            pack = spread_matrix(shared, 16, used).astype(BF)
            for c in range(0, s_padded.shape[0], BLOCK):
                store_rows(
                    v_down, (4, 2, 2), slice(0, width), c,
                    dot_tn(pack[:, c : c + BLOCK], d_sdown[...]).astype(BF),
                )

        def expert_pass(e, loop, blocks):
            expert = mine * exp_dev + e

            def picked(load):
                return jnp.sum(jnp.where(lane == expert, load(gates), 0.0), axis=1, keepdims=True)

            def q_sum(pair, load, value):
                value = value * load(named)
                for n, b in enumerate(pair):
                    at = slice(n * (BLOCK // 2), (n + 1) * (BLOCK // 2))
                    old = m_grads[b // 2, b % 2, :, width:].astype(F32)
                    new = jnp.where(lane[: BLOCK // 2] == expert, value[at], old)
                    m_grads[b // 2, b % 2, :, width:] = new.astype(BF)

            for copy in loads:
                cp.arrived(copy)
            loads.clear()
            one_expert(
                loop, blocks, x, g, w_gate, w_up, w_down, picked,
                wact, g_a, g_b, m_outs, m_grads, route if e == 0 else None, q_sum, e == 0,
            )

        def next_weights(e):
            loads.extend(cp.local(a.at[e], b) for a, b in weights)

        def stream(e, n, sent, kept, at, ring_first):
            streams["GUD"[n] + str(e)] = one = expert_stream(
                cp, place, gr, sent, kept, e_got[n], e_bufs[n], e_total[e][n], at, ring_first,
                (e, n) not in Y_FIRST, free.at[n], e > 0,
            )
            next(one)

        def expert_sums(e, n):
            if n < 2:
                d, back, x_out = ((d_gate, g_a, x_gate), (d_up, g_b, x_up))[n]
                for c in range(0, width, BLOCK):
                    store_rows(
                        d, (2, 4, 2), slice(0, hidden), c, dot_tn(columns_of(x, c), flat(back)).astype(BF)
                    )
                stream(
                    e, n, d.at[place.mate], d.at[core],
                    lambda k, z: x_out.at[e, core, place.y_at[k], z], True,
                )
            else:
                for c in range(0, hidden, 128):
                    left = wact[:, :, c : c + 128].reshape(group, 128)
                    store_rows(d_down, (4, 2), slice(0, width), c, dot_tn(left, flat(g)).astype(BF))
                stream(
                    e, n, d_down.at[:, :, :, theirs], d_down.at[:, :, :, ours],
                    lambda k, z: x_down.at[e, place.y_at[k], z, :, ours], True,
                )

        def own_probs():
            probs[...] = router(x[mine], lane[:rows])

        def start_x():
            for n, (c, b) in enumerate(zip(cuts, b_grads)):
                streams["X" + str(n)] = one = sum_ring_pair(
                    cp, ge, view(m_grads, c), view(m_grads, c), b, total_grads.at[:, c]
                )
                next(one)

        pieces = {"sp": shared_pass, "ss": shared_sums, "x": start_x, "w1": functools.partial(next_weights, 1)}
        for n, pair in enumerate(arrivals):
            pieces["p" + str(n)] = functools.partial(expert_pass, 0, (0, 1), lambda i, pair=pair: pair)
        pieces["q1"] = functools.partial(expert_pass, 1, (0, steps // 2), in_turn)
        pieces["r1"] = functools.partial(expert_pass, 1, (steps // 2, steps), in_turn)
        pieces["pr"] = own_probs
        for e in range(exp_dev):
            for n in range(3):
                pieces["gud"[n] + str(e)] = functools.partial(expert_sums, e, n)
        follow(ORDER_A, pieces)

    def follow(order, pieces):
        for name in order:
            if name in pieces:
                pieces[name]()
            else:
                next(streams[name], None)

    pl.run_scoped(
        phase_a,
        pltpu.VMEM((8, rows, width), BF),
        pltpu.VMEM(h_extra.shape, BF),
        pltpu.VMEM(h_router.shape, BF),
        pltpu.VMEM(h_both.shape, BF),
        pltpu.VMEM(h_padded.shape, BF),
        pltpu.VMEM((width, hidden), BF),
        pltpu.VMEM((width, hidden), BF),
        pltpu.VMEM((hidden, width), BF),
        *[pltpu.VMEM((8, rows, hidden), BF)] * 3,
        *[pltpu.VMEM((8, rows, EXTRA), F32)] * 2,
        *[pltpu.VMEM((8, rows, h_both.shape[1] // 2), BF)] * 3,
        *[pltpu.VMEM((h_both.shape[1] // 2, width), BF)] * 2,
        pltpu.VMEM((2, 4, 2, half_part, hidden), BF),
        pltpu.VMEM((2, 4, 2, half_part, hidden), BF),
        pltpu.VMEM((4, 2, hidden // 8, width), BF),
    )

    def phase_b(
        v_probs, v_qkvs, v_w, w_whole, residual, cot, tok, attended, cosine, sine,
        v_whole, v_qkv, totals, padded, g_att, g_residual, g_keys, g_values, g_qkv, g_branch,
    ):
        loads = [
            cp.local(a, b)
            for a, b in (
                (h_residual, residual), (h_cot, cot), (h_whole, w_whole), (h_attended, attended),
                (h_qkv, v_qkvs), (h_probs, v_probs), (h_cosine, cosine), (h_sine, sine),
                (w_slices.at[:, : v_w.shape[1]], v_w), (h_hidden, x), (h_tok, tok),
            )
        ]
        alive = live[...]
        kept = {}

        step = 256

        def second_norm():
            for copy in loads:
                cp.arrived(copy)
            router_grad = total_grads[:, width:] * alive
            prob = probs[...]
            logit_grad = prob * (router_grad - jnp.sum(prob * router_grad, axis=1, keepdims=True))
            squares = jnp.zeros((rows, 1), F32)
            mean_k = jnp.zeros((rows, 1), F32)
            for c in range(0, width, step):
                part = residual[:, c : c + step]
                squares += jnp.sum(part * part, axis=1, keepdims=True)
            scale = lax.rsqrt(squares / width + EPS)
            gain_rows = []
            for c in range(0, width, step):
                k = total_grads[:, c : c + step] + lax.dot_general(
                    logit_grad, w_whole[c : c + step, width:].astype(F32), (((1,), (1,)), ((), ())),
                    preferred_element_type=F32, precision=HIGH,
                )
                normed = residual[:, c : c + step] * scale
                gain_rows.append(jnp.sum(k * normed, axis=0, keepdims=True))
                k = k * gains[1:2, c : c + step]
                mean_k += jnp.sum(k * normed, axis=1, keepdims=True)
                g_residual[:, c : c + step] = k
            mean_k = mean_k / width
            for c in range(0, width, step):
                normed = residual[:, c : c + step] * scale
                grad = cot[:, c : c + step].astype(F32) + scale * (
                    g_residual[:, c : c + step] - normed * mean_k
                )
                g_residual[:, c : c + step] = grad
                g_branch[:, c : c + step] = (alive * grad).astype(BF)
            for c in range(0, width, step):
                g_att[c // step] = dot_nt(g_branch[...], w_whole[c : c + step, :width]).astype(BF)
            for c in range(width // step, 8):
                g_att[c] = jnp.zeros((rows, span), BF)
            kept["third"] = [cp.local(g_att.at[mine], g_heads.at[mine])] + [
                cp.send(g_att.at[(mine + k) % 8], g_heads.at[mine], place.to_ep(k)) for k in range(1, 8)
            ]
            kept["norm"] = logit_grad, scale, gain_rows

        def whole_sums():
            logit_grad, scale, gain_rows = kept["norm"]
            for i in range(2):
                c = slice(i * width // 2, (i + 1) * width // 2)
                v_whole[2 * i : 2 * i + 2, :, :, :, :width] = (
                    dot_tn(attended[:, c], g_branch[...]).astype(BF).reshape(2, 2, 2, width // 16, width)
                )
                hid = (residual[:, c] * scale * gains[1:2, c]).astype(BF).astype(F32)
                small = lax.dot_general(
                    hid, logit_grad, (((0,), (0,)), ((), ())), preferred_element_type=F32, precision=HIGH
                )
                gain_row = jnp.concatenate(gain_rows, axis=1)[:, c]
                lane = lax.broadcasted_iota(jnp.int32, (width // 2, EXTRA), 1)
                column = jnp.broadcast_to(gain_row, (8, width // 2)).T[:, :1]
                small = jnp.where(lane == EXTRA - 1, column, small)
                v_whole[2 * i : 2 * i + 2, :, :, :, width:] = small.astype(BF).reshape(
                    2, 2, 2, width // 16, EXTRA
                )
            dense("W", 0, v_whole, False, 0, o_whole)

        def dense(name, i, v, ring_first, spread, result):
            one = dense_stream(cp, place, gr, v, got[i], bufs[i], totals[i], ring_first)
            if spread is not None:
                one = spread_stream(cp, place, one, totals[i], padded[spread], result)
            streams[name] = one
            next(one)

        def small_dense():
            dense("S", 1, v_shared, True, 1, o_shared)
            dense("N", 2, v_down, True, None, None)

        def start_out():
            streams["O"] = sum_ring_pair(cp, ge, m_outs, m_outs, b_outs, out, (residual,))
            next(streams["O"])

        def head(h):
            if h == 0:
                for copy in kept["third"]:
                    cp.arrived(copy)
            attention_back_head(h, g_heads, v_qkvs, v_probs, cosine, sine, g_keys, g_values, g_qkv)

        def hidden_part():
            @pl.loop(0, group // BLOCK)
            def _(i):
                at = pl.ds(pl.multiple_of(i * BLOCK, BLOCK), BLOCK)
                part = dot_nt(g_qkv[at, :], v_w[...]).astype(BF)
                m_grads[i, :, :, :width] = part.reshape(2, rows, width)

            hcuts = (pl.ds(0, half), pl.ds(half, width - half))
            for n, ((b,), c) in enumerate(zip(b_grads, hcuts)):
                streams["H" + str(n)] = one = sum_ring_pair(
                    cp, ge, view(m_grads, c), view(m_grads, c), [b.at[:, :, pl.ds(0, c.size)]],
                    total_hidden.at[:, c],
                )
                next(one)

        def qkv_sums():
            for i in range(2):
                c = slice(i * width // 2, (i + 1) * width // 2)
                v_qkv[2 * i : 2 * i + 2] = (
                    dot_tn(x[:, :, c].reshape(group, width // 2), g_qkv[...]).astype(BF).reshape(2, 2, 2, width // 16, 3 * span)
                )
            dense("Q", 3, v_qkv, True, 2, o_qkv)

        def first_norm():
            squares = jnp.zeros((rows, 1), F32)
            mean_k = jnp.zeros((rows, 1), F32)
            for c in range(0, width, step):
                part = tok[:, c : c + step].astype(F32)
                squares += jnp.sum(part * part, axis=1, keepdims=True)
            scale = lax.rsqrt(squares / width + EPS)
            for c in range(0, width, step):
                normed = tok[:, c : c + step].astype(F32) * scale
                k = total_hidden[:, c : c + step] * gains[0:1, c : c + step]
                mean_k += jnp.sum(k * normed, axis=1, keepdims=True)
            mean_k = mean_k / width
            for c in range(0, width, step):
                normed = tok[:, c : c + step].astype(F32) * scale
                k = total_hidden[:, c : c + step] * gains[0:1, c : c + step]
                d_tok[:, c : c + step] = g_residual[:, c : c + step] + scale * (k - normed * mean_k)

        follow(
            ORDER_B,
            {
                "n2": second_norm, "dw": whole_sums, "sn": small_dense, "o": start_out,
                "h0": functools.partial(head, 0), "h1": functools.partial(head, 1),
                "hp": hidden_part, "dq": qkv_sums, "n1": first_norm,
            },
        )
        run_streams(*streams.values())
        o_down[...] = totals[2][...]
        cp.finish()

    columns = (wide, h_both.shape[1], width, 3 * span)
    depth = (half_part, half_part, ROW_PAD, half_part)
    pl.run_scoped(
        phase_b,
        pltpu.VMEM(h_probs.shape, BF),
        pltpu.VMEM(h_qkv.shape, BF),
        pltpu.VMEM((width, 3 * span), BF),
        pltpu.VMEM(h_whole.shape, BF),
        pltpu.VMEM((rows, width), F32),
        *[pltpu.VMEM((rows, width), BF)] * 3,
        *[pltpu.VMEM((group, HD), F32)] * 2,
        pltpu.VMEM((4, 2, 2, half_part, wide), BF),
        pltpu.VMEM((4, 2, 2, half_part, 3 * span), BF),
        [pltpu.VMEM((r, c), BF) for r, c in zip(depth, columns)],
        [pltpu.VMEM((8, ROW_PAD, columns[i]), BF) for i in (0, 1, 3)],
        pltpu.VMEM((8, rows, span), BF),
        pltpu.VMEM((rows, width), F32),
        *[pltpu.VMEM((group, HD), F32)] * 2,
        pltpu.VMEM((group, 3 * span), BF),
        pltpu.VMEM((rows, width), BF),
    )


def call_rest(
    experts, top, x_own, g_all, e_gate, e_up, e_down, h_probs, h_hidden, h_qkv, w_slices, h_whole,
    h_residual, h_cot, h_tok, h_attended, h_cosine, h_sine,
    extra, w_router, s_both, s_padded, live, gains,
):
    anyspace = pl.BlockSpec(memory_space=pl.ANY)
    vmem = pl.BlockSpec(memory_space=pltpu.VMEM)
    rows, width = h_cot.shape
    span = HEADS_DEV * HD
    wide = width + EXTRA
    cut = wide // 2 // 128 * 128
    exp_dev, _, hidden = e_gate.shape
    part = width // 16
    columns = (wide, s_both.shape[1], width, 3 * span)
    depth = (part, part, ROW_PAD, part)
    orders = (False, True, True, True)
    halves = ((part, hidden), (part, hidden), (hidden // 8, width // 2))
    bufs_of = lambda first, r, c: (ring_pair_bufs if first else pair_ring_bufs)(r, c)
    shape = jax.ShapeDtypeStruct
    return pl.pallas_call(
        functools.partial(kernel_rest, experts, top),
        out_shape=(
            shape((rows, width), BF),
            shape((rows, width), F32),
            shape((exp_dev, 2, 4, 2, part, hidden), BF),
            shape((exp_dev, 2, 4, 2, part, hidden), BF),
            shape((exp_dev, 4, 2, hidden // 8, width), BF),
            shape((8, ROW_PAD, 3 * span), BF),
            shape((8, ROW_PAD, columns[1]), BF),
            shape((8, ROW_PAD, wide), BF),
            shape((ROW_PAD, width), BF),
        ),
        in_specs=[anyspace] * 20 + [vmem] * 2,
        out_specs=(vmem, vmem) + (anyspace,) * 6 + (vmem,),
        scratch_shapes=[
            pltpu.VMEM((8, rows, width), BF),
            pltpu.VMEM((4, 2, rows, wide), BF),
            pltpu.VMEM((4, 2, rows, width), BF),
            [ring_pair_bufs(rows, c) for c in (cut, wide - cut)],
            ring_pair_bufs(rows, width),
            pltpu.VMEM((rows, wide), F32),
            pltpu.VMEM((rows, width), F32),
            [pltpu.VMEM((4, 2) + h, BF) for h in halves],
            [ring_pair_bufs(*h) for h in halves],
            [[pltpu.VMEM(h, BF) for h in halves] for _ in range(exp_dev)],
            pltpu.VMEM((4, 2, 2, part, columns[1]), BF),
            pltpu.VMEM((4, 2, 2, ROW_PAD, width), BF),
            [pltpu.VMEM((4, 2, r, c), BF) for r, c in zip(depth, columns)],
            [bufs_of(first, r, c) for first, r, c in zip(orders, depth, columns)],
            pltpu.VMEM((8, rows, span), BF),
            pltpu.VMEM((rows, EXTRA), F32),
            pltpu.SemaphoreType.REGULAR((3,)),
            pltpu.SemaphoreType.DMA((440,)),
            pltpu.SemaphoreType.DMA((440,)),
        ],
        compiler_params=pltpu.CompilerParams(
            collective_id=2, has_side_effects=True, vmem_limit_bytes=int(63.9 * 2**20)
        ),
        name="rest",
    )(
        x_own, g_all, e_gate, e_up, e_down, h_probs, h_hidden, h_qkv, w_slices, h_whole,
        h_residual, h_cot, h_tok, h_attended, h_cosine, h_sine,
        extra, w_router, s_both, s_padded, live, gains,
    )


def kernel_finish(
    o_qkv, o_shared, o_whole, o_down, w_query, w_key, w_value, norm_attn, b_gate, b_up, b_down,
    d_query, d_key, d_value, d_output, d_router, d_sgate, d_sup, d_sdown, d_norm_one, d_norm_two,
    d_gate, d_up, d_down,
):
    used, width = w_query.shape
    hidden = d_sgate.shape[1]
    span = HEADS_DEV * HD
    for low, full in ((b_gate, d_gate), (b_up, d_up), (b_down, d_down)):
        full[...] = low[...].astype(F32)

    step = pl.program_id(0)

    @pl.when(step == 1)
    def _():
        gain = jnp.zeros((used, 1), F32)
        for n, (w, d) in enumerate(((w_query, d_query), (w_key, d_key), (w_value, d_value))):
            for owner in range(width // span):
                c = slice(owner * span, (owner + 1) * span)
                part = o_qkv[owner, :used, n * span : (n + 1) * span].astype(F32)
                d[:, c] = part
                gain += jnp.sum(part * w[:, c].astype(F32), axis=1, keepdims=True)
        d_norm_one[...] = as_row(gain) / norm_attn[...].astype(F32)

    @pl.when(step == 2)
    def _():
        for n, d in enumerate((d_sgate, d_sup)):
            total = jnp.zeros((ROW_PAD, hidden), F32)
            for owner in range(8):
                pick = shared_columns(owner, hidden, d_sdown.shape[0])
                total += dot_nt(o_shared[owner, :, n * 128 : (n + 1) * 128], pick)
            d[...] = total[:used]

    @pl.when(step == 3)
    def _():
        total = o_whole[0].astype(F32)
        for i in range(1, 8):
            total += o_whole[i].astype(F32)
        d_output[...] = total[:used, :width]
        d_router[...] = total[:used, width : width + d_router.shape[1]]
        d_norm_two[...] = as_row(total[:used, width + EXTRA - 1 :])
        d_sdown[...] = o_down[: d_sdown.shape[0]].astype(F32)


def call_finish(
    o_qkv, o_shared, o_whole, o_down, w_query, w_key, w_value, norm_attn, b_gate, b_up, b_down,
    experts, hidden,
):
    used, width = w_query.shape
    down_used = hidden // 128
    shape = jax.ShapeDtypeStruct
    steps = 4
    fixed = lambda a: pl.BlockSpec(a.shape, lambda i: (0,) * len(a.shape))
    part = lambda a: pl.BlockSpec((a.shape[0] // steps, a.shape[1]), lambda i: (i, 0))
    small = (
        [shape((used, width), F32)] * 4
        + [shape((used, experts), F32)]
        + [shape((used, hidden), F32)] * 2
        + [shape((down_used, width), F32)]
        + [shape((1, used), F32)] * 2
    )
    large = [shape(a.shape, F32) for a in (b_gate, b_up, b_down)]
    operands = (o_qkv, o_shared, o_whole, o_down, w_query, w_key, w_value, norm_attn)
    return pl.pallas_call(
        kernel_finish,
        grid=(steps,),
        out_shape=tuple(small + large),
        in_specs=[fixed(a) for a in operands] + [part(a) for a in (b_gate, b_up, b_down)],
        out_specs=tuple([fixed(a) for a in small] + [part(a) for a in large]),
        compiler_params=pltpu.CompilerParams(
            vmem_limit_bytes=VMEM_LIMIT, dimension_semantics=("arbitrary",)
        ),
        name="finish",
    )(*operands, b_gate, b_up, b_down)


def body(
    tokens, cotangent, lengths, token_mask, routes,
    w_query, w_key, w_value, w_output, w_router,
    shared_gate, shared_up, shared_down, norm_attn, norm_ffn,
    expert_gate, expert_up, expert_down,
):
    rows, width = tokens.shape
    used = w_query.shape[0]
    exp_dev, _, hidden = expert_gate.shape
    experts = w_router.shape[1]
    group = rows * 8
    frequency = 10000.0 ** (-(np.arange(HD // 2, dtype=np.float32) * np.float32(2.0) / HD))
    angles = np.arange(group, dtype=np.float32)[:, None] * frequency.astype(np.float32)[None, :]
    cosine = jnp.asarray(np.tile(np.cos(angles), (1, 2)), F32)
    sine = jnp.asarray(np.concatenate([-np.sin(angles), np.sin(angles)], axis=1), F32)
    (
        w_slices, w_both, w_whole, w_router_all, w_down, cot_all, extra,
        hidden_one, qkv, attn_probs, gain_rows, residual, attended, hidden_two, live,
    ) = call_front(
        tokens, cotangent, lengths[None], token_mask[None], routes.T,
        w_query, w_key, w_value, w_output, w_router,
        shared_gate, shared_up, shared_down, norm_attn[None], norm_ffn[None], cosine, sine,
    )
    out, d_tokens, e_gate, e_up, e_down, o_qkv, o_shared, o_whole, o_down = call_rest(
        experts, routes.shape[1],
        hidden_two, cot_all, expert_gate, expert_up, expert_down,
        attn_probs, hidden_one.reshape(8, rows, width), qkv,
        w_slices.reshape(width, -1), w_whole.reshape(width, -1),
        residual, cotangent, tokens, attended, cosine, sine,
        extra, w_router_all.reshape(width, EXTRA),
        w_both.reshape(width, -1), w_down.reshape(-1, width), live, gain_rows,
    )
    (
        d_query, d_key, d_value, d_output, d_router, d_sgate, d_sup, d_sdown, d_norm_one, d_norm_two,
        d_gate, d_up, d_down,
    ) = call_finish(
        o_qkv, o_shared, o_whole, o_down, w_query, w_key, w_value, norm_attn[None],
        e_gate.reshape(-1, hidden), e_up.reshape(-1, hidden), e_down.reshape(-1, width),
        experts, hidden,
    )
    return (
        out, d_tokens, d_query, d_key, d_value, d_output, d_router, d_sgate, d_sup, d_sdown,
        d_norm_one.reshape(used), d_norm_two.reshape(used),
        d_gate.reshape(exp_dev, width, hidden), d_up.reshape(exp_dev, width, hidden),
        d_down.reshape(exp_dev, hidden, width),
    )


def solution(mesh):
    both = ("rep", "ep")
    row = P(both, None)
    expert = P("ep", None, None)
    in_specs = (
        row, row, P("rep"), P(both), row, row, row, row, row, row, row, row, row,
        P(both), P(both), expert, expert, expert,
    )
    out_specs = (
        row, row, row, row, row, row, row, row, row, row, P(both), P(both),
        expert, expert, expert,
    )
    return jax.shard_map(body, mesh=mesh, in_specs=in_specs, out_specs=out_specs, check_vma=False)
```

```python
import functools
import itertools
import math

import jax
import jax.numpy as jnp
import numpy as np
from jax import lax
from jax.experimental import pallas as pl
from jax.experimental.pallas import tpu as pltpu
from jax.sharding import PartitionSpec as P

HD = 128
EPS = 1e-6
BF = jnp.bfloat16
F32 = jnp.float32
MESH = pl.DeviceIdType.MESH
HIGH = lax.Precision.HIGHEST
HEADS_DEV = 2
EXTRA = 128
ROW_PAD = 16
VMEM_LIMIT = 60 << 20
LIVE = 7


def dot(a, b):
    return jnp.dot(a, b, preferred_element_type=F32)


def dot_nt(a, b):
    return lax.dot_general(a, b, (((1,), (1,)), ((), ())), preferred_element_type=F32)


def dot_tn(a, b):
    return lax.dot_general(a, b, (((0,), (0,)), ((), ())), preferred_element_type=F32)


class Place:
    def __init__(self):
        self.rep = lax.axis_index("rep")
        self.ep = lax.axis_index("ep")
        self.y = self.rep // 4
        self.zl = (self.rep // 2) % 2
        self.core = self.rep % 2
        self.x = self.ep // 2
        self.zh = self.ep % 2

        self.mate = 1 - self.core
        self.y_at = {k: (self.y + k) % 4 for k in (-1, 0, 1, 2)}
        self.from_x = {k: self.ep_at(self.x + k, self.zh) for k in (-1, 1, 2)}
        self.from_z = {k: self.ep_at(self.x + k, 1 - self.zh) for k in (-1, 0, 1, 2)}
        self._x = {k: (self.rep, self.ep_at(self.x + k, self.zh)) for k in (-1, 1)}
        self._y = {k: (self.rep_at(self.y + k, self.zl, self.core), self.ep) for k in (-1, 1)}
        self._ep = {k: (self.rep, (self.ep + k) % 8) for k in range(1, 8)}
        self._zh = (self.rep, self.ep_at(self.x, 1 - self.zh))
        self._zl = (self.rep_at(self.y, 1 - self.zl, self.core), self.ep)
        self._core = (self.rep_at(self.y, self.zl, self.mate), self.ep)

    def rep_at(self, y, zl, core):
        return (y % 4) * 4 + zl * 2 + core

    def ep_at(self, x, zh):
        return (x % 4) * 2 + zh

    def to_x(self, step):
        return self._x[step]

    def to_zh(self):
        return self._zh

    def to_ep(self, shift):
        return self._ep[shift]

    def to_y(self, step):
        return self._y[step]

    def to_zl(self):
        return self._zl

    def to_core(self):
        return self._core


class Later:
    def __init__(self, ref, path=()):
        self.ref, self.path = ref, path

    @property
    def at(self):
        return LaterAt(self)

    @property
    def shape(self):
        return self.made().shape

    @property
    def dtype(self):
        return self.ref.dtype

    def made(self):
        ref = self.ref
        for index in self.path:
            ref = ref.at[index]
        return ref

    def __getitem__(self, index):
        return self.made()[index]

    def __setitem__(self, index, value):
        self.made()[index] = value


class LaterAt:
    def __init__(self, later):
        self.later = later

    def __getitem__(self, index):
        return Later(self.later.ref, self.later.path + (index,))


def made(ref):
    return ref.made() if isinstance(ref, Later) else ref


class Copies:
    def __init__(self, send_sem, recv_sem):
        self.send_sem, self.recv_sem = send_sem, recv_sem
        self.number = itertools.count()
        self.sent, self.open = [], []

    def send(self, src, dst, device):
        i = next(self.number)

        def copy():
            return pltpu.make_async_remote_copy(
                src_ref=made(src),
                dst_ref=made(dst),
                send_sem=self.send_sem.at[i],
                recv_sem=self.recv_sem.at[i],
                device_id=device,
                device_id_type=MESH,
            )

        copy().start()
        self.sent.append(copy)
        self.open.append(copy)
        return copy

    def local(self, src, dst):
        i = next(self.number)

        def copy():
            return pltpu.make_async_copy(made(src), made(dst), self.recv_sem.at[i])

        copy().start()
        self.open.append(copy)
        return copy

    def arrived(self, copy):
        if any(copy is c for c in self.sent):
            copy().wait_recv()
        else:
            copy().wait()
        self.open = [c for c in self.open if c is not copy]

    def sent_off(self, copy):
        copy().wait_send()
        self.sent = [c for c in self.sent if c is not copy]

    def drain(self, stream):
        for _ in stream:
            pass

    def finish(self):
        for copy in list(self.open):
            self.arrived(copy)
        for copy in list(self.sent):
            self.sent_off(copy)


def greet(devices, meanwhile=lambda: None):
    barrier = pltpu.get_barrier_semaphore()
    for device in devices:
        pl.semaphore_signal(barrier, inc=1, device_id=device, device_id_type=MESH)
    meanwhile()
    pl.semaphore_wait(barrier, len(devices))


def as_column(row):
    shape = (row.shape[1],) * 2
    same = lax.broadcasted_iota(jnp.int32, shape, 0) == lax.broadcasted_iota(jnp.int32, shape, 1)
    return jnp.sum(jnp.where(same, row, 0.0), axis=1, keepdims=True)


def as_row(column):
    shape = (column.shape[0],) * 2
    same = lax.broadcasted_iota(jnp.int32, shape, 0) == lax.broadcasted_iota(jnp.int32, shape, 1)
    return jnp.sum(jnp.where(same, column, 0.0), axis=0, keepdims=True)


def shared_columns(owner, hidden, used):
    shape = (hidden, 128)
    unit = lax.broadcasted_iota(jnp.int32, shape, 0)
    k = lax.broadcasted_iota(jnp.int32, shape, 1)
    taken = (k < 16 * used) & (unit == (k // used) * 8 * used + owner * used + k % used)
    return jnp.where(taken, 1.0, 0.0).astype(BF)


def run_streams(*streams):
    live = list(streams)
    while live:
        for stream in list(live):
            try:
                next(stream)
            except StopIteration:
                live.remove(stream)


def half_columns(columns):
    return (columns // 128 + 1) // 2 * 128


def ep_peers(place):
    return [place.to_ep(k) for k in range(1, 8)]


def rep_peers(place):
    return [place.to_y(1), place.to_y(-1), place.to_zl(), place.to_core()]


def gather_ep(cp, place, src, dst, columns):
    cut = half_columns(columns)
    lo, hi = pl.ds(0, cut), pl.ds(cut, columns - cut)
    mine = place.ep
    own = cp.local(src, dst.at[mine])
    right = cp.send(src, dst.at[mine], place.to_x(1))
    left = cp.send(src, dst.at[mine], place.to_x(-1))
    over = cp.send(src, dst.at[mine], place.to_zh())
    yield
    from_left, from_right, far = (place.from_x[k] for k in (-1, 1, 2))
    from_over = place.from_z[0]
    cp.arrived(own)
    cp.arrived(right)
    half_a = cp.send(dst.at[from_left, :, lo], dst.at[from_left, :, lo], place.to_x(1))
    cp.arrived(left)
    half_b = cp.send(dst.at[from_right, :, hi], dst.at[from_right, :, hi], place.to_x(-1))
    yield
    cp.arrived(over)
    last = []
    last.append(cp.send(dst.at[from_over], dst.at[from_over], place.to_x(1)))
    last.append(cp.send(dst.at[from_over], dst.at[from_over], place.to_x(-1)))
    yield
    cp.arrived(half_a)
    cp.arrived(half_b)
    last.append(cp.send(dst.at[far], dst.at[far], place.to_zh()))
    yield
    for copy in last:
        cp.arrived(copy)
    for copy in [right, left, over, half_a, half_b] + last:
        cp.sent_off(copy)


def gather_ring_y(cp, place, src, dst, columns, slot):
    cut = half_columns(columns)
    lo, hi = pl.ds(0, cut), pl.ds(cut, columns - cut)
    up = cp.send(src, dst.at[slot(place.y)], place.to_y(1))
    down = cp.send(src, dst.at[slot(place.y)], place.to_y(-1))
    yield
    cp.arrived(up)
    below = slot(place.y - 1)
    half_a = cp.send(dst.at[below, :, lo], dst.at[below, :, lo], place.to_y(1))
    cp.arrived(down)
    above = slot(place.y + 1)
    half_b = cp.send(dst.at[above, :, hi], dst.at[above, :, hi], place.to_y(-1))
    yield
    cp.arrived(half_a)
    cp.arrived(half_b)


def gather_rep(cp, place, src, dst, columns, z_first):
    mine = place.rep
    last = [cp.local(src, dst.at[mine]), cp.send(src, dst.at[mine], place.to_core())]

    def slot(zl):
        return lambda y: place.rep_at(y, zl, place.core)

    def pass_core(index):
        last.append(cp.send(dst.at[index], dst.at[index], place.to_core()))

    here, there = slot(place.zl), slot(1 - place.zl)
    if z_first:
        over = cp.send(src, dst.at[mine], place.to_zl())
        first = gather_ring_y(cp, place, src, dst, columns, here)
        next(first)
        yield
        cp.arrived(over)
        second = gather_ring_y(
            cp, place, dst.at[there(place.y)], dst, columns, there
        )
        next(second)
        pass_core(there(place.y))
        yield
        next(first)
        for k in (-1, 1):
            pass_core(here(place.y + k))
        yield
        next(second)
        for k in (-1, 1):
            pass_core(there(place.y + k))
        yield
        next(first, None)
        pass_core(here(place.y + 2))
        yield
        next(second, None)
        pass_core(there(place.y + 2))
    else:
        over = [cp.send(src, dst.at[mine], place.to_zl())]
        ring = gather_ring_y(cp, place, src, dst, columns, here)
        next(ring)
        yield
        next(ring)
        for k in (-1, 1):
            block = dst.at[here(place.y + k)]
            over.append(cp.send(block, block, place.to_zl()))
            pass_core(here(place.y + k))
        yield
        next(ring, None)
        block = dst.at[here(place.y + 2)]
        over.append(cp.send(block, block, place.to_zl()))
        pass_core(here(place.y + 2))
        yield
        for copy, k in zip(over, (0, -1, 1, 2)):
            cp.arrived(copy)
            pass_core(there(place.y + k))
            yield
    yield
    for copy in last:
        cp.arrived(copy)


def spread_matrix(rows, blocks, used):
    shape = (rows, blocks * ROW_PAD)
    to = lax.broadcasted_iota(jnp.int32, shape, 0)
    at = lax.broadcasted_iota(jnp.int32, shape, 1)
    return jnp.where((at // ROW_PAD) * used + at % ROW_PAD == to, 1.0, 0.0) * jnp.where(
        at % ROW_PAD < used, 1.0, 0.0
    )


ORDER_F = (
    "a", "k1", "wa", "T", "T", "L", "L", "T", "L", "k2", "L", "c", "L", "L",
    "T", "pr", "W", "h0", "C", "h1", "W", "W", "C", "W", "C", "D", "D", "W",
    "D", "D", "W", "D", "D", "op", "C",
)


def kernel_front(
    tok, cot, length, mask, routes, w_query, w_key, w_value, w_output, w_route,
    shared_gate, shared_up, shared_down, norm_attn, norm_ffn, h_cosine, h_sine,
    w_slices, w_both, w_whole, w_router, w_down, cot_all, extra,
    o_hidden, o_qkv, o_probs, gains, residual, attended, hidden, live,
    hidden_one, qkv, probs, cosine, sine, slices, whole, down, wide_tok,
    land_slices, land_whole, pack_slices, pack_whole, v_slices, v_whole, v_tok,
    heads, land_heads, live_row, send_sem, recv_sem,
):
    place = Place()
    cp = Copies(send_sem, recv_sem)
    rows, width = tok.shape
    group = 8 * rows
    span = HEADS_DEV * HD
    mine = place.ep
    top = routes.shape[0]

    def own_inputs():
        position = mine * rows + lax.broadcasted_iota(jnp.int32, (1, rows), 1)
        alive = jnp.where((position < length[...]) & (mask[...] == 1), 1.0, 0.0)
        live[...] = as_column(alive)
        block = jnp.concatenate(
            [routes[...].astype(F32), alive, jnp.zeros((EXTRA - top - 1, rows), F32)], axis=0
        )
        wide_tok[:, :width] = tok[...]
        wide_tok[:, width:] = block.T.astype(BF)
        for ref in (slices, whole, down):
            ref[...] = jnp.zeros_like(ref)
        rows_of = slice(0, w_query.shape[0])
        whole[rows_of, :width] = w_output[...]
        whole[rows_of, width : width + w_route.shape[1]] = w_route[...]
        down[: shared_down.shape[0], :] = shared_down[...]
        gains_of = [as_column(g[...].astype(F32)) for g in (norm_attn, norm_ffn)]
        lane = lax.broadcasted_iota(jnp.int32, (w_query.shape[0], 128), 1)
        spare = 16 * shared_down.shape[0]
        for owner in range(8):
            if owner * span < width:
                for n, w in enumerate((w_query, w_key, w_value)):
                    slices[owner, rows_of, n * span : (n + 1) * span] = w[:, owner * span : (owner + 1) * span]
            pick = shared_columns(owner, shared_gate.shape[1], shared_down.shape[0])
            gate = dot(shared_gate[...], pick)
            gate = jnp.where(lane == spare, gains_of[0], jnp.where(lane == spare + 1, gains_of[1], gate))
            slices[owner, rows_of, 3 * span : 3 * span + 128] = gate.astype(BF)
            slices[owner, rows_of, 3 * span + 128 :] = dot(shared_up[...], pick).astype(BF)

    tables = [cp.local(h_cosine, cosine), cp.local(h_sine, sine)]
    greet(ep_peers(place) + rep_peers(place), own_inputs)
    streams, kept = {}, {}
    used = pack_slices.shape[0] // 8
    per = BLOCK // rows

    def pack(land, packed):
        spread = spread_matrix(8 * used, 8, used).astype(BF)
        for c in range(0, land.shape[2], 128):
            block = land[:, :, c : c + 128].reshape(8 * ROW_PAD, 128)
            packed[:, c : c + 128] = dot(spread, block).astype(BF)

    def start(name, stream):
        streams[name] = stream
        next(stream)

    def to_owners():
        kept["slices"] = [cp.local(slices.at[mine], land_slices.at[mine])] + [
            cp.send(slices.at[(mine + k) % 8], land_slices.at[mine], place.to_ep(k)) for k in range(1, 8)
        ]
        start("T", gather_ep(cp, place, wide_tok, v_tok, wide_tok.shape[1]))

    def to_all():
        kept["whole"] = [cp.local(whole, land_whole.at[mine])] + [
            cp.send(whole, land_whole.at[mine], place.to_ep(k)) for k in range(1, 8)
        ]

    def pack_first():
        for copy in kept["slices"]:
            cp.arrived(copy)
        pack(land_slices, pack_slices)
        start("L", gather_rep(cp, place, pack_slices, v_slices, slices.shape[2], True))

    def pack_second():
        for copy in kept["whole"]:
            cp.arrived(copy)
        pack(land_whole, pack_whole)
        start("W", gather_rep(cp, place, pack_whole, v_whole, whole.shape[1], True))
        start("D", gather_rep(cp, place, down, w_down, down.shape[1], True))

    def start_cot():
        start("C", gather_ep(cp, place, cot, cot_all, width))

    def projections():
        cp.local(v_slices, w_slices)
        cp.local(v_slices.at[:, :, pl.ds(3 * span, 256)], w_both)
        cp.local(v_tok.at[:, :, pl.ds(width, EXTRA)], extra)
        block = v_slices[:, :, 3 * span : 3 * span + 128].reshape(width, 128).astype(F32).T
        gains[...] = block[112:120, :]
        live_row[...] = jnp.concatenate(
            [v_tok[i, :, width:].astype(F32).T[:8, :] for i in range(8)], axis=1
        )

        for copy in tables:
            cp.arrived(copy)

        @pl.loop(0, group // BLOCK)
        def _(i):
            at = pl.ds(pl.multiple_of(i * BLOCK, BLOCK), BLOCK)
            values = v_tok[pl.ds(i * per, per), :, :width].reshape(BLOCK, width).astype(F32)
            scale = lax.rsqrt(jnp.sum(values * values, axis=1, keepdims=True) / width + EPS)
            low = (values * scale * gains[0:1, :]).astype(BF)
            hidden_one[at, :] = low
            raw = dot(low, v_slices[:, :, : 3 * span].reshape(width, 3 * span))
            cos, sin = cosine[at, :], sine[at, :]
            for h in range(2 * HEADS_DEV):
                c = slice(h * HD, (h + 1) * HD)
                qkv[at, c] = turn(raw[:, c], cos, sin).astype(BF)
            qkv[at, 2 * span :] = raw[:, 2 * span :].astype(BF)

        cp.local(hidden_one, o_hidden)
        cp.local(qkv, o_qkv)

    def head(h):
        attention_head(h, qkv, live_row, probs, heads)
        cp.local(probs.at[h], o_probs.at[h])
        if h == HEADS_DEV - 1:
            column = pl.ds(pl.multiple_of(mine * span, 128), span)
            kept["heads"] = [cp.local(heads.at[mine], land_heads.at[:, column])] + [
                cp.send(heads.at[(mine + k) % 8], land_heads.at[:, column], place.to_ep(k))
                for k in range(1, 8)
            ]

    def output():
        cp.local(v_whole, w_whole)
        cp.local(v_whole.at[:, :, pl.ds(width, EXTRA)], w_router)
        for copy in kept["heads"]:
            cp.arrived(copy)
        low = land_heads[:, :width]
        attended[...] = low
        step = 256
        squares = jnp.zeros((rows, 1), F32)
        for c in range(0, width, step):
            matrix = v_whole[:, :, c : c + step].reshape(width, step)
            part = tok[:, c : c + step].astype(F32) + live[...] * dot(low, matrix)
            residual[:, c : c + step] = part
            squares += jnp.sum(part * part, axis=1, keepdims=True)
        scale = lax.rsqrt(squares / width + EPS)
        hidden[...] = (residual[...] * scale * gains[1:2, :]).astype(BF)

    pieces = {
        "a": to_owners, "wa": to_all, "k1": pack_first, "k2": pack_second, "c": start_cot, "pr": projections,
        "h0": functools.partial(head, 0), "h1": functools.partial(head, 1), "op": output,
    }
    for name in ORDER_F:
        if name in pieces:
            pieces[name]()
        else:
            next(streams[name], None)
    run_streams(*streams.values())
    cp.finish()


def call_front(
    tok, cot, length, mask, routes, w_query, w_key, w_value, w_output, w_route,
    shared_gate, shared_up, shared_down, norm_attn, norm_ffn, cosine, sine,
):
    anyspace = pl.BlockSpec(memory_space=pl.ANY)
    vmem = pl.BlockSpec(memory_space=pltpu.VMEM)
    rows, width = cot.shape
    used = w_query.shape[0]
    group = 8 * rows
    span = HEADS_DEV * HD
    shape = jax.ShapeDtypeStruct
    columns, wide = 3 * span + 256, width + EXTRA
    return pl.pallas_call(
        kernel_front,
        out_shape=(
            shape((16, 8 * used, columns), BF),
            shape((16, 8 * used, columns - 3 * span), BF),
            shape((16, 8 * used, wide), BF),
            shape((16, 8 * used, EXTRA), BF),
            shape((16, ROW_PAD, width), BF),
            shape((8,) + cot.shape, BF),
            shape((8, rows, EXTRA), BF),
            shape((group, width), BF),
            shape((group, 3 * span), BF),
            shape((HEADS_DEV, group, group), BF),
            shape((8, width), F32),
            shape((rows, width), F32),
            shape((rows, width), BF),
            shape((rows, width), BF),
            shape((rows, 1), F32),
        ),
        in_specs=[vmem, anyspace] + [vmem] * 13 + [anyspace] * 2,
        out_specs=(anyspace,) * 10 + (vmem,) * 5,
        scratch_shapes=[
            pltpu.VMEM((group, width), BF),
            pltpu.VMEM((group, 3 * span), BF),
            pltpu.VMEM((HEADS_DEV, group, group), BF),
            pltpu.VMEM((group, HD), F32),
            pltpu.VMEM((group, HD), F32),
            pltpu.VMEM((8, ROW_PAD, columns), BF),
            pltpu.VMEM((ROW_PAD, wide), BF),
            pltpu.VMEM((ROW_PAD, width), BF),
            pltpu.VMEM((rows, wide), BF),
            pltpu.VMEM((8, ROW_PAD, columns), BF),
            pltpu.VMEM((8, ROW_PAD, wide), BF),
            pltpu.VMEM((8 * used, columns), BF),
            pltpu.VMEM((8 * used, wide), BF),
            pltpu.VMEM((16, 8 * used, columns), BF),
            pltpu.VMEM((16, 8 * used, wide), BF),
            pltpu.VMEM((8, rows, wide), BF),
            pltpu.VMEM((8, rows, span), BF),
            pltpu.VMEM((rows, 8 * span), BF),
            pltpu.VMEM((8, group), F32),
            pltpu.SemaphoreType.DMA((200,)),
            pltpu.SemaphoreType.DMA((200,)),
        ],
        compiler_params=pltpu.CompilerParams(
            collective_id=0, has_side_effects=True, vmem_limit_bytes=VMEM_LIMIT
        ),
        name="front",
    )(
        tok, cot, length, mask, routes, w_query, w_key, w_value, w_output, w_route,
        shared_gate, shared_up, shared_down, norm_attn, norm_ffn, cosine, sine,
    )


def add_into(out, terms):
    lead = out.shape[:-2]
    count = math.prod(lead)

    def add(index):
        if len(terms) == 2 and out.dtype == BF:
            out[index] = terms[0][index] + terms[1][index]
            return
        total = terms[0][index].astype(F32)
        for term in terms[1:]:
            total += term[index].astype(F32)
        out[index] = total.astype(out.dtype)

    if count == 1:
        add((0,) * len(lead) + (slice(None),))
    else:
        inner = lead[-1] if lead else 1

        @pl.loop(0, count)
        def _(i):
            add(((i // inner, i % inner) if len(lead) == 2 else (i,)) + (slice(None),))


class Grid:
    def __init__(self, ring, pair, up, down, over):
        self.here, self.up_at, self.down_at, self.far = ring, (ring + 1) % 4, (ring + 3) % 4, (ring + 2) % 4
        self.pair, self.other = pair, 1 - pair
        self.up, self.down, self.over = up, down, over


def grid_rep(place):
    return Grid(place.y, place.zl, place.to_y(1), place.to_y(-1), place.to_zl())


def grid_ep(place):
    return Grid(place.x, place.zh, place.to_x(1), place.to_x(-1), place.to_zh())


def ring_pair_bufs(rows, columns):
    return [pltpu.VMEM((7, rows, columns), BF)]


def sum_ring_pair(cp, g, source, mine, bufs, out, more=()):
    (buf,) = bufs
    near, last, half, over = (0, 1), ((2, 3), (4, 5)), 0, 6
    b = lambda i: buf.at[i]
    s1 = cp.send(source.at[g.far, 0], b(near[0]), g.up)
    s2 = cp.send(source.at[g.far, 1], b(near[1]), g.down)
    s3 = cp.send(source.at[g.up_at, 1], b(last[0][1]), g.up)
    s4 = cp.send(source.at[g.down_at, 0], b(last[1][0]), g.down)
    yield
    cp.arrived(s1)
    add_into(mine.at[g.up_at, 0], [mine.at[g.up_at, 0], b(near[0])])
    s5 = cp.send(mine.at[g.up_at, 0], b(last[0][0]), g.up)
    cp.arrived(s2)
    add_into(mine.at[g.down_at, 1], [mine.at[g.down_at, 1], b(near[1])])
    s6 = cp.send(mine.at[g.down_at, 1], b(last[1][1]), g.down)
    yield
    for copy in (s3, s4, s5, s6):
        cp.arrived(copy)
    add_into(
        b(half),
        [mine.at[g.here, g.other], buf.at[2 + g.other], buf.at[4 + g.other]],
    )
    s7 = cp.send(b(half), b(over), g.over)
    yield
    cp.arrived(s7)
    add_into(
        out, [mine.at[g.here, g.pair], buf.at[2 + g.pair], buf.at[4 + g.pair], b(over), *more]
    )
    for copy in (s1, s2, s3, s4, s5, s6, s7):
        cp.sent_off(copy)


def pair_ring_bufs(rows, columns):
    cut = half_columns(columns)
    return [
        pltpu.VMEM((4, rows, columns), BF),
        pltpu.VMEM((2, rows, columns), BF),
        pltpu.VMEM((rows, cut), BF),
        pltpu.VMEM((rows, columns - cut), BF),
    ]


def sum_pair_ring(cp, g, source, mine, bufs, out):
    acc, last, near_lo, near_hi = bufs
    columns = acc.shape[2]
    cut = half_columns(columns)
    lo, hi = pl.ds(0, cut), pl.ds(cut, columns - cut)
    s0 = cp.send(source.at[:, g.other], acc, g.over)
    yield
    cp.arrived(s0)
    add_into(acc, [acc, mine.at[:, g.pair]])
    s1 = cp.send(acc.at[g.far, :, lo], near_lo, g.up)
    s2 = cp.send(acc.at[g.far, :, hi], near_hi, g.down)
    s3 = cp.send(acc.at[g.up_at, :, hi], last.at[0, :, hi], g.up)
    s4 = cp.send(acc.at[g.down_at, :, lo], last.at[1, :, lo], g.down)
    yield
    cp.arrived(s1)
    part = acc.at[g.up_at, :, lo]
    add_into(part, [part, near_lo])
    s5 = cp.send(part, last.at[0, :, lo], g.up)
    cp.arrived(s2)
    part = acc.at[g.down_at, :, hi]
    add_into(part, [part, near_hi])
    s6 = cp.send(part, last.at[1, :, hi], g.down)
    yield
    for copy in (s3, s4, s5, s6):
        cp.arrived(copy)
    add_into(out, [acc.at[g.here], last.at[0], last.at[1]])
    for copy in (s0, s1, s2, s3, s4, s5, s6):
        cp.sent_off(copy)


def gather_expert(cp, place, grid, src, at, z_first):
    zl, other = grid.pair, grid.other
    columns = src.shape[1]
    cut = half_columns(columns)
    lo, hi = pl.ds(0, cut), pl.ds(cut, columns - cut)
    up, down, over, mate = place.to_y(1), place.to_y(-1), place.to_zl(), place.to_core()

    def forward(k, z, to):
        return cp.send(at(k, z), at(k, z), to)

    def ring_halves(z):
        a = cp.send(at(-1, z).at[:, lo], at(-1, z).at[:, lo], up)
        b = cp.send(at(1, z).at[:, hi], at(1, z).at[:, hi], down)
        return a, b

    own = cp.local(src, at(0, zl))
    first = [cp.send(src, at(0, zl), to) for to in (up, down)]
    across = cp.send(src, at(0, zl), over)
    cp.send(src, at(0, zl), mate)
    yield
    if z_first:
        cp.arrived(across)
        second = [forward(0, other, to) for to in (up, down)]
        forward(0, other, mate)
        yield
        halves = []
        for pair, z in ((first, zl), (second, other)):
            for copy in pair:
                cp.arrived(copy)
            halves.append(ring_halves(z))
            forward(-1, z, mate)
            forward(1, z, mate)
            yield
        for pair, z in zip(halves, (zl, other)):
            for copy in pair:
                cp.arrived(copy)
            forward(2, z, mate)
            yield
    else:
        for copy in first:
            cp.arrived(copy)
        halves = ring_halves(zl)
        crossed = [across]
        for k in (-1, 1):
            crossed.append(forward(k, zl, over))
            forward(k, zl, mate)
        yield
        for copy in halves:
            cp.arrived(copy)
        crossed.append(forward(2, zl, over))
        forward(2, zl, mate)
        yield
        for copy, k in zip(crossed, (0, -1, 1, 2)):
            cp.arrived(copy)
            forward(k, other, mate)
            yield
    cp.arrived(own)


def expert_stream(cp, place, grid, sent, kept, got, bufs, total, at, ring_first, z_first, free, again):
    neighbours = rep_peers(place)
    if again:
        pl.semaphore_wait(free, len(neighbours))
    b = cp.send(sent, got, place.to_core())
    yield
    cp.arrived(b)
    add_into(got, [got, kept])
    cp.sent_off(b)
    summed = sum_ring_pair if ring_first else sum_pair_ring
    yield from summed(cp, grid, got, got, bufs, total)
    if not again:
        for device in neighbours:
            pl.semaphore_signal(free, inc=1, device_id=device, device_id_type=MESH)
    yield from gather_expert(cp, place, grid, total, at, z_first)


def dense_stream(cp, place, grid, grad, got, bufs, total, ring_first):
    b = cp.send(grad.at[:, :, 1 - place.core], got, place.to_core())
    yield
    cp.arrived(b)
    own = grad.at[:, :, place.core]
    add_into(got, [got, own])
    summed = sum_ring_pair if ring_first else sum_pair_ring
    yield from summed(cp, grid, got, got, bufs, total)


def spread_stream(cp, place, stream, total, padded, result):
    yield from stream
    used = total.shape[0] // 8
    spread = spread_matrix(8 * used, 8, used).astype(BF)
    columns = total.shape[1]
    for c in range(0, columns, 128):
        padded[:, :, c : c + 128] = (
            dot_tn(spread, total[:, c : c + 128]).astype(BF).reshape(8, ROW_PAD, 128)
        )
    cp.local(padded.at[place.ep], result.at[place.ep])
    for k in range(1, 8):
        cp.send(padded.at[(place.ep + k) % 8], result.at[place.ep], place.to_ep(k))


def advance(*streams):
    for stream in streams:
        next(stream, None)


BLOCK = 256


def turn(values, cosine, sine):
    return values * cosine + pltpu.roll(values, HD // 2, 1) * sine


def attention_head(h, qkv, live, probs, heads):
    group = qkv.shape[0]
    span = HEADS_DEV * HD
    per = BLOCK // heads.shape[1]
    rows = lax.broadcasted_iota(jnp.int32, (BLOCK, BLOCK), 0)
    columns = lax.broadcasted_iota(jnp.int32, (BLOCK, BLOCK), 1)
    q, k, v = (slice(n * span + h * HD, n * span + (h + 1) * HD) for n in range(3))
    for i in range(group // BLOCK):
        at = slice(i * BLOCK, (i + 1) * BLOCK)
        n = (i + 1) * BLOCK
        scores = dot_nt(qkv[at, q], qkv[:n, k]) * HD**-0.5
        parts = []
        for j in range(i + 1):
            alive = live[LIVE : LIVE + 1, j * BLOCK : (j + 1) * BLOCK] > 0.5
            if j == i:
                alive = (alive & (columns < rows)) | (columns == rows)
            parts.append(jnp.where(alive, scores[:, j * BLOCK : (j + 1) * BLOCK], -1e30))
        scores = jnp.concatenate(parts, axis=1) if len(parts) > 1 else parts[0]
        top = jnp.max(scores, axis=1, keepdims=True)
        weights = jnp.exp(scores - top)
        low = (weights * (1.0 / jnp.sum(weights, axis=1, keepdims=True))).astype(BF)
        probs[h, at, :n] = low
        heads[i * per : (i + 1) * per, :, h * HD : (h + 1) * HD] = (
            dot(low, qkv[:n, v]).astype(BF).reshape(per, BLOCK // per, HD)
        )


def attention_back_head(h, g_heads, qkv, probs, cosine, sine, g_keys, g_values, g_qkv):
    group = qkv.shape[0]
    blocks, rows = g_heads.shape[:2]
    per = BLOCK // rows
    span = HEADS_DEV * HD
    scale = HD**-0.5
    q, k, v = (slice(n * span + h * HD, n * span + (h + 1) * HD) for n in range(3))
    head = slice(h * HD, (h + 1) * HD)
    for i in reversed(range(group // BLOCK)):
        at = slice(i * BLOCK, (i + 1) * BLOCK)
        n = (i + 1) * BLOCK
        g_att = g_heads[i * per : (i + 1) * per, :, head].reshape(BLOCK, HD)
        low = probs[h, at, :n]
        weights = low.astype(F32)
        g_probs = dot_nt(g_att, qkv[:n, v])
        delta = jnp.sum(weights * g_probs, axis=1, keepdims=True)
        g_scores = (weights * (g_probs - delta)).astype(BF)
        g_query = dot(g_scores, qkv[:n, k]) * scale
        g_qkv[at, q] = turn(g_query, cosine[at, :], -sine[at, :]).astype(BF)
        g_key = dot_tn(g_scores, qkv[at, q])
        g_value = dot_tn(low, g_att)
        if i == group // BLOCK - 1:
            g_keys[...] = g_key
            g_values[...] = g_value
        else:
            g_keys[:n, :] += g_key
            g_values[:n, :] += g_value
    g_qkv[:, k] = turn(g_keys[...] * scale, cosine[...], -sine[...]).astype(BF)
    g_qkv[:, v] = g_values[...].astype(BF)


def store_rows(ref, lead, columns, row, value):
    depth = ref.shape[len(lead)]
    done = 0
    while done < value.shape[0]:
        block, offset = divmod(row + done, depth)
        take = min(depth - offset, value.shape[0] - done)
        at = tuple(int(i) for i in np.unravel_index(block, lead))
        ref[at + (slice(offset, offset + take), columns)] = value[done : done + take]
        done += take


def one_expert(
    loop, blocks, x, g, w_gate, w_up, w_down, weight, wact, g_a, g_b, outs, grads, before, q_sum, first
):
    width = g.shape[2]

    @pl.loop(*loop)
    def _(i):
        pair = blocks(i)

        def load(ref):
            return jnp.concatenate([ref[b] for b in pair], axis=0)

        def store(ref, value):
            for n, b in enumerate(pair):
                ref[b] = value[n * (BLOCK // 2) : (n + 1) * (BLOCK // 2)]

        if before is not None:
            before(pair, load, store)
        share = weight(load)
        rows = load(x)
        gate = dot(rows, w_gate[...])
        up = dot(rows, w_up[...])
        raw = dot_nt(load(g), w_down[...])
        sig = 1.0 / (1.0 + jnp.exp(-gate))
        silu = gate * sig
        act = silu * up
        if q_sum is not None:
            q_sum(pair, load, jnp.sum(act * raw, axis=1, keepdims=True))
        low = (act * share).astype(BF)
        store(wact, low)
        raw = raw * share
        a = (raw * up * (sig + silu * (1.0 - sig))).astype(BF)
        b = (raw * silu).astype(BF)
        store(g_a, a)
        store(g_b, b)
        part = dot(low, w_down[...])
        back = dot_nt(a, w_gate[...]) + dot_nt(b, w_up[...])
        for n, k in enumerate(pair):
            at = slice(n * (BLOCK // 2), (n + 1) * (BLOCK // 2))
            more, behind = part[at], back[at]
            if not first:
                more += outs[k // 2, k % 2].astype(F32)
                behind += grads[k // 2, k % 2, :, :width].astype(F32)
            outs[k // 2, k % 2] = more.astype(BF)
            grads[k // 2, k % 2, :, :width] = behind.astype(BF)


ORDER_A = (
    "A", "A", "p0", "A", "p1", "A", "p2", "p3", "w1", "pr", "g0", "u0", "d0", "G0",
    "sp", "G0", "U0", "D0", "q1", "G0", "U0", "r1", "G0", "U0", "D0", "x", "g1", "G0",
    "G0", "X0", "D0", "U0", "u1", "G1", "G0", "G0", "D0", "X1", "d1", "U1", "G1", "U0",
    "U0", "D0", "ss", "X0", "D1",
)
ORDER_B = (
    "G0", "G0", "X1", "D0", "X0", "U1", "X1", "n2", "G1", "U0", "dw", "U0", "sn", "D0",
    "o", "G1", "D1", "G1", "W", "h0", "O", "S", "N", "U1", "U0", "U0", "D0", "D0",
    "D0", "h1", "O", "S", "G1", "G1", "D1", "N", "hp", "W", "S", "G1", "dq", "N",
    "G1", "G1", "U1", "H0", "W", "Q", "O", "H1", "D1", "W", "S", "N", "Q", "U1",
    "U1", "H0", "D1", "D1", "H1", "Q", "H0", "U1", "H1", "n1", "U1", "Q", "D1", "D1",
    "U1", "U1", "D1", "D1",
)
Y_FIRST = ()


def kernel_rest(
    experts, top,
    x_own, g_all, e_gate, e_up, e_down, h_probs, h_hidden, h_qkv, w_slices, h_whole,
    h_residual, h_cot, h_tok, h_attended, h_cosine, h_sine,
    h_extra, h_router, h_both, h_padded, live, gains,
    out, d_tok, x_gate, x_up, x_down, o_qkv, o_shared, o_whole, o_down,
    x, m_grads, m_outs, b_grads, b_outs, total_grads, total_hidden, e_got, e_bufs, e_total,
    v_shared, v_down, got, bufs, g_heads, probs, free, send_sem, recv_sem,
):
    place = Place()
    cp = Copies(send_sem, recv_sem)
    rows, width = x_own.shape
    group = 8 * rows
    mine, core = place.ep, place.core
    ge, gr = grid_ep(place), grid_rep(place)
    wide = width + EXTRA
    exp_dev, _, hidden = e_gate.shape
    span = HEADS_DEV * HD
    cut = wide // 2 // 128 * 128
    cuts = (pl.ds(0, cut), pl.ds(cut, wide - cut))
    m_grads, m_outs, total_grads, total_hidden, x_gate, x_up, x_down = (
        Later(ref) for ref in (m_grads, m_outs, total_grads, total_hidden, x_gate, x_up, x_down)
    )
    later = lambda refs: [Later(ref) if hasattr(ref, "at") else later(ref) for ref in refs]
    b_grads, b_outs, e_got, e_bufs, e_total = (
        later(refs) for refs in (b_grads, b_outs, e_got, e_bufs, e_total)
    )
    half_part = width // 16
    half = width // 2
    ours = pl.ds(pl.multiple_of(core * half, 128), half)
    theirs = pl.ds(pl.multiple_of(place.mate * half, 128), half)
    streams = {}
    from_x, from_z = place.from_x, place.from_z

    def view(ref, c):
        return ref.at[:, :, :, c]

    def phase_a(
        g, extra, w_router, s_both, s_padded, w_gate, w_up, w_down, wact, g_a, g_b, gates, named,
        swact, sg_a, sg_b, s_down, d_sdown, d_gate, d_up, d_down,
    ):
        first = [cp.local(h_extra, extra), cp.local(h_router, w_router), cp.local(g_all, g)]
        small = [cp.local(h_both, s_both), cp.local(h_padded, s_padded)]
        weights = ((e_gate, w_gate), (e_up, w_up), (e_down, w_down))
        loads = [cp.local(a.at[0], b) for a, b in weights]
        greet(ep_peers(place) + rep_peers(place))
        streams["A"] = gather_ep(cp, place, x_own, Later(x), width)
        next(streams["A"])
        for copy in first:
            cp.arrived(copy)
        lane = lax.broadcasted_iota(jnp.int32, (BLOCK, EXTRA), 1)

        def router(values, lanes):
            logits = jnp.where(lanes < experts, dot(values, w_router[...]), -1e30)
            weights = jnp.exp(logits - jnp.max(logits, axis=1, keepdims=True))
            return weights / jnp.sum(weights, axis=1, keepdims=True)

        def route(pair, load, store):
            prob = router(load(x), lane)
            routes = load(extra)
            whole = routes.astype(F32).astype(jnp.int32)
            chosen = lane == whole[:, 0:1]
            for j in range(1, top):
                chosen = chosen | (lane == whole[:, j : j + 1])
            store(named, jnp.where(chosen, 1.0, 0.0))
            store(gates, jnp.where(chosen, prob, 0.0) * routes[:, top : top + 1].astype(F32))
            for b in pair:
                m_grads[b // 2, b % 2, :, width:] = jnp.zeros((BLOCK // 2, EXTRA), BF)

        shared = s_down.shape[0]
        used = s_padded.shape[0] // ROW_PAD * 7 // 16
        steps = group // BLOCK
        in_turn = lambda i: (2 * i, 2 * i + 1)
        flat = lambda ref: ref[...].reshape(group, ref.shape[2])
        columns_of = lambda ref, c: ref[:, :, c : c + BLOCK].reshape(group, BLOCK)
        arrivals = (
            (place.ep, from_x[-1]), (from_x[1], from_z[0]), (from_x[2], from_z[-1]), (from_z[1], from_z[2]),
        )

        def shared_pass():
            for copy in small:
                cp.arrived(copy)
            pack = spread_matrix(shared, 16, used).astype(BF)
            s_down[...] = dot(pack, s_padded[...]).astype(BF)
            one_expert(
                (0, steps), in_turn, x, g, s_both.at[:, :shared], s_both.at[:, shared:], s_down,
                lambda load: load(extra)[:, top : top + 1].astype(F32),
                swact, sg_a, sg_b, m_outs, m_grads, None, None, False,
            )

        def shared_sums():
            for c in range(0, width, BLOCK):
                left = columns_of(x, c)
                for n, back in enumerate((sg_a, sg_b)):
                    store_rows(
                        v_shared, (4, 2, 2), slice(n * shared, (n + 1) * shared), c,
                        dot_tn(left, flat(back)).astype(BF),
                    )
            d_sdown[...] = dot_tn(flat(swact), flat(g)).astype(BF)
            pack = spread_matrix(shared, 16, used).astype(BF)
            for c in range(0, s_padded.shape[0], BLOCK):
                store_rows(
                    v_down, (4, 2, 2), slice(0, width), c,
                    dot_tn(pack[:, c : c + BLOCK], d_sdown[...]).astype(BF),
                )

        def expert_pass(e, loop, blocks):
            expert = mine * exp_dev + e

            def picked(load):
                return jnp.sum(jnp.where(lane == expert, load(gates), 0.0), axis=1, keepdims=True)

            def q_sum(pair, load, value):
                value = value * load(named)
                for n, b in enumerate(pair):
                    at = slice(n * (BLOCK // 2), (n + 1) * (BLOCK // 2))
                    old = m_grads[b // 2, b % 2, :, width:].astype(F32)
                    new = jnp.where(lane[: BLOCK // 2] == expert, value[at], old)
                    m_grads[b // 2, b % 2, :, width:] = new.astype(BF)

            for copy in loads:
                cp.arrived(copy)
            loads.clear()
            one_expert(
                loop, blocks, x, g, w_gate, w_up, w_down, picked,
                wact, g_a, g_b, m_outs, m_grads, route if e == 0 else None, q_sum, e == 0,
            )

        def next_weights(e):
            loads.extend(cp.local(a.at[e], b) for a, b in weights)

        def stream(e, n, sent, kept, at, ring_first):
            streams["GUD"[n] + str(e)] = one = expert_stream(
                cp, place, gr, sent, kept, e_got[n], e_bufs[n], e_total[e][n], at, ring_first,
                (e, n) not in Y_FIRST, free.at[n], e > 0,
            )
            next(one)

        def expert_sums(e, n):
            if n < 2:
                d, back, x_out = ((d_gate, g_a, x_gate), (d_up, g_b, x_up))[n]
                for c in range(0, width, BLOCK):
                    store_rows(
                        d, (2, 4, 2), slice(0, hidden), c, dot_tn(columns_of(x, c), flat(back)).astype(BF)
                    )
                stream(
                    e, n, d.at[place.mate], d.at[core],
                    lambda k, z: x_out.at[e, core, place.y_at[k], z], True,
                )
            else:
                for c in range(0, hidden, 128):
                    left = wact[:, :, c : c + 128].reshape(group, 128)
                    store_rows(d_down, (4, 2), slice(0, width), c, dot_tn(left, flat(g)).astype(BF))
                stream(
                    e, n, d_down.at[:, :, :, theirs], d_down.at[:, :, :, ours],
                    lambda k, z: x_down.at[e, place.y_at[k], z, :, ours], True,
                )

        def own_probs():
            probs[...] = router(x[mine], lane[:rows])

        def start_x():
            for n, (c, b) in enumerate(zip(cuts, b_grads)):
                streams["X" + str(n)] = one = sum_ring_pair(
                    cp, ge, view(m_grads, c), view(m_grads, c), b, total_grads.at[:, c]
                )
                next(one)

        pieces = {"sp": shared_pass, "ss": shared_sums, "x": start_x, "w1": functools.partial(next_weights, 1)}
        for n, pair in enumerate(arrivals):
            pieces["p" + str(n)] = functools.partial(expert_pass, 0, (0, 1), lambda i, pair=pair: pair)
        pieces["q1"] = functools.partial(expert_pass, 1, (0, steps // 2), in_turn)
        pieces["r1"] = functools.partial(expert_pass, 1, (steps // 2, steps), in_turn)
        pieces["pr"] = own_probs
        for e in range(exp_dev):
            for n in range(3):
                pieces["gud"[n] + str(e)] = functools.partial(expert_sums, e, n)
        follow(ORDER_A, pieces)

    def follow(order, pieces):
        for name in order:
            if name in pieces:
                pieces[name]()
            else:
                next(streams[name], None)

    pl.run_scoped(
        phase_a,
        pltpu.VMEM((8, rows, width), BF),
        pltpu.VMEM(h_extra.shape, BF),
        pltpu.VMEM(h_router.shape, BF),
        pltpu.VMEM(h_both.shape, BF),
        pltpu.VMEM(h_padded.shape, BF),
        pltpu.VMEM((width, hidden), BF),
        pltpu.VMEM((width, hidden), BF),
        pltpu.VMEM((hidden, width), BF),
        *[pltpu.VMEM((8, rows, hidden), BF)] * 3,
        *[pltpu.VMEM((8, rows, EXTRA), F32)] * 2,
        *[pltpu.VMEM((8, rows, h_both.shape[1] // 2), BF)] * 3,
        *[pltpu.VMEM((h_both.shape[1] // 2, width), BF)] * 2,
        pltpu.VMEM((2, 4, 2, half_part, hidden), BF),
        pltpu.VMEM((2, 4, 2, half_part, hidden), BF),
        pltpu.VMEM((4, 2, hidden // 8, width), BF),
    )

    def phase_b(
        v_probs, v_qkvs, v_w, w_whole, residual, cot, tok, attended, cosine, sine,
        v_whole, v_qkv, totals, padded, g_att, g_residual, g_keys, g_values, g_qkv, g_branch,
    ):
        loads = [
            cp.local(a, b)
            for a, b in (
                (h_residual, residual), (h_cot, cot), (h_whole, w_whole), (h_attended, attended),
                (h_qkv, v_qkvs), (h_probs, v_probs), (h_cosine, cosine), (h_sine, sine),
                (w_slices.at[:, : v_w.shape[1]], v_w), (h_hidden, x), (h_tok, tok),
            )
        ]
        alive = live[...]
        kept = {}

        step = 256

        def second_norm():
            for copy in loads:
                cp.arrived(copy)
            router_grad = total_grads[:, width:] * alive
            prob = probs[...]
            logit_grad = prob * (router_grad - jnp.sum(prob * router_grad, axis=1, keepdims=True))
            squares = jnp.zeros((rows, 1), F32)
            mean_k = jnp.zeros((rows, 1), F32)
            for c in range(0, width, step):
                part = residual[:, c : c + step]
                squares += jnp.sum(part * part, axis=1, keepdims=True)
            scale = lax.rsqrt(squares / width + EPS)
            gain_rows = []
            for c in range(0, width, step):
                k = total_grads[:, c : c + step] + lax.dot_general(
                    logit_grad, w_whole[c : c + step, width:].astype(F32), (((1,), (1,)), ((), ())),
                    preferred_element_type=F32, precision=HIGH,
                )
                normed = residual[:, c : c + step] * scale
                gain_rows.append(jnp.sum(k * normed, axis=0, keepdims=True))
                k = k * gains[1:2, c : c + step]
                mean_k += jnp.sum(k * normed, axis=1, keepdims=True)
                g_residual[:, c : c + step] = k
            mean_k = mean_k / width
            for c in range(0, width, step):
                normed = residual[:, c : c + step] * scale
                grad = cot[:, c : c + step].astype(F32) + scale * (
                    g_residual[:, c : c + step] - normed * mean_k
                )
                g_residual[:, c : c + step] = grad
                g_branch[:, c : c + step] = (alive * grad).astype(BF)
            for c in range(0, width, step):
                g_att[c // step] = dot_nt(g_branch[...], w_whole[c : c + step, :width]).astype(BF)
            for c in range(width // step, 8):
                g_att[c] = jnp.zeros((rows, span), BF)
            kept["third"] = [cp.local(g_att.at[mine], g_heads.at[mine])] + [
                cp.send(g_att.at[(mine + k) % 8], g_heads.at[mine], place.to_ep(k)) for k in range(1, 8)
            ]
            kept["norm"] = logit_grad, scale, gain_rows

        def whole_sums():
            logit_grad, scale, gain_rows = kept["norm"]
            for i in range(2):
                c = slice(i * width // 2, (i + 1) * width // 2)
                v_whole[2 * i : 2 * i + 2, :, :, :, :width] = (
                    dot_tn(attended[:, c], g_branch[...]).astype(BF).reshape(2, 2, 2, width // 16, width)
                )
                hid = (residual[:, c] * scale * gains[1:2, c]).astype(BF).astype(F32)
                small = lax.dot_general(
                    hid, logit_grad, (((0,), (0,)), ((), ())), preferred_element_type=F32, precision=HIGH
                )
                gain_row = jnp.concatenate(gain_rows, axis=1)[:, c]
                lane = lax.broadcasted_iota(jnp.int32, (width // 2, EXTRA), 1)
                column = jnp.broadcast_to(gain_row, (8, width // 2)).T[:, :1]
                small = jnp.where(lane == EXTRA - 1, column, small)
                v_whole[2 * i : 2 * i + 2, :, :, :, width:] = small.astype(BF).reshape(
                    2, 2, 2, width // 16, EXTRA
                )
            dense("W", 0, v_whole, False, 0, o_whole)

        def dense(name, i, v, ring_first, spread, result):
            one = dense_stream(cp, place, gr, v, got[i], bufs[i], totals[i], ring_first)
            if spread is not None:
                one = spread_stream(cp, place, one, totals[i], padded[spread], result)
            streams[name] = one
            next(one)

        def small_dense():
            dense("S", 1, v_shared, True, 1, o_shared)
            dense("N", 2, v_down, True, None, None)

        def start_out():
            streams["O"] = sum_ring_pair(cp, ge, m_outs, m_outs, b_outs, out, (residual,))
            next(streams["O"])

        def head(h):
            if h == 0:
                for copy in kept["third"]:
                    cp.arrived(copy)
            attention_back_head(h, g_heads, v_qkvs, v_probs, cosine, sine, g_keys, g_values, g_qkv)

        def hidden_part():
            @pl.loop(0, group // BLOCK)
            def _(i):
                at = pl.ds(pl.multiple_of(i * BLOCK, BLOCK), BLOCK)
                part = dot_nt(g_qkv[at, :], v_w[...]).astype(BF)
                m_grads[i, :, :, :width] = part.reshape(2, rows, width)

            hcuts = (pl.ds(0, half), pl.ds(half, width - half))
            for n, ((b,), c) in enumerate(zip(b_grads, hcuts)):
                streams["H" + str(n)] = one = sum_ring_pair(
                    cp, ge, view(m_grads, c), view(m_grads, c), [b.at[:, :, pl.ds(0, c.size)]],
                    total_hidden.at[:, c],
                )
                next(one)

        def qkv_sums():
            for i in range(2):
                c = slice(i * width // 2, (i + 1) * width // 2)
                v_qkv[2 * i : 2 * i + 2] = (
                    dot_tn(x[:, :, c].reshape(group, width // 2), g_qkv[...]).astype(BF).reshape(2, 2, 2, width // 16, 3 * span)
                )
            dense("Q", 3, v_qkv, True, 2, o_qkv)

        def first_norm():
            squares = jnp.zeros((rows, 1), F32)
            mean_k = jnp.zeros((rows, 1), F32)
            for c in range(0, width, step):
                part = tok[:, c : c + step].astype(F32)
                squares += jnp.sum(part * part, axis=1, keepdims=True)
            scale = lax.rsqrt(squares / width + EPS)
            for c in range(0, width, step):
                normed = tok[:, c : c + step].astype(F32) * scale
                k = total_hidden[:, c : c + step] * gains[0:1, c : c + step]
                mean_k += jnp.sum(k * normed, axis=1, keepdims=True)
            mean_k = mean_k / width
            for c in range(0, width, step):
                normed = tok[:, c : c + step].astype(F32) * scale
                k = total_hidden[:, c : c + step] * gains[0:1, c : c + step]
                d_tok[:, c : c + step] = g_residual[:, c : c + step] + scale * (k - normed * mean_k)

        follow(
            ORDER_B,
            {
                "n2": second_norm, "dw": whole_sums, "sn": small_dense, "o": start_out,
                "h0": functools.partial(head, 0), "h1": functools.partial(head, 1),
                "hp": hidden_part, "dq": qkv_sums, "n1": first_norm,
            },
        )
        run_streams(*streams.values())
        o_down[...] = totals[2][...]
        cp.finish()

    columns = (wide, h_both.shape[1], width, 3 * span)
    depth = (half_part, half_part, ROW_PAD, half_part)
    pl.run_scoped(
        phase_b,
        pltpu.VMEM(h_probs.shape, BF),
        pltpu.VMEM(h_qkv.shape, BF),
        pltpu.VMEM((width, 3 * span), BF),
        pltpu.VMEM(h_whole.shape, BF),
        pltpu.VMEM((rows, width), F32),
        *[pltpu.VMEM((rows, width), BF)] * 3,
        *[pltpu.VMEM((group, HD), F32)] * 2,
        pltpu.VMEM((4, 2, 2, half_part, wide), BF),
        pltpu.VMEM((4, 2, 2, half_part, 3 * span), BF),
        [pltpu.VMEM((r, c), BF) for r, c in zip(depth, columns)],
        [pltpu.VMEM((8, ROW_PAD, columns[i]), BF) for i in (0, 1, 3)],
        pltpu.VMEM((8, rows, span), BF),
        pltpu.VMEM((rows, width), F32),
        *[pltpu.VMEM((group, HD), F32)] * 2,
        pltpu.VMEM((group, 3 * span), BF),
        pltpu.VMEM((rows, width), BF),
    )


def call_rest(
    experts, top, x_own, g_all, e_gate, e_up, e_down, h_probs, h_hidden, h_qkv, w_slices, h_whole,
    h_residual, h_cot, h_tok, h_attended, h_cosine, h_sine,
    extra, w_router, s_both, s_padded, live, gains,
):
    anyspace = pl.BlockSpec(memory_space=pl.ANY)
    vmem = pl.BlockSpec(memory_space=pltpu.VMEM)
    rows, width = h_cot.shape
    span = HEADS_DEV * HD
    wide = width + EXTRA
    cut = wide // 2 // 128 * 128
    exp_dev, _, hidden = e_gate.shape
    part = width // 16
    columns = (wide, s_both.shape[1], width, 3 * span)
    depth = (part, part, ROW_PAD, part)
    orders = (False, True, True, True)
    halves = ((part, hidden), (part, hidden), (hidden // 8, width // 2))
    bufs_of = lambda first, r, c: (ring_pair_bufs if first else pair_ring_bufs)(r, c)
    shape = jax.ShapeDtypeStruct
    return pl.pallas_call(
        functools.partial(kernel_rest, experts, top),
        out_shape=(
            shape((rows, width), BF),
            shape((rows, width), F32),
            shape((exp_dev, 2, 4, 2, part, hidden), BF),
            shape((exp_dev, 2, 4, 2, part, hidden), BF),
            shape((exp_dev, 4, 2, hidden // 8, width), BF),
            shape((8, ROW_PAD, 3 * span), BF),
            shape((8, ROW_PAD, columns[1]), BF),
            shape((8, ROW_PAD, wide), BF),
            shape((ROW_PAD, width), BF),
        ),
        in_specs=[anyspace] * 20 + [vmem] * 2,
        out_specs=(vmem, vmem) + (anyspace,) * 6 + (vmem,),
        scratch_shapes=[
            pltpu.VMEM((8, rows, width), BF),
            pltpu.VMEM((4, 2, rows, wide), BF),
            pltpu.VMEM((4, 2, rows, width), BF),
            [ring_pair_bufs(rows, c) for c in (cut, wide - cut)],
            ring_pair_bufs(rows, width),
            pltpu.VMEM((rows, wide), F32),
            pltpu.VMEM((rows, width), F32),
            [pltpu.VMEM((4, 2) + h, BF) for h in halves],
            [ring_pair_bufs(*h) for h in halves],
            [[pltpu.VMEM(h, BF) for h in halves] for _ in range(exp_dev)],
            pltpu.VMEM((4, 2, 2, part, columns[1]), BF),
            pltpu.VMEM((4, 2, 2, ROW_PAD, width), BF),
            [pltpu.VMEM((4, 2, r, c), BF) for r, c in zip(depth, columns)],
            [bufs_of(first, r, c) for first, r, c in zip(orders, depth, columns)],
            pltpu.VMEM((8, rows, span), BF),
            pltpu.VMEM((rows, EXTRA), F32),
            pltpu.SemaphoreType.REGULAR((3,)),
            pltpu.SemaphoreType.DMA((440,)),
            pltpu.SemaphoreType.DMA((440,)),
        ],
        compiler_params=pltpu.CompilerParams(
            collective_id=2, has_side_effects=True, vmem_limit_bytes=int(63.9 * 2**20)
        ),
        name="rest",
    )(
        x_own, g_all, e_gate, e_up, e_down, h_probs, h_hidden, h_qkv, w_slices, h_whole,
        h_residual, h_cot, h_tok, h_attended, h_cosine, h_sine,
        extra, w_router, s_both, s_padded, live, gains,
    )


def kernel_finish(
    o_qkv, o_shared, o_whole, o_down, w_query, w_key, w_value, norm_attn, b_gate, b_up, b_down, out_in, tok_in,
    d_query, d_key, d_value, d_output, d_router, d_sgate, d_sup, d_sdown, d_norm_one, d_norm_two,
    d_gate, d_up, d_down, out, d_tok,
):
    used, width = w_query.shape
    out[...] = out_in[...]
    d_tok[...] = tok_in[...]
    hidden = d_sgate.shape[1]
    span = HEADS_DEV * HD
    for low, full in ((b_gate, d_gate), (b_up, d_up), (b_down, d_down)):
        full[...] = low[...].astype(F32)

    step = pl.program_id(0)

    @pl.when(step == 1)
    def _():
        gain = jnp.zeros((used, 1), F32)
        for n, (w, d) in enumerate(((w_query, d_query), (w_key, d_key), (w_value, d_value))):
            for owner in range(width // span):
                c = slice(owner * span, (owner + 1) * span)
                part = o_qkv[owner, :used, n * span : (n + 1) * span].astype(F32)
                d[:, c] = part
                gain += jnp.sum(part * w[:, c].astype(F32), axis=1, keepdims=True)
        d_norm_one[...] = as_row(gain) / norm_attn[...].astype(F32)

    @pl.when(step == 2)
    def _():
        for n, d in enumerate((d_sgate, d_sup)):
            total = jnp.zeros((ROW_PAD, hidden), F32)
            for owner in range(8):
                pick = shared_columns(owner, hidden, d_sdown.shape[0])
                total += dot_nt(o_shared[owner, :, n * 128 : (n + 1) * 128], pick)
            d[...] = total[:used]

    @pl.when(step == 3)
    def _():
        total = o_whole[0].astype(F32)
        for i in range(1, 8):
            total += o_whole[i].astype(F32)
        d_output[...] = total[:used, :width]
        d_router[...] = total[:used, width : width + d_router.shape[1]]
        d_norm_two[...] = as_row(total[:used, width + EXTRA - 1 :])
        d_sdown[...] = o_down[: d_sdown.shape[0]].astype(F32)


def call_finish(
    o_qkv, o_shared, o_whole, o_down, w_query, w_key, w_value, norm_attn, b_gate, b_up, b_down,
    out, d_tok, experts, hidden,
):
    used, width = w_query.shape
    down_used = hidden // 128
    shape = jax.ShapeDtypeStruct
    steps = 4
    fixed = lambda a: pl.BlockSpec(a.shape, lambda i: (0,) * len(a.shape))
    part = lambda a: pl.BlockSpec((a.shape[0] // steps, a.shape[1]), lambda i: (i, 0))
    small = (
        [shape((used, width), F32)] * 4
        + [shape((used, experts), F32)]
        + [shape((used, hidden), F32)] * 2
        + [shape((down_used, width), F32)]
        + [shape((1, used), F32)] * 2
    )
    cast = (b_gate, b_up, b_down, out, d_tok)
    large = [shape(a.shape, F32) for a in cast[:3]] + [shape(a.shape, a.dtype) for a in cast[3:]]
    operands = (o_qkv, o_shared, o_whole, o_down, w_query, w_key, w_value, norm_attn)
    return pl.pallas_call(
        kernel_finish,
        grid=(steps,),
        out_shape=tuple(small + large),
        in_specs=[fixed(a) for a in operands] + [part(a) for a in cast],
        out_specs=tuple([fixed(a) for a in small] + [part(a) for a in large]),
        compiler_params=pltpu.CompilerParams(
            vmem_limit_bytes=VMEM_LIMIT, dimension_semantics=("arbitrary",)
        ),
        name="finish",
    )(*operands, *cast)


def body(
    tokens, cotangent, lengths, token_mask, routes,
    w_query, w_key, w_value, w_output, w_router,
    shared_gate, shared_up, shared_down, norm_attn, norm_ffn,
    expert_gate, expert_up, expert_down,
):
    rows, width = tokens.shape
    used = w_query.shape[0]
    exp_dev, _, hidden = expert_gate.shape
    experts = w_router.shape[1]
    group = rows * 8
    frequency = 10000.0 ** (-(np.arange(HD // 2, dtype=np.float32) * np.float32(2.0) / HD))
    angles = np.arange(group, dtype=np.float32)[:, None] * frequency.astype(np.float32)[None, :]
    cosine = jnp.asarray(np.tile(np.cos(angles), (1, 2)), F32)
    sine = jnp.asarray(np.concatenate([-np.sin(angles), np.sin(angles)], axis=1), F32)
    (
        w_slices, w_both, w_whole, w_router_all, w_down, cot_all, extra,
        hidden_one, qkv, attn_probs, gain_rows, residual, attended, hidden_two, live,
    ) = call_front(
        tokens, cotangent, lengths[None], token_mask[None], routes.T,
        w_query, w_key, w_value, w_output, w_router,
        shared_gate, shared_up, shared_down, norm_attn[None], norm_ffn[None], cosine, sine,
    )
    out, d_tokens, e_gate, e_up, e_down, o_qkv, o_shared, o_whole, o_down = call_rest(
        experts, routes.shape[1],
        hidden_two, cot_all, expert_gate, expert_up, expert_down,
        attn_probs, hidden_one.reshape(8, rows, width), qkv,
        w_slices.reshape(width, -1), w_whole.reshape(width, -1),
        residual, cotangent, tokens, attended, cosine, sine,
        extra, w_router_all.reshape(width, EXTRA),
        w_both.reshape(width, -1), w_down.reshape(-1, width), live, gain_rows,
    )
    (
        d_query, d_key, d_value, d_output, d_router, d_sgate, d_sup, d_sdown, d_norm_one, d_norm_two,
        d_gate, d_up, d_down, out, d_tokens,
    ) = call_finish(
        o_qkv, o_shared, o_whole, o_down, w_query, w_key, w_value, norm_attn[None],
        e_gate.reshape(-1, hidden), e_up.reshape(-1, hidden), e_down.reshape(-1, width),
        out, d_tokens, experts, hidden,
    )
    return (
        out, d_tokens, d_query, d_key, d_value, d_output, d_router, d_sgate, d_sup, d_sdown,
        d_norm_one.reshape(used), d_norm_two.reshape(used),
        d_gate.reshape(exp_dev, width, hidden), d_up.reshape(exp_dev, width, hidden),
        d_down.reshape(exp_dev, hidden, width),
    )


def solution(mesh):
    both = ("rep", "ep")
    row = P(both, None)
    expert = P("ep", None, None)
    in_specs = (
        row, row, P("rep"), P(both), row, row, row, row, row, row, row, row, row,
        P(both), P(both), expert, expert, expert,
    )
    out_specs = (
        row, row, row, row, row, row, row, row, row, row, P(both), P(both),
        expert, expert, expert,
    )
    return jax.shard_map(body, mesh=mesh, in_specs=in_specs, out_specs=out_specs, check_vma=False)
```
